32 devices in a mesh: dp: 2 (over x), ffn: 4 (over z), hid: 4 (over y, core).
Axes of the slice: x: 2, y: 2, z: 4, core: 2. Of those that a mesh axis runs over, the one named last changes fastest.
Arguments:
- stream: bfloat16 [512, 16384], P('dp', 'hid'), may hold values from -160 to 160
- steering: float32 [16384], P('hid'), may hold values from -40 to 40
- strength: float32 [512], P('dp'), may hold values from 0.5 to 2
- norm_gain_vector: float32 [16384], P('hid'), may hold values from 0.25 to 1.75
- frozen_weights: bfloat16 [2, 16384, 26624], P('dp', 'hid', 'ffn'), may hold values from -0.046875 to 0.046875
- adapter_down_factors: bfloat16 [2, 16384, 16], P(None, 'hid'), may hold values from -0.046875 to 0.046875
- adapter_up_factors: bfloat16 [2, 16, 26624], P(None, None, 'ffn'), may hold values from -1.5 to 1.5
- cotangent: bfloat16 [512, 26624], P(('dp', 'hid'), 'ffn'), may hold values from -6 to 6
Outputs:
- residual_stream_gradient: bfloat16 [512, 16384], P('dp', 'hid')
- steering_vector_gradient: float32 [16384], P('hid')
- adapter_down_gradient: float32 [2, 16384, 16], P(None, 'hid')
- adapter_up_gradient: float32 [2, 16, 26624], P(None, None, 'ffn')
The draws below stay inside these ranges and needn't reach their ends.
All inputs are finite; a program needn't handle non-finite values.
Results may differ from the reference program's by a relative error of at most 0.0068.
Values may be sent and summed in bfloat16 or wider, within the bound.
No kernel may reach another device: no remote copies, remote signals or barrier semaphores. Data moves between devices by JAX's collectives and lax.ppermute only.
A program may use at most 256 MiB of HBM per device.

```python
import math
import jax
import jax.numpy as jnp
from jax import lax

MODEL_WIDTH = 16384
HIDDEN_HALF = 26624
ADAPTER_RANK = 16
TOKENS = 512


def column_scales(key, count):
    ramp = jnp.exp(jnp.arange(count, dtype=jnp.float32) / count * math.log(3.0))
    spread = jnp.exp(jax.random.uniform(key, (count,), jnp.float32, 0.0, math.log(10.0))) / math.sqrt(10.0)
    return ramp * spread


def draw_stream(key, part):
    first, second, third = jax.random.split(jax.random.fold_in(key, 11), 3)
    columns = column_scales(second, MODEL_WIDTH)
    row_scale = jnp.exp(jax.random.uniform(third, (TOKENS, 1), jnp.float32, math.log(0.4), math.log(4.0)))
    base = jax.random.truncated_normal(first, -4.0, 4.0, (TOKENS, MODEL_WIDTH), jnp.float32)
    return (base * row_scale * columns[None, :]).astype(jnp.bfloat16)


def draw_steering(key, part):
    first, second = jax.random.split(jax.random.fold_in(key, 23), 2)
    columns = column_scales(second, MODEL_WIDTH)
    base = jax.random.truncated_normal(first, -4.0, 4.0, (MODEL_WIDTH,), jnp.float32)
    return base * columns


def levels(own_key, shape, cuts, smallest, high):
    level, own = 1.0, jax.random.fold_in(own_key, 6)
    for dim, parts in cuts:
        steps = jnp.exp(jax.random.uniform(jax.random.fold_in(own, dim), (parts,), jnp.float32, smallest / len(cuts), high / len(cuts)))
        level = level * jnp.repeat(steps, shape[dim] // parts).reshape([-1 if axis == dim else 1 for axis in range(len(shape))])
    return level


def gaussian(stream_key, shape, deviation, most, cuts=(), kind=jnp.bfloat16):
    array = deviation * jax.random.normal(stream_key, shape, jnp.float32)
    if cuts:
        array = array * levels(stream_key, shape, cuts, -0.22, 0.18)
    return jnp.clip(array, -most, most).astype(kind)


def setup_inputs(seed: int = 0) -> dict:
    key_of = jax.random.split(jax.random.key(seed), 9)
    stream = draw_stream(jax.random.fold_in(key_of[8], 71), 0)
    steering = draw_steering(jax.random.fold_in(key_of[8], 71), 0)
    strength = jnp.clip(jnp.exp(math.log(2.0) - 1.3862944 * jax.random.uniform(key_of[2], (TOKENS,), jnp.float32) ** levels(key_of[2], (TOKENS,), ((0, 2),), -0.2, 0.2)), 0.5, 2.0)
    norm_gain_vector = jnp.clip(1.0 + 0.15 * jax.random.normal(key_of[3], (MODEL_WIDTH,), jnp.float32), 0.25, 1.75)
    frozen_weights = gaussian(key_of[4], (2, MODEL_WIDTH, HIDDEN_HALF), MODEL_WIDTH ** -0.5, 0.046875, ((0, 2), (1, 4), (2, 4)))
    adapter_down_factors = gaussian(key_of[5], (2, MODEL_WIDTH, ADAPTER_RANK), MODEL_WIDTH ** -0.5, 0.046875, ((1, 4),))
    adapter_up_factors = gaussian(key_of[6], (2, ADAPTER_RANK, HIDDEN_HALF), ADAPTER_RANK ** -0.5, 1.5, ((2, 4),))
    cotangent = gaussian(key_of[7], (TOKENS, HIDDEN_HALF), 1.0, 6.0, ((0, 8), (1, 4)))
    return dict(stream=stream, steering=steering, strength=strength, norm_gain_vector=norm_gain_vector, frozen_weights=frozen_weights, adapter_down_factors=adapter_down_factors, adapter_up_factors=adapter_up_factors, cotangent=cotangent)


ADAPTER_SCALE = 0.5

def reference(stream, steering, strength, norm_gain_vector, frozen_weights, adapter_down_factors, adapter_up_factors, cotangent):
    rows = stream.astype(jnp.float32)
    stream_ms = lax.optimization_barrier(jnp.mean(rows * rows, axis=1)) + 1e-06
    steer_ms = jnp.mean(steering * steering) + 1e-06
    scale = strength * jnp.sqrt(stream_ms / steer_ms)
    steered = rows + scale[:, None] * steering[None, :]
    inv_rms = lax.rsqrt(lax.optimization_barrier(jnp.mean(steered * steered, axis=1)) + 1e-05)
    normalized_input = (steered * inv_rms[:, None] * norm_gain_vector[None, :]).astype(jnp.bfloat16)
    lowrank_rows = jnp.einsum('jq,hqp->jhp', normalized_input.astype(jnp.float32), adapter_down_factors.astype(jnp.float32)).astype(jnp.bfloat16)
    gate_values = jnp.dot(normalized_input, frozen_weights[0], preferred_element_type=jnp.float32)
    gate_values = gate_values + ADAPTER_SCALE * jnp.dot(lowrank_rows[:, 0].astype(jnp.float32), adapter_up_factors[0].astype(jnp.float32))
    up_projection_values = jnp.dot(normalized_input, frozen_weights[1], preferred_element_type=jnp.float32)
    up_projection_values = up_projection_values + ADAPTER_SCALE * jnp.dot(lowrank_rows[:, 1].astype(jnp.float32), adapter_up_factors[1].astype(jnp.float32))
    sigma = jax.nn.sigmoid(gate_values)
    incoming_gradient = cotangent.astype(jnp.float32)
    gate_grad = incoming_gradient * up_projection_values * sigma * (1.0 + gate_values * (1.0 - sigma))
    upper_grad = incoming_gradient * gate_values * sigma
    activation_gradient = jnp.stack([gate_grad, upper_grad], axis=1).astype(jnp.bfloat16)
    lowrank_backward = jnp.einsum('sua,uqa->suq', activation_gradient.astype(jnp.float32), adapter_up_factors.astype(jnp.float32)).astype(jnp.bfloat16)
    normalized_gradient = jnp.dot(activation_gradient[:, 0], frozen_weights[0].T, preferred_element_type=jnp.float32)
    normalized_gradient = normalized_gradient + jnp.dot(activation_gradient[:, 1], frozen_weights[1].T, preferred_element_type=jnp.float32)
    normalized_gradient = normalized_gradient + ADAPTER_SCALE * jnp.einsum('qme,mfe->qf', lowrank_backward.astype(jnp.float32), adapter_down_factors.astype(jnp.float32))
    product = lax.optimization_barrier(jnp.mean(steered * norm_gain_vector[None, :] * normalized_gradient, axis=1))
    steered_grad = inv_rms[:, None] * norm_gain_vector[None, :] * normalized_gradient - (inv_rms ** 3 * product)[:, None] * steered
    residual_stream_gradient = steered_grad.astype(jnp.bfloat16)
    steering_vector_gradient = lax.optimization_barrier(jnp.sum(scale[:, None] * steered_grad, axis=0))
    adapter_down_gradient = ADAPTER_SCALE * jnp.einsum('cl,can->aln', normalized_input.astype(jnp.float32), lowrank_backward.astype(jnp.float32))
    adapter_up_gradient = ADAPTER_SCALE * jnp.einsum('qyj,qyi->yji', lowrank_rows.astype(jnp.float32), activation_gradient.astype(jnp.float32))
    return (residual_stream_gradient, steering_vector_gradient, adapter_down_gradient, adapter_up_gradient)
```

```python
import jax
import jax.numpy as jnp
from jax import lax
from jax.experimental import pallas as pl
from jax.experimental.pallas import tpu as pltpu
from jax.sharding import PartitionSpec as P

MODEL_WIDTH = 16384
ADAPTER_SCALE = 0.5
HIDDEN_CHUNKS = 2
WIDTH_CHUNKS = 4
VMEM_BYTES = 48 * 1024 * 1024

F32 = jnp.float32
BF16 = jnp.bfloat16


def bits_of(n):
    return n.bit_length() - 1


def reversed_bits(x, n):
    out = 0
    for i in range(n):
        out = out + (((x >> i) & 1) << (n - 1 - i))
    return out


def tile_of(n, cap):
    return max(t for t in range(128, cap + 1, 128) if n % t == 0)


def split_tiles(count, parts):
    edges = [count * i // parts for i in range(parts + 1)]
    return [(a, b - a) for a, b in zip(edges, edges[1:]) if b > a]


def take_blocks(x, sources, block):
    pieces = [lax.dynamic_slice_in_dim(x, s * block, block, axis=0) for s in sources]
    return jnp.concatenate(pieces, axis=0)


def to_relative(x, me, n):
    b = bits_of(n)
    return take_blocks(x, [me ^ reversed_bits(p, b) for p in range(n)], x.shape[0] // n)


def from_relative(x, me, n):
    b = bits_of(n)
    return take_blocks(x, [reversed_bits(t ^ me, b) for t in range(n)], x.shape[0] // n)


def relative_to_relative(x, me, n, other, m):
    count = max(n, m)
    rn, rm = count // n, count // m
    sources = []
    for p in range(count):
        natural = (reversed_bits(p // rm, bits_of(m)) ^ other) * rm + p % rm
        sources.append(reversed_bits((natural // rn) ^ me, bits_of(n)) * rn + natural % rn)
    return take_blocks(x, sources, x.shape[0] // count)


def swap(x, axis, n, mask):
    return lax.ppermute(x, axis, [(i, i ^ mask) for i in range(n)])


def halve(keep, send, axis, n, bit=0):
    received = swap(send, axis, n, 1 << bit)
    total = keep + received.astype(F32)
    if bit + 1 == bits_of(n):
        return total
    half = total.shape[0] // 2
    return halve(total[:half], total[half:].astype(BF16), axis, n, bit + 1)


def double(x, axis, n):
    for bit in reversed(range(bits_of(n))):
        x = jnp.concatenate([x, swap(x, axis, n, 1 << bit)], axis=0)
    return x


def forward_kernel(x_ref, w_ref, keep_ref, send_ref):
    y = jnp.dot(x_ref[...], w_ref[0], preferred_element_type=F32)
    half = keep_ref.shape[0]
    keep_ref[...] = y[:half]
    send_ref[...] = y[half:].astype(BF16)


def forward_matmul(x, weights, first, tiles, tile):
    rows, depth = x.shape
    half = rows // 2
    return pl.pallas_call(
        forward_kernel,
        grid=(tiles,),
        in_specs=[
            pl.BlockSpec((rows, depth), lambda i: (0, 0)),
            pl.BlockSpec((1, depth, tile), lambda i: (0, 0, first + i)),
        ],
        out_specs=[pl.BlockSpec((half, tile), lambda i: (0, i))] * 2,
        out_shape=[
            jax.ShapeDtypeStruct((half, tiles * tile), F32),
            jax.ShapeDtypeStruct((half, tiles * tile), BF16),
        ],
        compiler_params=pltpu.CompilerParams(vmem_limit_bytes=VMEM_BYTES),
        cost_estimate=pl.CostEstimate(
            flops=2 * rows * depth * tiles * tile,
            bytes_accessed=2 * depth * (rows + tiles * tile) + 6 * half * tiles * tile,
            transcendentals=0,
        ),
        name="forward_matmul",
    )(x, weights)


def backward_kernel(*refs):
    *g_refs, w_ref, keep_ref, send_ref = refs
    y, at = None, 0
    for g_ref in g_refs:
        width = g_ref.shape[1]
        part = lax.dot_general(
            g_ref[...], w_ref[0, :, at : at + width], (((1,), (1,)), ((), ())), preferred_element_type=F32
        )
        y = part if y is None else y + part
        at += width
    half = keep_ref.shape[0]
    keep_ref[...] = y[:half]
    send_ref[...] = y[half:].astype(BF16)


def backward_matmul(grads, weights, first, tiles, tile):
    rows = grads[0].shape[0]
    half, hidden = rows // 2, weights.shape[2]
    return pl.pallas_call(
        backward_kernel,
        grid=(tiles,),
        in_specs=[pl.BlockSpec(g.shape, lambda i: (0, 0)) for g in grads]
        + [pl.BlockSpec((1, tile, hidden), lambda i: (0, first + i, 0))],
        out_specs=[pl.BlockSpec((half, tile), lambda i: (0, i))] * 2,
        out_shape=[
            jax.ShapeDtypeStruct((half, tiles * tile), F32),
            jax.ShapeDtypeStruct((half, tiles * tile), BF16),
        ],
        compiler_params=pltpu.CompilerParams(vmem_limit_bytes=VMEM_BYTES),
        cost_estimate=pl.CostEstimate(
            flops=2 * rows * hidden * tiles * tile,
            bytes_accessed=2 * hidden * (rows + tiles * tile) + 6 * half * tiles * tile,
            transcendentals=0,
        ),
        name="backward_matmul",
    )(*grads, weights)


def make_local(dp, hid, ffn):
    def local(stream, steering, strength, gain, weights, down, up, cotangent):
        d, h, f = lax.axis_index("dp"), lax.axis_index("hid"), lax.axis_index("ffn")
        tokens, width = stream.shape
        hidden = weights.shape[2]
        own = tokens // hid
        rank = down.shape[2]
        first_pair = d == 0

        peer_stream = swap(stream, "dp", dp, 1)
        rows = stream.astype(F32)
        total_rows, total_steer = lax.psum(
            (jnp.sum(rows * rows, axis=1), jnp.sum(steering * steering)), "hid"
        )
        stream_ms = total_rows / MODEL_WIDTH + 1e-06
        steer_ms = total_steer / MODEL_WIDTH + 1e-06
        scale = strength * jnp.sqrt(stream_ms / steer_ms)
        steered = rows + scale[:, None] * steering[None, :]
        steered_power = lax.psum(jnp.sum(steered * steered, axis=1), "hid")
        inv_rms = lax.rsqrt(steered_power / MODEL_WIDTH + 1e-05)
        stats = jnp.stack([scale, inv_rms], axis=1)
        peer_stats = swap(stats, "dp", dp, 1)

        def normalize(rows, stats):
            steered = rows.astype(F32) + stats[:, :1] * steering[None, :]
            return (steered * stats[:, 1:] * gain[None, :]).astype(BF16)

        normed = [
            normalize(to_relative(r, h, hid), to_relative(s, h, hid))
            for r, s in ((stream, stats), (peer_stream, peer_stats))
        ]

        tile = tile_of(hidden, 256)
        chunks = split_tiles(hidden // tile, HIDDEN_CHUNKS)
        acts = [
            [
                halve(*forward_matmul(x, weights, first, count, tile), "hid", hid)
                for first, count in chunks
            ]
            for x in normed
        ]

        low_part = jnp.concatenate(
            [
                from_relative(
                    jnp.einsum("td,kdr->tkr", x, down, preferred_element_type=F32).reshape(tokens, 2 * rank), h, hid
                )
                for x in normed
            ],
            axis=0,
        )
        low = jnp.sum(lax.all_gather(low_part, "hid", axis=0), axis=0).astype(BF16)
        low_own = lax.dynamic_slice_in_dim(low[:tokens], h * own, own, axis=0)

        grads, back_part, up_parts = [], 0.0, []
        low_mine = jnp.concatenate(
            [to_relative(part, f, ffn) for part in (low[:tokens], low[tokens:])], axis=0
        )
        low_mine = jnp.where(first_pair, low_mine[:, :rank], low_mine[:, rank:])
        for c, (first, count) in enumerate(chunks):
            columns = slice(first * tile, (first + count) * tile)
            mine = acts[0][c]
            other = swap(acts[1][c].astype(BF16), "dp", dp, 1).astype(F32)
            factors = up[:, :, columns]
            gate = jnp.where(first_pair, mine, other) + ADAPTER_SCALE * jnp.dot(
                low_own[:, :rank], factors[0], preferred_element_type=F32
            )
            upper = jnp.where(first_pair, other, mine) + ADAPTER_SCALE * jnp.dot(
                low_own[:, rank:], factors[1], preferred_element_type=F32
            )
            sigma = jax.nn.sigmoid(gate)
            flow = cotangent[:, columns].astype(F32)
            gate_grad = (flow * upper * sigma * (1.0 + gate * (1.0 - sigma))).astype(BF16)
            upper_grad = (flow * gate * sigma).astype(BF16)
            back_part = back_part + jnp.concatenate(
                [
                    lax.dot_general(g, factors[k], (((1,), (1,)), ((), ())), preferred_element_type=F32)
                    for k, g in enumerate((gate_grad, upper_grad))
                ],
                axis=1,
            )
            mine_grad = jnp.where(first_pair, gate_grad, upper_grad)
            peer_grad = swap(jnp.where(first_pair, upper_grad, gate_grad), "dp", dp, 1)
            whole = jnp.concatenate(
                [
                    relative_to_relative(double(g, "hid", hid), h, hid, f, ffn)
                    for g in (mine_grad, peer_grad)
                ],
                axis=0,
            )
            grads.append(whole)
            up_parts.append(
                ADAPTER_SCALE
                * lax.dot_general(low_mine, whole, (((0,), (0,)), ((), ())), preferred_element_type=F32)
            )

        up_mine = jnp.concatenate(up_parts, axis=1)
        up_other = swap(up_mine.astype(BF16), "dp", dp, 1).astype(F32)
        up_gradient = jnp.where(
            first_pair, jnp.stack([up_mine, up_other]), jnp.stack([up_other, up_mine])
        )

        back = lax.all_gather(back_part, ("dp", "hid", "ffn"), axis=0).reshape(dp, hid, ffn, own, 2 * rank)
        back = jnp.sum(back, axis=2).astype(BF16).reshape(dp, tokens, 2 * rank)
        back_own = lax.dynamic_index_in_dim(back, d, axis=0, keepdims=False)
        back_peer = lax.dynamic_index_in_dim(back, 1 - d, axis=0, keepdims=False)
        back_normed = jnp.concatenate([to_relative(b, h, hid) for b in (back_own, back_peer)], axis=0)
        all_normed = jnp.concatenate(normed, axis=0)
        down_gradient = jnp.stack(
            [
                ADAPTER_SCALE
                * lax.dot_general(
                    all_normed,
                    back_normed[:, k * rank : (k + 1) * rank],
                    (((0,), (0,)), ((), ())),
                    preferred_element_type=F32,
                )
                for k in range(2)
            ]
        )

        width_tile = tile_of(width, 256)
        shard = tokens // ffn
        back_shard = lax.dynamic_slice_in_dim(back_own, f * shard, shard, axis=0)
        stream_shard = lax.dynamic_slice_in_dim(stream, f * shard, shard, axis=0)
        stats_shard = lax.dynamic_slice_in_dim(stats, f * shard, shard, axis=0)
        down_rows = jnp.concatenate([down[0], down[1]], axis=1)

        def low_rank_term(b, columns):
            return ADAPTER_SCALE * lax.dot_general(
                b, down_rows[columns], (((1,), (1,)), ((), ())), preferred_element_type=F32
            )

        inner, gathered = 0.0, []
        for first, count in split_tiles(width // width_tile, WIDTH_CHUNKS):
            columns = slice(first * width_tile, (first + count) * width_tile)
            keep, send = backward_matmul(grads, weights, first, count, width_tile)
            part = keep + swap(send, "dp", dp, 1).astype(F32)
            half = tokens // 2
            share = halve(part[:half], part[half:].astype(BF16), "ffn", ffn)
            steered_shard = stream_shard[:, columns].astype(F32) + stats_shard[:, :1] * steering[None, columns]
            inner = inner + jnp.sum(
                steered_shard * gain[None, columns] * (share + low_rank_term(back_shard, columns)), axis=1
            )
            gathered.append(from_relative(double(share.astype(BF16), "ffn", ffn), f, ffn))
        inner = lax.all_gather(inner, ("hid", "ffn"), axis=0).reshape(hid, tokens)
        dot = jnp.sum(inner, axis=0) / MODEL_WIDTH

        normed_grad = jnp.concatenate(gathered, axis=1).astype(F32) + low_rank_term(back_own, slice(None))
        steered_grad = (
            inv_rms[:, None] * gain[None, :] * normed_grad
            - (inv_rms**3 * dot)[:, None] * (stream.astype(F32) + scale[:, None] * steering[None, :])
        )
        steering_gradient = lax.psum(jnp.sum(scale[:, None] * steered_grad, axis=0), "dp")
        return steered_grad.astype(BF16), steering_gradient, down_gradient, up_gradient

    return local


def solution(mesh):
    in_specs = (
        P("dp", "hid"),
        P("hid"),
        P("dp"),
        P("hid"),
        P("dp", "hid", "ffn"),
        P(None, "hid", None),
        P(None, None, "ffn"),
        P(("dp", "hid"), "ffn"),
    )
    out_specs = (P("dp", "hid"), P("hid"), P(None, "hid", None), P(None, None, "ffn"))
    local = make_local(mesh.shape["dp"], mesh.shape["hid"], mesh.shape["ffn"])
    return jax.shard_map(local, mesh=mesh, in_specs=in_specs, out_specs=out_specs, check_vma=False)
```

```python
import jax
import jax.numpy as jnp
from jax import lax
from jax.experimental import pallas as pl
from jax.experimental.pallas import tpu as pltpu
from jax.sharding import PartitionSpec as P

MODEL_WIDTH = 16384
ADAPTER_SCALE = 0.5
WIDTH_CHUNKS = 4
VMEM_BYTES = 40 * 1024 * 1024

F32 = jnp.float32
BF16 = jnp.bfloat16
ANY = pl.BlockSpec(memory_space=pl.ANY)


def bits_of(n):
    return n.bit_length() - 1


def reversed_bits(x, n):
    out = 0
    for i in range(n):
        out = out + (((x >> i) & 1) << (n - 1 - i))
    return out


def tile_of(n, cap):
    return max(t for t in range(128, cap + 1, 128) if n % t == 0)


def split_tiles(count, parts):
    edges = [count * i // parts for i in range(parts + 1)]
    return [(a, b - a) for a, b in zip(edges, edges[1:]) if b > a]


def swap(x, axis, n, mask):
    return lax.ppermute(x, axis, [(i, i ^ mask) for i in range(n)])


def double(x, axis, n, dim=0):
    for bit in reversed(range(bits_of(n))):
        x = jnp.concatenate([x, swap(x, axis, n, 1 << bit)], axis=dim)
    return x


def ordered(x, *first):
    return lax.optimization_barrier((x, *first))[0]


def total_of(parts, start, stop):
    out = parts[0][start:stop]
    for part in parts[1:]:
        out = out + part[start:stop].astype(F32)
    return out


def halve(keep, send, axis, n):
    parts = [keep, swap(send, axis, n, 1)]
    for bit in range(1, bits_of(n)):
        rows = parts[-1].shape[0]
        parts.append(swap(total_of(parts, rows // 2, rows).astype(BF16), axis, n, 1 << bit))
    return parts


def params():
    return pltpu.CompilerParams(vmem_limit_bytes=VMEM_BYTES)


def normalize(stream, stats, steering, gain, down, h, hid):
    tokens, width = stream.shape
    block = tokens // hid
    ranks = down.shape[0]

    def place(p, h_ref):
        return h_ref[0] ^ reversed_bits(p, bits_of(hid))

    def kernel(h_ref, x_ref, s_ref, steer_ref, gain_ref, down_ref, out_ref, low_ref):
        steered = x_ref[...].astype(F32) + s_ref[:, :1] * steer_ref[...]
        normed = (steered * s_ref[:, 1:] * gain_ref[...]).astype(BF16)
        out_ref[...] = normed
        low_ref[...] = lax.dot_general(
            normed, down_ref[...], (((1,), (1,)), ((), ())), preferred_element_type=F32
        )

    return pl.pallas_call(
        kernel,
        grid_spec=pltpu.PrefetchScalarGridSpec(
            num_scalar_prefetch=1,
            grid=(hid,),
            in_specs=[
                pl.BlockSpec((block, width), lambda p, h_ref: (place(p, h_ref), 0)),
                pl.BlockSpec((block, 2), lambda p, h_ref: (place(p, h_ref), 0)),
                pl.BlockSpec((1, width), lambda p, h_ref: (0, 0)),
                pl.BlockSpec((1, width), lambda p, h_ref: (0, 0)),
                pl.BlockSpec((ranks, width), lambda p, h_ref: (0, 0)),
            ],
            out_specs=[
                pl.BlockSpec((block, width), lambda p, h_ref: (p, 0)),
                pl.BlockSpec((block, ranks), lambda p, h_ref: (p, 0)),
            ],
        ),
        out_shape=[
            jax.ShapeDtypeStruct((tokens, width), BF16),
            jax.ShapeDtypeStruct((tokens, ranks), F32),
        ],
        compiler_params=params(),
        cost_estimate=pl.CostEstimate(
            flops=2 * tokens * width * ranks, bytes_accessed=4 * tokens * width, transcendentals=0
        ),
        name="normalize",
    )(h.reshape(1), stream, stats, steering.reshape(1, width), gain.reshape(1, width), down)


def forward_matmul(x, weights, first, tiles, tile, after=()):
    rows, depth = x.shape
    half = rows // 2
    parts = 4
    step = depth // parts

    def kernel(x_ref, *refs):
        w_refs, (keep_ref, send_ref) = refs[:parts], refs[-2:]
        y = None
        for i, w_ref in enumerate(w_refs):
            part = jnp.dot(x_ref[:, i * step : (i + 1) * step], w_ref[0], preferred_element_type=F32)
            y = part if y is None else y + part
        keep_ref[...] = y[:half]
        send_ref[...] = y[half:].astype(BF16)

    return pl.pallas_call(
        kernel,
        grid=(tiles,),
        in_specs=[pl.BlockSpec((rows, depth), lambda i: (0, 0))]
        + [pl.BlockSpec((1, step, tile), lambda i, k=k: (0, k, first + i)) for k in range(parts)]
        + [ANY] * len(after),
        out_specs=[pl.BlockSpec((half, tile), lambda i: (0, i))] * 2,
        out_shape=[
            jax.ShapeDtypeStruct((half, tiles * tile), F32),
            jax.ShapeDtypeStruct((half, tiles * tile), BF16),
        ],
        compiler_params=params(),
        cost_estimate=pl.CostEstimate(
            flops=2 * rows * depth * tiles * tile,
            bytes_accessed=2 * depth * (rows + tiles * tile) + 6 * half * tiles * tile,
            transcendentals=0,
        ),
        name="forward_matmul",
    )(x, *[weights] * parts, *after)


def gated_gradients(d, mine, other, cotangent, first, low, up, own, after=()):
    columns = other.shape[1]
    rank = up.shape[1]
    tile = tile_of(columns, 1024)
    tiles = columns // tile
    base = first // tile

    def kernel(d_ref, *refs):
        mine_refs = refs[: len(mine)]
        other_ref, flow_ref, low_ref, up_ref = refs[len(mine) : len(mine) + 4]
        mine_out, other_out, back_ref = refs[-3:]
        own_is_gate = d_ref[0] == 0
        total = mine_refs[0][...].astype(F32)
        for ref in mine_refs[1:]:
            total = total + ref[...].astype(F32)
        passed = other_ref[...].astype(F32)
        low_terms = [
            ADAPTER_SCALE
            * jnp.dot(low_ref[:, k * rank : (k + 1) * rank], up_ref[k], preferred_element_type=F32)
            for k in range(2)
        ]
        gate = jnp.where(own_is_gate, total, passed) + low_terms[0]
        upper = jnp.where(own_is_gate, passed, total) + low_terms[1]
        sigma = 1.0 / (1.0 + jnp.exp(-gate))
        flow = flow_ref[...].astype(F32)
        gate_grad = (flow * upper * sigma * (1.0 + gate * (1.0 - sigma))).astype(BF16)
        upper_grad = (flow * gate * sigma).astype(BF16)
        mine_out[...] = jnp.where(own_is_gate, gate_grad, upper_grad)
        other_out[...] = jnp.where(own_is_gate, upper_grad, gate_grad)

        @pl.when(pl.program_id(0) == 0)
        def _():
            back_ref[...] = jnp.zeros_like(back_ref)

        contract = (((1,), (1,)), ((), ()))
        for k, grad in enumerate((gate_grad, upper_grad)):
            back_ref[:, k * rank : (k + 1) * rank] += lax.dot_general(
                grad, up_ref[k], contract, preferred_element_type=F32
            )
        back_ref[:, 2 * rank :] += jnp.sum(
            gate_grad.astype(F32) * gate + upper_grad.astype(F32) * upper, axis=1, keepdims=True
        )

    here = pl.BlockSpec((own, tile), lambda i, d_ref: (0, i))
    there = pl.BlockSpec((own, tile), lambda i, d_ref: (0, base + i))
    return pl.pallas_call(
        kernel,
        grid_spec=pltpu.PrefetchScalarGridSpec(
            num_scalar_prefetch=1,
            grid=(tiles,),
            in_specs=[here] * (len(mine) + 1)
            + [
                there,
                pl.BlockSpec((own, 2 * rank), lambda i, d_ref: (0, 0)),
                pl.BlockSpec((2, rank, tile), lambda i, d_ref: (0, 0, base + i)),
            ]
            + [ANY] * len(after),
            out_specs=[here, here, pl.BlockSpec((own, 2 * rank + 1), lambda i, d_ref: (0, 0))],
        ),
        out_shape=[
            jax.ShapeDtypeStruct((own, columns), BF16),
            jax.ShapeDtypeStruct((own, columns), BF16),
            jax.ShapeDtypeStruct((own, 2 * rank + 1), F32),
        ],
        compiler_params=params(),
        cost_estimate=pl.CostEstimate(
            flops=8 * own * columns * rank, bytes_accessed=16 * own * columns, transcendentals=own * columns
        ),
        name="gated_gradients",
    )(d.reshape(1), *mine, other, cotangent, low, up, *after)


def backward_matmul(grads, weights, chunk, first, tiles, tile, base=None, partial=False, after=()):
    rows, hidden = sum(g.shape[0] for g in grads), grads[0].shape[1]
    half = rows // 2
    n_base = 0 if base is None else 1

    def kernel(*refs):
        g_refs = refs[: len(grads)]
        w_ref = refs[len(grads)]
        g = jnp.concatenate([ref[...] for ref in g_refs], axis=0)
        y = lax.dot_general(g, w_ref[0], (((1,), (1,)), ((), ())), preferred_element_type=F32)
        if n_base:
            y = y + refs[len(grads) + 1][...]
        if partial:
            refs[-1][...] = y
        else:
            refs[-2][...] = y[:half]
            refs[-1][...] = y[half:].astype(BF16)

    if partial:
        out_specs = pl.BlockSpec((rows, tile), lambda i: (0, i))
        out_shape = jax.ShapeDtypeStruct((rows, tiles * tile), F32)
    else:
        out_specs = [pl.BlockSpec((half, tile), lambda i: (0, i))] * 2
        out_shape = [
            jax.ShapeDtypeStruct((half, tiles * tile), F32),
            jax.ShapeDtypeStruct((half, tiles * tile), BF16),
        ]
    return pl.pallas_call(
        kernel,
        grid=(tiles,),
        in_specs=[pl.BlockSpec(g.shape, lambda i: (0, 0)) for g in grads]
        + [pl.BlockSpec((1, tile, hidden), lambda i: (0, first + i, chunk))]
        + [pl.BlockSpec((rows, tile), lambda i: (0, first + i))] * n_base
        + [ANY] * len(after),
        out_specs=out_specs,
        out_shape=out_shape,
        compiler_params=params(),
        cost_estimate=pl.CostEstimate(
            flops=2 * rows * hidden * tiles * tile,
            bytes_accessed=2 * hidden * (rows + tiles * tile) + (4 + 4 * n_base) * rows * tiles * tile,
            transcendentals=0,
        ),
        name="backward_matmul",
    )(*grads, weights, *(() if base is None else (base,)), *after)


def finish(parts, stream, stats, back, down, steering, gain, columns):
    rows = stream.shape[0]
    width = parts[0].shape[1]
    start = columns // width

    def kernel(*refs):
        part_refs = refs[: len(parts)]
        x_ref, s_ref, back_ref, down_ref, steer_ref, gain_ref, out_ref, sum_ref = refs[len(parts) :]
        total = part_refs[0][...].astype(F32)
        for ref in part_refs[1:]:
            total = total + ref[...].astype(F32)
        total = total + ADAPTER_SCALE * jnp.dot(back_ref[...], down_ref[...], preferred_element_type=F32)
        steered = x_ref[...].astype(F32) + s_ref[:, 0:1] * steer_ref[...]
        grad = s_ref[:, 1:2] * gain_ref[...] * total - s_ref[:, 2:3] * steered
        out_ref[...] = grad.astype(BF16)
        sum_ref[...] = jnp.sum(s_ref[:, 0:1] * grad, axis=0, keepdims=True)

    across = lambda n: pl.BlockSpec((n, width), lambda i: (0, start))
    return pl.pallas_call(
        kernel,
        grid=(1,),
        in_specs=[pl.BlockSpec((rows, width), lambda i: (0, 0))] * len(parts)
        + [
            across(rows),
            pl.BlockSpec(stats.shape, lambda i: (0, 0)),
            pl.BlockSpec(back.shape, lambda i: (0, 0)),
            across(down.shape[0]),
            across(1),
            across(1),
        ],
        out_specs=[pl.BlockSpec((rows, width), lambda i: (0, 0)), pl.BlockSpec((1, width), lambda i: (0, 0))],
        out_shape=[jax.ShapeDtypeStruct((rows, width), BF16), jax.ShapeDtypeStruct((1, width), F32)],
        compiler_params=params(),
        cost_estimate=pl.CostEstimate(
            flops=2 * rows * width * down.shape[0], bytes_accessed=10 * rows * width, transcendentals=0
        ),
        name="finish",
    )(*parts, stream, stats, back, down, steering.reshape(1, -1), gain.reshape(1, -1))


def make_local(dp, hid, ffn):
    def local(stream, steering, strength, gain, weights, down, up, cotangent):
        d, h, f = lax.axis_index("dp"), lax.axis_index("hid"), lax.axis_index("ffn")
        tokens, width = stream.shape
        hidden = weights.shape[2]
        own = tokens // hid
        rank = down.shape[2]
        first_pair = d == 0
        down_rows = jnp.transpose(down, (0, 2, 1)).reshape(2 * rank, width)

        peer_stream = swap(stream, "dp", dp, 1)
        rows = stream.astype(F32)
        total_rows, total_steer = lax.psum(
            (jnp.sum(rows * rows, axis=1), jnp.sum(steering * steering)), "hid"
        )
        stream_ms = total_rows / MODEL_WIDTH + 1e-06
        steer_ms = total_steer / MODEL_WIDTH + 1e-06
        scale = strength * jnp.sqrt(stream_ms / steer_ms)
        steered = rows + scale[:, None] * steering[None, :]
        steered_power = lax.psum(jnp.sum(steered * steered, axis=1), "hid")
        inv_rms = lax.rsqrt(steered_power / MODEL_WIDTH + 1e-05)
        stats = jnp.stack([scale, inv_rms], axis=1)
        peer_stats = swap(stats, "dp", dp, 1)

        count = 2 if hidden % 256 == 0 else 1
        chunk = hidden // count
        tile = tile_of(chunk, 256)
        tiles = chunk // tile
        own_normed, own_low = normalize(stream, stats, steering, gain, down_rows, h, hid)
        own_acts = []
        for c in range(count):
            keep, send = forward_matmul(own_normed, weights, c * tiles, tiles, tile)
            own_acts.append(halve(keep, send, "hid", hid))
        peer_normed, peer_low = normalize(peer_stream, peer_stats, steering, gain, down_rows, h, hid)
        peer_acts = []
        for c in range(count):
            wait = (own_acts[c - 1][-1],) if c else ()
            keep, send = forward_matmul(peer_normed, weights, c * tiles, tiles, tile, wait)
            peer_acts.append(halve(keep, send, "hid", hid))

        low = jnp.stack([own_low, peer_low])
        for bit in range(bits_of(hid)):
            half = low.shape[1] // 2
            low = low[:, :half] + swap(low[:, half:], "hid", hid, 1 << bit)
        low = low.astype(BF16)
        low_own = low[0]
        low_mine = jnp.where(first_pair, low[:, :, :rank], low[:, :, rank:])
        low_mine = double(low_mine, "hid", hid, dim=1)

        width_tile = tile_of(width, 256)
        grads, back, base, wait = [], 0.0, None, ()
        for c in range(count):
            other = swap(total_of(peer_acts[c], 0, own).astype(BF16), "dp", dp, 1)
            mine_grad, other_grad, back_part = gated_gradients(
                d, own_acts[c], other, cotangent, c * chunk, low_own, up, own, wait
            )
            back = back + back_part
            peer_grad = swap(other_grad, "dp", dp, 1)
            pieces, wait = [], (peer_grad,)
            for g in (mine_grad, peer_grad):
                for bit in reversed(range(1, bits_of(hid))):
                    got = swap(g, "hid", hid, 1 << bit)
                    if g is mine_grad:
                        wait += (got,)
                    if c and g is peer_grad:
                        got = ordered(got, base)
                    g = jnp.concatenate([g, got], axis=0)
                pieces += [g, swap(g, "hid", hid, 1)]
            grads.append(pieces)
            if c < count - 1:
                base = backward_matmul(
                    pieces, weights, c, 0, width // width_tile, width_tile, base=base, partial=True
                )

        for bit in range(bits_of(ffn)):
            back = back + swap(back, "ffn", ffn, 1 << bit)
        back = jnp.stack([back, swap(back, "dp", dp, 1)])
        back = double(back, "hid", hid, dim=1)
        back_low = back[:, :, : 2 * rank].astype(BF16)
        acts_product = back[0, :, 2 * rank]

        shard = tokens // ffn
        place = reversed_bits(f, bits_of(ffn))
        block = min(own, shard)

        def natural(row):
            index = row // own
            return (h ^ reversed_bits(index, bits_of(hid))) * own + row % own

        def shard_rows(x):
            return jnp.concatenate(
                [
                    lax.dynamic_slice_in_dim(x, natural(place * shard + i * block), block, axis=0)
                    for i in range(shard // block)
                ],
                axis=0,
            )

        stats_shard = shard_rows(stats)
        dot_shard = lax.dynamic_slice_in_dim(acts_product, place * shard, shard, axis=0)
        dot_factor = stats_shard[:, 1] ** 2 * dot_shard / MODEL_WIDTH
        stats_shard = jnp.concatenate([stats_shard, dot_factor[:, None]], axis=1)
        stream_shard = shard_rows(stream)
        back_shard = lax.dynamic_slice_in_dim(back_low[0], place * shard, shard, axis=0)

        out = jnp.zeros((tokens, width), BF16)
        sums = []
        steps = split_tiles(width // width_tile, WIDTH_CHUNKS)
        products, received = [], []
        for first, n in steps:
            keep, send = backward_matmul(grads[-1], weights, count - 1, first, n, width_tile, base=base)
            products.append(keep)
            received.append(swap(send, "dp", dp, 1))
        results = []
        for j, (first, n) in enumerate(steps):
            held = received[j]
            if j >= 2:
                held = ordered(held, results[j - 2])
            part = products[j] + held.astype(F32)
            parts = [part]
            for bit in range(bits_of(ffn)):
                half = parts[-1].shape[0] // 2
                mine = (f >> bit) & 1
                halves = [
                    [lax.dynamic_slice_in_dim(p, side * half, half, axis=0) for p in parts]
                    for side in (mine, 1 - mine)
                ]
                parts = halves[0] + [swap(total_of(halves[1], 0, half).astype(BF16), "ffn", ffn, 1 << bit)]
            result, sum_part = finish(
                parts, stream_shard, stats_shard, back_shard, down_rows, steering, gain, first * width_tile
            )
            sums.append(sum_part)
            results.append(result)
            result = double(result, "ffn", ffn)
            for p in range(ffn):
                owner = reversed_bits(f ^ reversed_bits(p, bits_of(ffn)), bits_of(ffn))
                for i in range(shard // block):
                    out = lax.dynamic_update_slice(
                        out,
                        result[p * shard + i * block : p * shard + (i + 1) * block],
                        (natural(owner * shard + i * block), first * width_tile),
                    )

        steering_gradient = jnp.concatenate(sums, axis=1)
        for bit in range(bits_of(ffn)):
            steering_gradient = steering_gradient + swap(steering_gradient, "ffn", ffn, 1 << bit)
        steering_gradient = steering_gradient + swap(steering_gradient, "dp", dp, 1)

        up_parts = []
        for pieces in grads:
            total, at = 0.0, 0
            low_rows = low_mine.reshape(2 * tokens, rank)
            for g in pieces:
                total = total + lax.dot_general(
                    low_rows[at : at + g.shape[0]], g, (((0,), (0,)), ((), ())), preferred_element_type=F32
                )
                at += g.shape[0]
            up_parts.append(ADAPTER_SCALE * total)
        up_mine = jnp.concatenate(up_parts, axis=1)
        up_other = swap(up_mine.astype(BF16), "dp", dp, 1).astype(F32)
        up_gradient = jnp.where(
            first_pair, jnp.stack([up_mine, up_other]), jnp.stack([up_other, up_mine])
        )
        down_gradient = 0.0
        for x, b in ((own_normed, back_low[0]), (peer_normed, back_low[1])):
            down_gradient = down_gradient + lax.dot_general(
                b, x, (((0,), (0,)), ((), ())), preferred_element_type=F32
            )
        down_gradient = jnp.transpose(
            (ADAPTER_SCALE * down_gradient).reshape(2, rank, width), (0, 2, 1)
        )
        return out, steering_gradient.reshape(width), down_gradient, up_gradient

    return local


def solution(mesh):
    in_specs = (
        P("dp", "hid"),
        P("hid"),
        P("dp"),
        P("hid"),
        P("dp", "hid", "ffn"),
        P(None, "hid", None),
        P(None, None, "ffn"),
        P(("dp", "hid"), "ffn"),
    )
    out_specs = (P("dp", "hid"), P("hid"), P(None, "hid", None), P(None, None, "ffn"))
    local = make_local(mesh.shape["dp"], mesh.shape["hid"], mesh.shape["ffn"])
    return jax.shard_map(local, mesh=mesh, in_specs=in_specs, out_specs=out_specs, check_vma=False)
```

```python
import jax
import jax.numpy as jnp
from jax import lax
from jax.experimental import pallas as pl
from jax.experimental.pallas import tpu as pltpu
from jax.sharding import PartitionSpec as P

MODEL_WIDTH = 16384
ADAPTER_SCALE = 0.5
HIDDEN_CHUNKS = 3
WIDTH_CHUNKS = 4
VMEM_BYTES = 28 * 1024 * 1024

F32 = jnp.float32
BF16 = jnp.bfloat16
ANY = pl.BlockSpec(memory_space=pl.ANY)
RESIDENT = pl.BlockSpec(memory_space=pltpu.VMEM)


def bits_of(n):
    return n.bit_length() - 1


def reversed_bits(x, n):
    out = 0
    for i in range(n):
        out = out + (((x >> i) & 1) << (n - 1 - i))
    return out


def tile_of(n, cap):
    return max(t for t in range(128, cap + 1, 128) if n % t == 0)


def split_tiles(count, parts):
    edges = [count * i // parts for i in range(parts + 1)]
    return [(a, b - a) for a, b in zip(edges, edges[1:]) if b > a]


def swap(x, axis, n, mask):
    return lax.ppermute(x, axis, [(i, i ^ mask) for i in range(n)])


def double(x, axis, n, dim=0):
    for bit in reversed(range(bits_of(n))):
        x = jnp.concatenate([x, swap(x, axis, n, 1 << bit)], axis=dim)
    return x


def ordered(x, *first):
    return lax.optimization_barrier((x, *first))[0]


def total_of(parts, start, stop):
    out = parts[0][start:stop]
    for part in parts[1:]:
        out = out + part[start:stop].astype(F32)
    return out


def params():
    return pltpu.CompilerParams(vmem_limit_bytes=VMEM_BYTES)


def normalize(pieces, stats, steering, gain, down, h, hid, side, into=None):
    tokens = stats.shape[0]
    width = steering.shape[0]
    block = tokens // hid
    ranks = down.shape[0]
    n_into = 0 if into is None else 1

    def token_block(p, s_ref):
        return s_ref[0] ^ reversed_bits(p, bits_of(hid))

    def kernel(s_ref, *refs):
        x_refs = refs[: len(pieces)]
        stat_ref, steer_ref, gain_ref, down_ref = refs[len(pieces) : len(pieces) + 4]
        out_ref, low_ref = refs[-2:]
        x = jnp.concatenate([ref[...].astype(F32) for ref in x_refs], axis=1)
        steered = x + stat_ref[:, :1] * steer_ref[...]
        normed = (steered * stat_ref[:, 1:] * gain_ref[...]).astype(BF16)
        out_ref[...] = normed
        low_ref[...] = lax.dot_general(
            normed, down_ref[...], (((1,), (1,)), ((), ())), preferred_element_type=F32
        )

    scalars = [h]
    specs = []
    for x, where in pieces:
        if where is None:
            specs.append(pl.BlockSpec((block, x.shape[1]), lambda p, s_ref: (token_block(p, s_ref), 0)))
        else:
            scalars.append(where.me)
            specs.append(
                pl.BlockSpec((block, x.shape[1]), lambda p, s_ref: (where.at(token_block(p, s_ref), s_ref[1]), 0))
            )
    whole = lambda n: pl.BlockSpec((n, width), lambda p, s_ref: (0, 0))
    return pl.pallas_call(
        kernel,
        grid_spec=pltpu.PrefetchScalarGridSpec(
            num_scalar_prefetch=1,
            grid=(hid,),
            in_specs=specs
            + [
                pl.BlockSpec((block, 2), lambda p, s_ref: (token_block(p, s_ref), 0)),
                whole(1),
                whole(1),
                whole(ranks),
            ]
            + [ANY] * n_into,
            out_specs=[
                pl.BlockSpec((block, width), lambda p, s_ref: (2 * p + side, 0)),
                pl.BlockSpec((block, ranks), lambda p, s_ref: (p, 0)),
            ],
        ),
        out_shape=[
            jax.ShapeDtypeStruct((2 * tokens, width), BF16),
            jax.ShapeDtypeStruct((tokens, ranks), F32),
        ],
        input_output_aliases={len(pieces) + 5: 0} if n_into else {},
        compiler_params=params(),
        cost_estimate=pl.CostEstimate(
            flops=2 * tokens * width * ranks, bytes_accessed=4 * tokens * width, transcendentals=0
        ),
        name="normalize",
    )(
        jnp.stack(scalars),
        *[x for x, _ in pieces],
        stats,
        steering.reshape(1, width),
        gain.reshape(1, width),
        down,
        *((into,) if n_into else ()),
    )


class GatheredRows:
    def __init__(self, me, n, shard, block):
        self.me, self.n, self.ratio = me, n, shard // block

    def at(self, index, me):
        owner = index // self.ratio
        return reversed_bits(owner ^ me, bits_of(self.n)) * self.ratio + index % self.ratio


def forward_matmul(x, weights, first, tiles, start, stop, tile, into=(), after=()):
    rows, depth = x.shape
    half = rows // 2

    def kernel(x_ref, w_ref, *refs):
        keep_ref, send_ref = refs[-2:]
        y = jnp.dot(x_ref[...], w_ref[0], preferred_element_type=F32)
        keep_ref[...] = y[:half]
        send_ref[...] = y[half:].astype(BF16)

    return pl.pallas_call(
        kernel,
        grid=(stop - start,),
        in_specs=[RESIDENT, pl.BlockSpec((1, depth, tile), lambda i: (0, 0, first + start + i))]
        + [ANY] * (len(into) + len(after)),
        out_specs=[pl.BlockSpec((half, tile), lambda i: (0, start + i))] * 2,
        out_shape=[
            jax.ShapeDtypeStruct((half, tiles * tile), F32),
            jax.ShapeDtypeStruct((half, tiles * tile), BF16),
        ],
        input_output_aliases={2 + i: i for i in range(len(into))},
        compiler_params=params(),
        cost_estimate=pl.CostEstimate(
            flops=2 * rows * depth * (stop - start) * tile,
            bytes_accessed=2 * depth * (rows + (stop - start) * tile) + 6 * half * (stop - start) * tile,
            transcendentals=0,
        ),
        name="forward_matmul",
    )(x, weights, *into, *after)


def share_sums(parts, own):
    columns = parts[0].shape[1]
    tile = tile_of(columns, 1536)

    def kernel(*refs):
        total = refs[0][...].astype(F32)
        for ref in refs[1 : len(parts)]:
            total = total + ref[...].astype(F32)
        refs[-2][...] = total[:own].astype(BF16)
        refs[-1][...] = total[own:].astype(BF16)

    return pl.pallas_call(
        kernel,
        grid=(columns // tile,),
        in_specs=[pl.BlockSpec((2 * own, tile), lambda i: (1, i))] * len(parts),
        out_specs=[pl.BlockSpec((own, tile), lambda i: (0, i))] * 2,
        out_shape=[jax.ShapeDtypeStruct((own, columns), BF16)] * 2,
        compiler_params=params(),
        cost_estimate=pl.CostEstimate(
            flops=2 * own * columns, bytes_accessed=16 * own * columns, transcendentals=0
        ),
        name="share_sums",
    )(*parts)


def gated_gradients(d, mine, other, cotangent, first, low, up, own, after=()):
    columns = other.shape[1]
    rank = up.shape[1]
    tile = max(t for t in range(128, 2049, 128) if columns % t == 0 and first % t == 0)
    tiles = columns // tile
    base = first // tile

    def kernel(d_ref, *refs):
        mine_refs = refs[: len(mine)]
        other_ref, flow_ref, low_ref, up_ref = refs[len(mine) : len(mine) + 4]
        mine_out, other_out, back_ref = refs[-3:]
        own_is_gate = d_ref[0] == 0
        total = mine_refs[0][...].astype(F32)
        for ref in mine_refs[1:]:
            total = total + ref[...].astype(F32)
        passed = other_ref[...].astype(F32)
        low_terms = [
            ADAPTER_SCALE
            * jnp.dot(low_ref[:, k * rank : (k + 1) * rank], up_ref[k], preferred_element_type=F32)
            for k in range(2)
        ]
        gate = jnp.where(own_is_gate, total, passed) + low_terms[0]
        upper = jnp.where(own_is_gate, passed, total) + low_terms[1]
        sigma = 1.0 / (1.0 + jnp.exp(-gate))
        flow = flow_ref[...].astype(F32)
        gate_grad = (flow * upper * sigma * (1.0 + gate * (1.0 - sigma))).astype(BF16)
        upper_grad = (flow * gate * sigma).astype(BF16)
        mine_out[...] = jnp.where(own_is_gate, gate_grad, upper_grad)
        other_out[...] = jnp.where(own_is_gate, upper_grad, gate_grad)

        @pl.when(pl.program_id(0) == 0)
        def _():
            back_ref[...] = jnp.zeros_like(back_ref)

        contract = (((1,), (1,)), ((), ()))
        for k, grad in enumerate((gate_grad, upper_grad)):
            back_ref[:, k * rank : (k + 1) * rank] += lax.dot_general(
                grad, up_ref[k], contract, preferred_element_type=F32
            )
        back_ref[:, 2 * rank :] += jnp.sum(
            gate_grad.astype(F32) * gate + upper_grad.astype(F32) * upper, axis=1, keepdims=True
        )

    here = pl.BlockSpec((own, tile), lambda i, d_ref: (0, i))
    there = pl.BlockSpec((own, tile), lambda i, d_ref: (0, base + i))
    return pl.pallas_call(
        kernel,
        grid_spec=pltpu.PrefetchScalarGridSpec(
            num_scalar_prefetch=1,
            grid=(tiles,),
            in_specs=[here] * (len(mine) + 1)
            + [
                there,
                pl.BlockSpec((own, 2 * rank), lambda i, d_ref: (0, 0)),
                pl.BlockSpec((2, rank, tile), lambda i, d_ref: (0, 0, base + i)),
            ]
            + [ANY] * len(after),
            out_specs=[here, here, pl.BlockSpec((own, 2 * rank + 1), lambda i, d_ref: (0, 0))],
        ),
        out_shape=[
            jax.ShapeDtypeStruct((own, columns), BF16),
            jax.ShapeDtypeStruct((own, columns), BF16),
            jax.ShapeDtypeStruct((own, 2 * rank + 1), F32),
        ],
        compiler_params=params(),
        cost_estimate=pl.CostEstimate(
            flops=8 * own * columns * rank, bytes_accessed=16 * own * columns, transcendentals=own * columns
        ),
        name="gated_gradients",
    )(d.reshape(1), *mine, other, cotangent, low, up, *after)


def backward_matmul(pieces, weights, hidden_start, first, tiles, tile, base=None, base_first=0, partial=False, after=()):
    rows = sum(g.shape[0] for g in pieces)
    half = rows // 2
    n_base = 0 if base is None else 1
    hidden = pieces[0].shape[1]

    def kernel(*refs):
        w_ref = refs[len(pieces)]
        g = jnp.concatenate([ref[...] for ref in refs[: len(pieces)]], axis=0)
        y = lax.dot_general(g, w_ref[0], (((1,), (1,)), ((), ())), preferred_element_type=F32)
        if n_base:
            y = y + refs[len(pieces) + 1][...]
        if partial:
            refs[-1][...] = y
        else:
            refs[-2][...] = y[:half]
            refs[-1][...] = y[half:].astype(BF16)

    if partial:
        out_specs = pl.BlockSpec((rows, tile), lambda i: (0, i))
        out_shape = jax.ShapeDtypeStruct((rows, tiles * tile), F32)
    else:
        out_specs = [pl.BlockSpec((half, tile), lambda i: (0, i))] * 2
        out_shape = [
            jax.ShapeDtypeStruct((half, tiles * tile), F32),
            jax.ShapeDtypeStruct((half, tiles * tile), BF16),
        ]
    return pl.pallas_call(
        kernel,
        grid=(tiles,),
        in_specs=[RESIDENT] * len(pieces)
        + [
            pl.BlockSpec(
                (pl.Element(1), pl.Element(tile), pl.Element(hidden)),
                lambda i: (0, (first + i) * tile, hidden_start),
            )
        ]
        + [pl.BlockSpec((rows, tile), lambda i: (0, first - base_first + i))] * n_base
        + [ANY] * len(after),
        out_specs=out_specs,
        out_shape=out_shape,
        compiler_params=params(),
        cost_estimate=pl.CostEstimate(
            flops=2 * rows * hidden * tiles * tile,
            bytes_accessed=2 * hidden * (rows + tiles * tile) + (4 + 4 * n_base) * rows * tiles * tile,
            transcendentals=0,
        ),
        name="backward_matmul",
    )(*pieces, weights, *(() if base is None else (base,)), *after)


def adapter_up(low, groups):
    rank = low.shape[0]

    def kernel(*refs):
        at = 1
        for i, pieces in enumerate(groups):
            g = jnp.concatenate([ref[...] for ref in refs[at : at + len(pieces)]], axis=0)
            at += len(pieces)
            refs[i - len(groups)][...] = ADAPTER_SCALE * jnp.dot(
                refs[0][...], g, preferred_element_type=F32
            )

    operands = [g for pieces in groups for g in pieces]
    widths = [pieces[0].shape[1] for pieces in groups]
    return pl.pallas_call(
        kernel,
        grid=(1,),
        in_specs=[RESIDENT] * (1 + len(operands)),
        out_specs=[pl.BlockSpec((rank, w), lambda i: (0, 0)) for w in widths],
        out_shape=[jax.ShapeDtypeStruct((rank, w), F32) for w in widths],
        compiler_params=params(),
        cost_estimate=pl.CostEstimate(
            flops=2 * rank * low.shape[1] * sum(widths),
            bytes_accessed=2 * low.shape[1] * sum(widths),
            transcendentals=0,
        ),
        name="adapter_up",
    )(low, *operands)


def assemble(pieces, places, block, tokens, width, columns, into=None):
    chunk = pieces[0].shape[1]
    start = columns // chunk

    def kernel(place_ref, *refs):
        out_ref = refs[-1]
        i = 0
        for ref in refs[: len(pieces)]:
            for r in range(0, ref.shape[0], block):
                out_ref[pl.ds(pl.multiple_of(place_ref[i], block), block), :] = ref[r : r + block, :]
                i += 1

    n_into = 0 if into is None else 1
    return pl.pallas_call(
        kernel,
        grid_spec=pltpu.PrefetchScalarGridSpec(
            num_scalar_prefetch=1,
            grid=(1,),
            in_specs=[pl.BlockSpec(x.shape, lambda i, p: (0, 0)) for x in pieces] + [ANY] * n_into,
            out_specs=pl.BlockSpec((tokens, chunk), lambda i, p: (0, start)),
        ),
        out_shape=jax.ShapeDtypeStruct((tokens, width), BF16),
        input_output_aliases={len(pieces) + 1: 0} if n_into else {},
        compiler_params=params(),
        cost_estimate=pl.CostEstimate(flops=0, bytes_accessed=4 * tokens * chunk, transcendentals=0),
        name="assemble",
    )(places, *pieces, *((into,) if n_into else ()))


def finish(parts, stream, stats, back, down, steering, gain, columns):
    rows = stream.shape[0]
    width = parts[0].shape[1]
    start = columns // width

    def kernel(*refs):
        part_refs = refs[: len(parts)]
        x_ref, s_ref, back_ref, down_ref, steer_ref, gain_ref, out_ref, sum_ref = refs[len(parts) :]
        total = part_refs[0][...].astype(F32)
        for ref in part_refs[1:]:
            total = total + ref[...].astype(F32)
        total = total + ADAPTER_SCALE * jnp.dot(back_ref[...], down_ref[...], preferred_element_type=F32)
        steered = x_ref[...].astype(F32) + s_ref[:, 0:1] * steer_ref[...]
        grad = s_ref[:, 1:2] * gain_ref[...] * total - s_ref[:, 2:3] * steered
        out_ref[...] = grad.astype(BF16)
        sum_ref[...] = jnp.sum(s_ref[:, 0:1] * grad, axis=0, keepdims=True)

    across = lambda n: pl.BlockSpec((n, width), lambda i: (0, start))
    return pl.pallas_call(
        kernel,
        grid=(1,),
        in_specs=[pl.BlockSpec((rows, width), lambda i: (0, 0))] * len(parts)
        + [
            across(rows),
            pl.BlockSpec(stats.shape, lambda i: (0, 0)),
            pl.BlockSpec(back.shape, lambda i: (0, 0)),
            across(down.shape[0]),
            across(1),
            across(1),
        ],
        out_specs=[pl.BlockSpec((rows, width), lambda i: (0, 0)), pl.BlockSpec((1, width), lambda i: (0, 0))],
        out_shape=[jax.ShapeDtypeStruct((rows, width), BF16), jax.ShapeDtypeStruct((1, width), F32)],
        compiler_params=params(),
        cost_estimate=pl.CostEstimate(
            flops=2 * rows * width * down.shape[0], bytes_accessed=10 * rows * width, transcendentals=0
        ),
        name="finish",
    )(*parts, stream, stats, back, down, steering.reshape(1, -1), gain.reshape(1, -1))


def make_local(dp, hid, ffn):
    def local(stream, steering, strength, gain, weights, down, up, cotangent):
        d, h, f = lax.axis_index("dp"), lax.axis_index("hid"), lax.axis_index("ffn")
        tokens, width = stream.shape
        hidden = weights.shape[2]
        own = tokens // hid
        rank = down.shape[2]
        first_pair = d == 0
        down_rows = jnp.transpose(down, (0, 2, 1)).reshape(2 * rank, width)

        shard = tokens // ffn
        split = width // 2 if hid >= ffn and width % 256 == 0 else width
        if split < width:
            mine = lax.dynamic_slice(stream, (f * shard, split), (shard, width - split))
            far = double(swap(mine, "dp", dp, 1), "ffn", ffn)
            near = swap(stream[:, :split], "dp", dp, 1)
            peer_pieces = [(near, None), (far, GatheredRows(f, ffn, shard, own))]
        else:
            peer_pieces = [(swap(stream, "dp", dp, 1), None)]
        rows = stream.astype(F32)
        total_rows, total_steer = lax.psum(
            (jnp.sum(rows * rows, axis=1), jnp.sum(steering * steering)), "hid"
        )
        stream_ms = total_rows / MODEL_WIDTH + 1e-06
        steer_ms = total_steer / MODEL_WIDTH + 1e-06
        scale = strength * jnp.sqrt(stream_ms / steer_ms)
        steered = rows + scale[:, None] * steering[None, :]
        steered_power = lax.psum(jnp.sum(steered * steered, axis=1), "hid")
        inv_rms = lax.rsqrt(steered_power / MODEL_WIDTH + 1e-05)
        stats = jnp.stack([scale, inv_rms], axis=1)
        peer_stats = swap(stats, "dp", dp, 1)

        tile = tile_of(hidden, 512)
        count = hidden // tile
        chunks = split_tiles(count, HIDDEN_CHUNKS)
        normed, own_low = normalize([(stream, None)], stats, steering, gain, down_rows, h, hid, 0)
        normed, peer_low = normalize(
            peer_pieces, peer_stats, steering, gain, down_rows, h, hid, 1, into=normed
        )

        low, low_steps = jnp.stack([own_low, peer_low]), []
        for bit in range(bits_of(hid)):
            half = low.shape[1] // 2
            low = low[:, :half] + swap(low[:, half:], "hid", hid, 1 << bit)
            low_steps.append(low)
        low = low.astype(BF16)
        low_own = low[0]

        acts, sent, others = [], [], []
        last_bit = 1 << (bits_of(hid) - 1)
        for c, (first, n) in enumerate(chunks):
            middle = (n + 1) // 2
            wait = tuple(sent[-1]) if c else ()
            if c >= 2:
                wait += (acts[c - 2][1],)
            half_done = forward_matmul(normed, weights, first, n, 0, middle, tile, after=wait)
            wait = tuple(low_steps[c : c + 1])
            if c:
                wait += (acts[c - 1][2],)
            if c >= 2:
                wait += (others[c - 2],)
            keep, send = forward_matmul(normed, weights, first, n, middle, n, tile, into=half_done, after=wait)
            parts = [keep, swap(send, "hid", hid, 1)]
            for bit in range(1, bits_of(hid) - 1):
                size = parts[-1].shape[0]
                send = total_of(parts, size // 2, size).astype(BF16)
                parts.append(swap(send, "hid", hid, 1 << bit))
            sent.append(share_sums(parts, own))
            peer_got = swap(sent[-1][1], "hid", hid, last_bit)
            own_got = swap(sent[-1][0], "hid", hid, last_bit)
            acts.append((parts, own_got, peer_got))
            others.append(
                swap((total_of(parts, own, 2 * own) + peer_got.astype(F32)).astype(BF16), "dp", dp, 1)
            )

        width_tile = tile_of(width, 512)
        halves = split_tiles(width // width_tile, 2)
        grads, back, bases, wait = [], 0.0, [], ()

        def partial_sums(c, which, base, after):
            first, n = halves[which]
            return backward_matmul(
                grads[c], weights, chunks[c][0] * tile, first, n, width_tile,
                base=base, base_first=first, partial=True, after=after,
            )

        for c, (first, n) in enumerate(chunks):
            parts, own_got, _ = acts[c]
            if c == len(chunks) - 1:
                bases = [partial_sums(0, 0, None, wait[:1])]
                wait += (bases[0],)
            mine_grad, other_grad, back_part = gated_gradients(
                d, parts + [own_got], others[c], cotangent, first * tile, low_own, up, own, wait
            )
            back = back + back_part
            peer_grad = swap(other_grad, "dp", dp, 1)
            wait = (peer_grad,)
            pieces = []
            for g in (mine_grad, peer_grad):
                blocks = [g]
                for bit in reversed(range(bits_of(hid))):
                    blocks += [swap(x, "hid", hid, 1 << bit) for x in blocks]
                if g is mine_grad:
                    wait += (blocks[1],)
                pieces += blocks
            grads.append(pieces)
        bases.append(partial_sums(0, 1, None, (mine_grad,)))
        for c in range(1, len(chunks) - 1):
            for which in range(2):
                bases[which] = partial_sums(c, which, bases[which], wait)
                wait = (grads[-1][len(grads[-1]) // 2 + 1],)
        base = bases[-1]
        bases = [(halves[i][0], bases[i]) for i in range(2)]

        for bit in range(bits_of(ffn)):
            back = back + swap(back, "ffn", ffn, 1 << bit)
        back = ordered(back, base)
        back = jnp.stack([back, swap(back, "dp", dp, 1)])
        back = double(back, "hid", hid, dim=1)
        back_low = back[:, :, : 2 * rank].astype(BF16)
        acts_product = back[0, :, 2 * rank]

        place = reversed_bits(f, bits_of(ffn))
        block = min(own, shard)

        def natural(row):
            index = row // own
            return (h ^ reversed_bits(index, bits_of(hid))) * own + row % own

        def shard_rows(x):
            return jnp.concatenate(
                [
                    lax.dynamic_slice_in_dim(x, natural(place * shard + i * block), block, axis=0)
                    for i in range(shard // block)
                ],
                axis=0,
            )

        stats_shard = shard_rows(stats)
        dot_shard = lax.dynamic_slice_in_dim(acts_product, place * shard, shard, axis=0)
        dot_factor = stats_shard[:, 1] ** 2 * dot_shard / MODEL_WIDTH
        stats_shard = jnp.concatenate([stats_shard, dot_factor[:, None]], axis=1)
        stream_shard = shard_rows(stream)
        back_shard = lax.dynamic_slice_in_dim(back_low[0], place * shard, shard, axis=0)

        out, sums, gathered = None, [], []
        steps = split_tiles(width // width_tile, WIDTH_CHUNKS)
        products, received = [], []
        for first, n in steps:
            held_first, held = [b for b in bases if b[0] <= first][-1]
            keep, send = backward_matmul(
                grads[-1], weights, chunks[-1][0] * tile, first, n, width_tile,
                base=held, base_first=held_first,
            )
            products.append(keep)
            received.append(swap(send, "dp", dp, 1))
        places = []
        for p in range(ffn):
            owner = reversed_bits(f ^ reversed_bits(p, bits_of(ffn)), bits_of(ffn))
            places += [natural(owner * shard + i * block) for i in range(shard // block)]
        places = jnp.stack(places)
        for j, (first, n) in enumerate(steps):
            got = received[j]
            if j >= 2:
                got = ordered(got, gathered[j - 2][1], *(gathered[j - 3][-1:] if j >= 3 else ()))
            parts = [products[j], got]
            for bit in range(bits_of(ffn)):
                half = parts[-1].shape[0] // 2
                mine = (f >> bit) & 1
                halves = [
                    [lax.dynamic_slice_in_dim(p, side * half, half, axis=0) for p in parts]
                    for side in (mine, 1 - mine)
                ]
                parts = [total_of(halves[0], 0, half)] + [
                    swap(total_of(halves[1], 0, half).astype(BF16), "ffn", ffn, 1 << bit)
                ]
            result, sum_part = finish(
                parts, stream_shard, stats_shard, back_shard, down_rows, steering, gain, first * width_tile
            )
            sums.append(sum_part)
            blocks = [result]
            for bit in reversed(range(bits_of(ffn))):
                blocks += [swap(x, "ffn", ffn, 1 << bit) for x in blocks]
            gathered.append(blocks)
            out = assemble(blocks, places, block, tokens, width, first * width_tile, into=out)

        steering_gradient = jnp.concatenate(sums, axis=1)
        for bit in range(bits_of(ffn)):
            steering_gradient = steering_gradient + swap(steering_gradient, "ffn", ffn, 1 << bit)
        steering_gradient = steering_gradient + swap(steering_gradient, "dp", dp, 1)

        low_mine = jnp.where(first_pair, low[:, :, :rank], low[:, :, rank:])
        low_mine = double(ordered(low_mine, base), "hid", hid, dim=1).reshape(2 * tokens, rank)
        up_mine = jnp.concatenate(adapter_up(ordered(low_mine.T, products[-1]), grads), axis=1)
        up_other = swap(ordered(up_mine.astype(BF16), received[-1]), "dp", dp, 1).astype(F32)
        up_gradient = jnp.where(
            first_pair, jnp.stack([up_mine, up_other]), jnp.stack([up_other, up_mine])
        )
        back_rows = back_low.reshape(2, hid, own, 2 * rank).transpose(1, 0, 2, 3).reshape(2 * tokens, 2 * rank)
        down_gradient = lax.dot_general(
            back_rows, normed, (((0,), (0,)), ((), ())), preferred_element_type=F32
        )
        down_gradient = jnp.transpose(
            (ADAPTER_SCALE * down_gradient).reshape(2, rank, width), (0, 2, 1)
        )
        return out, steering_gradient.reshape(width), down_gradient, up_gradient

    return local


def solution(mesh):
    in_specs = (
        P("dp", "hid"),
        P("hid"),
        P("dp"),
        P("hid"),
        P("dp", "hid", "ffn"),
        P(None, "hid", None),
        P(None, None, "ffn"),
        P(("dp", "hid"), "ffn"),
    )
    out_specs = (P("dp", "hid"), P("hid"), P(None, "hid", None), P(None, None, "ffn"))
    local = make_local(mesh.shape["dp"], mesh.shape["hid"], mesh.shape["ffn"])
    return jax.shard_map(local, mesh=mesh, in_specs=in_specs, out_specs=out_specs, check_vma=False)
```

```python
import jax
import jax.numpy as jnp
from jax import lax
from jax.experimental import pallas as pl
from jax.experimental.pallas import tpu as pltpu
from jax.sharding import PartitionSpec as P

MODEL_WIDTH = 16384
ADAPTER_SCALE = 0.5
HIDDEN_CHUNKS = 3
VMEM_MIB = 12
MATMUL_VMEM_MIB = 18
COST_SHARE = 0.01

F32 = jnp.float32
BF16 = jnp.bfloat16
ANY = pl.BlockSpec(memory_space=pl.ANY)
RESIDENT = pl.BlockSpec(memory_space=pltpu.VMEM)


def bits_of(n):
    return n.bit_length() - 1


def reversed_bits(x, n):
    out = 0
    for i in range(n):
        out = out + (((x >> i) & 1) << (n - 1 - i))
    return out


def tile_of(n, cap):
    return max(t for t in range(128, cap + 1, 128) if n % t == 0)


def split_tiles(count, parts):
    edges = [count * i // parts for i in range(parts + 1)]
    return [(a, b - a) for a, b in zip(edges, edges[1:]) if b > a]


def swap(x, axis, n, mask):
    return lax.ppermute(x, axis, [(i, i ^ mask) for i in range(n)])


def double(x, axis, n, dim=0):
    for bit in reversed(range(bits_of(n))):
        x = jnp.concatenate([x, swap(x, axis, n, 1 << bit)], axis=dim)
    return x


def ordered(x, *first):
    return lax.optimization_barrier((x, *first))[0]


def total_of(parts, start, stop):
    out = parts[0][start:stop]
    for part in parts[1:]:
        out = out + part[start:stop].astype(F32)
    return out


def params(mib=VMEM_MIB):
    return pltpu.CompilerParams(vmem_limit_bytes=mib * 1024 * 1024)


def cost(flops, size):
    return pl.CostEstimate(
        flops=int(flops * COST_SHARE), bytes_accessed=int(size * COST_SHARE), transcendentals=0
    )


def normalize(pieces, stats, steering, gain, down, h, hid, side, into=None):
    tokens = stats.shape[0]
    width = steering.shape[0]
    block = tokens // hid
    ranks = down.shape[0]
    n_into = 0 if into is None else 1

    def token_block(p, s_ref):
        return s_ref[0] ^ reversed_bits(p, bits_of(hid))

    def kernel(s_ref, *refs):
        x_refs = refs[: len(pieces)]
        stat_ref, steer_ref, gain_ref, down_ref = refs[len(pieces) : len(pieces) + 4]
        out_ref, low_ref = refs[-2:]
        x = jnp.concatenate([ref[...].astype(F32) for ref in x_refs], axis=1)
        steered = x + stat_ref[:, :1] * steer_ref[...]
        normed = (steered * stat_ref[:, 1:] * gain_ref[...]).astype(BF16)
        out_ref[...] = normed
        low_ref[...] = lax.dot_general(
            normed, down_ref[...], (((1,), (1,)), ((), ())), preferred_element_type=F32
        )

    scalars = [h]
    specs = []
    for x, where in pieces:
        if where is None:
            specs.append(pl.BlockSpec((block, x.shape[1]), lambda p, s_ref: (token_block(p, s_ref), 0)))
        else:
            scalars.append(where.me)
            specs.append(
                pl.BlockSpec((block, x.shape[1]), lambda p, s_ref: (where.at(token_block(p, s_ref), s_ref[1]), 0))
            )
    whole = lambda n: pl.BlockSpec((n, width), lambda p, s_ref: (0, 0))
    return pl.pallas_call(
        kernel,
        grid_spec=pltpu.PrefetchScalarGridSpec(
            num_scalar_prefetch=1,
            grid=(hid,),
            in_specs=specs
            + [
                pl.BlockSpec((block, 2), lambda p, s_ref: (token_block(p, s_ref), 0)),
                whole(1),
                whole(1),
                whole(ranks),
            ]
            + [ANY] * n_into,
            out_specs=[
                pl.BlockSpec((block, width), lambda p, s_ref: (2 * p + side, 0)),
                pl.BlockSpec((block, ranks), lambda p, s_ref: (p, 0)),
            ],
        ),
        out_shape=[
            jax.ShapeDtypeStruct((2 * tokens, width), BF16),
            jax.ShapeDtypeStruct((tokens, ranks), F32),
        ],
        input_output_aliases={len(pieces) + 5: 0} if n_into else {},
        compiler_params=params(),
        cost_estimate=cost(2 * tokens * width * ranks, 4 * tokens * width),
        name="normalize",
    )(
        jnp.stack(scalars),
        *[x for x, _ in pieces],
        stats,
        steering.reshape(1, width),
        gain.reshape(1, width),
        down,
        *((into,) if n_into else ()),
    )


class GatheredRows:
    def __init__(self, me, n, shard, block):
        self.me, self.n, self.ratio = me, n, shard // block

    def at(self, index, me):
        owner = index // self.ratio
        return reversed_bits(owner ^ me, bits_of(self.n)) * self.ratio + index % self.ratio


def forward_matmul(x, weights, first, tiles, start, stop, tile, into=(), after=()):
    rows, depth = x.shape
    half = rows // 2

    def kernel(x_ref, w_ref, *refs):
        keep_ref, send_ref = refs[-2:]
        y = jnp.dot(x_ref[...], w_ref[0], preferred_element_type=F32)
        keep_ref[...] = y[:half]
        send_ref[...] = y[half:].astype(BF16)

    return pl.pallas_call(
        kernel,
        grid=(stop - start,),
        in_specs=[RESIDENT, pl.BlockSpec((1, depth, tile), lambda i: (0, 0, first + start + i))]
        + [ANY] * (len(into) + len(after)),
        out_specs=[pl.BlockSpec((half, tile), lambda i: (0, start + i))] * 2,
        out_shape=[
            jax.ShapeDtypeStruct((half, tiles * tile), F32),
            jax.ShapeDtypeStruct((half, tiles * tile), BF16),
        ],
        input_output_aliases={2 + i: i for i in range(len(into))},
        compiler_params=params(MATMUL_VMEM_MIB),
        cost_estimate=cost(2 * rows * depth * (stop - start) * tile, 2 * depth * (rows + (stop - start) * tile) + 6 * half * (stop - start) * tile),
        name="forward_matmul",
    )(x, weights, *into, *after)


def share_sums(parts, own):
    columns = parts[0].shape[1]
    tile = tile_of(columns, 1536)

    def kernel(*refs):
        total = refs[0][...].astype(F32)
        for ref in refs[1 : len(parts)]:
            total = total + ref[...].astype(F32)
        refs[-2][...] = total[:own].astype(BF16)
        refs[-1][...] = total[own:].astype(BF16)

    return pl.pallas_call(
        kernel,
        grid=(columns // tile,),
        in_specs=[pl.BlockSpec((2 * own, tile), lambda i: (1, i))] * len(parts),
        out_specs=[pl.BlockSpec((own, tile), lambda i: (0, i))] * 2,
        out_shape=[jax.ShapeDtypeStruct((own, columns), BF16)] * 2,
        compiler_params=params(),
        cost_estimate=cost(2 * own * columns, 16 * own * columns),
        name="share_sums",
    )(*parts)


def gated_gradients(d, mine, other, cotangent, first, low, up, own, after=()):
    columns = other.shape[1]
    rank = up.shape[1]
    tile = max(t for t in range(128, 2049, 128) if columns % t == 0 and first % t == 0)
    tiles = columns // tile
    base = first // tile

    def kernel(d_ref, *refs):
        mine_refs = refs[: len(mine)]
        other_ref, flow_ref, low_ref, up_ref = refs[len(mine) : len(mine) + 4]
        mine_out, other_out, back_ref = refs[-3:]
        own_is_gate = d_ref[0] == 0
        total = mine_refs[0][...].astype(F32)
        for ref in mine_refs[1:]:
            total = total + ref[...].astype(F32)
        passed = other_ref[...].astype(F32)
        low_terms = [
            ADAPTER_SCALE
            * jnp.dot(low_ref[:, k * rank : (k + 1) * rank], up_ref[k], preferred_element_type=F32)
            for k in range(2)
        ]
        gate = jnp.where(own_is_gate, total, passed) + low_terms[0]
        upper = jnp.where(own_is_gate, passed, total) + low_terms[1]
        sigma = 1.0 / (1.0 + jnp.exp(-gate))
        flow = flow_ref[...].astype(F32)
        gate_grad = (flow * upper * sigma * (1.0 + gate * (1.0 - sigma))).astype(BF16)
        upper_grad = (flow * gate * sigma).astype(BF16)
        mine_out[...] = jnp.where(own_is_gate, gate_grad, upper_grad)
        other_out[...] = jnp.where(own_is_gate, upper_grad, gate_grad)

        @pl.when(pl.program_id(0) == 0)
        def _():
            back_ref[...] = jnp.zeros_like(back_ref)

        contract = (((1,), (1,)), ((), ()))
        for k, grad in enumerate((gate_grad, upper_grad)):
            back_ref[:, k * rank : (k + 1) * rank] += lax.dot_general(
                grad, up_ref[k], contract, preferred_element_type=F32
            )
        back_ref[:, 2 * rank :] += jnp.sum(
            gate_grad.astype(F32) * gate + upper_grad.astype(F32) * upper, axis=1, keepdims=True
        )

    here = pl.BlockSpec((own, tile), lambda i, d_ref: (0, i))
    there = pl.BlockSpec((own, tile), lambda i, d_ref: (0, base + i))
    return pl.pallas_call(
        kernel,
        grid_spec=pltpu.PrefetchScalarGridSpec(
            num_scalar_prefetch=1,
            grid=(tiles,),
            in_specs=[here] * (len(mine) + 1)
            + [
                there,
                pl.BlockSpec((own, 2 * rank), lambda i, d_ref: (0, 0)),
                pl.BlockSpec((2, rank, tile), lambda i, d_ref: (0, 0, base + i)),
            ]
            + [ANY] * len(after),
            out_specs=[here, here, pl.BlockSpec((own, 2 * rank + 1), lambda i, d_ref: (0, 0))],
        ),
        out_shape=[
            jax.ShapeDtypeStruct((own, columns), BF16),
            jax.ShapeDtypeStruct((own, columns), BF16),
            jax.ShapeDtypeStruct((own, 2 * rank + 1), F32),
        ],
        compiler_params=params(),
        cost_estimate=cost(8 * own * columns * rank, 16 * own * columns),
        name="gated_gradients",
    )(d.reshape(1), *mine, other, cotangent, low, up, *after)


def backward_matmul(pieces, weights, hidden_start, first, tiles, tile, base=None, base_first=0, partial=False, after=()):
    rows = sum(g.shape[0] for g in pieces)
    half = rows // 2
    n_base = 0 if base is None else 1
    hidden = pieces[0].shape[1]

    def kernel(*refs):
        w_ref = refs[len(pieces)]
        g = jnp.concatenate([ref[...] for ref in refs[: len(pieces)]], axis=0)
        y = lax.dot_general(g, w_ref[0], (((1,), (1,)), ((), ())), preferred_element_type=F32)
        if n_base:
            y = y + refs[len(pieces) + 1][...]
        if partial:
            refs[-1][...] = y
        else:
            refs[-2][...] = y[:half]
            refs[-1][...] = y[half:].astype(BF16)

    if partial:
        out_specs = pl.BlockSpec((rows, tile), lambda i: (0, i))
        out_shape = jax.ShapeDtypeStruct((rows, tiles * tile), F32)
    else:
        out_specs = [pl.BlockSpec((half, tile), lambda i: (0, i))] * 2
        out_shape = [
            jax.ShapeDtypeStruct((half, tiles * tile), F32),
            jax.ShapeDtypeStruct((half, tiles * tile), BF16),
        ]
    return pl.pallas_call(
        kernel,
        grid=(tiles,),
        in_specs=[RESIDENT] * len(pieces)
        + [
            pl.BlockSpec(
                (pl.Element(1), pl.Element(tile), pl.Element(hidden)),
                lambda i: (0, (first + i) * tile, hidden_start),
            )
        ]
        + [pl.BlockSpec((rows, tile), lambda i: (0, first - base_first + i))] * n_base
        + [ANY] * len(after),
        out_specs=out_specs,
        out_shape=out_shape,
        compiler_params=params(MATMUL_VMEM_MIB),
        cost_estimate=cost(2 * rows * hidden * tiles * tile, 2 * hidden * (rows + tiles * tile) + (4 + 4 * n_base) * rows * tiles * tile),
        name="backward_matmul",
    )(*pieces, weights, *(() if base is None else (base,)), *after)


def adapter_up(low, groups):
    rank = low.shape[0]

    def kernel(*refs):
        at = 1
        for i, pieces in enumerate(groups):
            g = jnp.concatenate([ref[...] for ref in refs[at : at + len(pieces)]], axis=0)
            at += len(pieces)
            refs[i - len(groups)][...] = ADAPTER_SCALE * jnp.dot(
                refs[0][...], g, preferred_element_type=F32
            )

    operands = [g for pieces in groups for g in pieces]
    widths = [pieces[0].shape[1] for pieces in groups]
    return pl.pallas_call(
        kernel,
        grid=(1,),
        in_specs=[RESIDENT] * (1 + len(operands)),
        out_specs=[pl.BlockSpec((rank, w), lambda i: (0, 0)) for w in widths],
        out_shape=[jax.ShapeDtypeStruct((rank, w), F32) for w in widths],
        compiler_params=params(),
        cost_estimate=cost(2 * rank * low.shape[1] * sum(widths), 2 * low.shape[1] * sum(widths)),
        name="adapter_up",
    )(low, *operands)


def assemble(pieces, places, block, tokens, width, columns, into=None):
    chunk = pieces[0][0].shape[1]
    start = columns // chunk

    def kernel(place_ref, *refs):
        out_ref, token_ref = refs[-2:]
        token_ref[...] = jnp.zeros_like(token_ref)
        i = 0
        count = sum(a.shape[0] // block for a, _ in pieces)
        for k, (a, b) in enumerate(pieces):
            for r in range(0, a.shape[0], block):
                rows = refs[2 * k][r : r + block, :]
                if b is not a:
                    rows = jnp.where(place_ref[count] == 1, rows, refs[2 * k + 1][r : r + block, :])
                out_ref[pl.ds(pl.multiple_of(place_ref[i], block), block), :] = rows
                i += 1

    n_into = 0 if into is None else 1
    operands = [x for pair in pieces for x in pair]
    return pl.pallas_call(
        kernel,
        grid_spec=pltpu.PrefetchScalarGridSpec(
            num_scalar_prefetch=1,
            grid=(1,),
            in_specs=[pl.BlockSpec(x.shape, lambda i, p: (0, 0)) for x in operands] + [ANY] * n_into,
            out_specs=[
                pl.BlockSpec((tokens, chunk), lambda i, p: (0, start)),
                pl.BlockSpec((8, 128), lambda i, p: (0, 0)),
            ],
        ),
        out_shape=[jax.ShapeDtypeStruct((tokens, width), BF16), jax.ShapeDtypeStruct((8, 128), F32)],
        input_output_aliases={len(operands) + 1: 0} if n_into else {},
        compiler_params=params(),
        cost_estimate=cost(0, 4 * tokens * chunk),
        name="assemble",
    )(places, *operands, *((into,) if n_into else ()))


def finish(parts, stream, stats, back, down, steering, gain, columns):
    rows = stream.shape[0]
    width = parts[0].shape[1]
    start = columns // width

    def kernel(*refs):
        part_refs = refs[: len(parts)]
        x_ref, s_ref, back_ref, down_ref, steer_ref, gain_ref, out_ref, sum_ref = refs[len(parts) :]
        total = part_refs[0][...].astype(F32)
        for ref in part_refs[1:]:
            total = total + ref[...].astype(F32)
        total = total + ADAPTER_SCALE * jnp.dot(back_ref[...], down_ref[...], preferred_element_type=F32)
        steered = x_ref[...].astype(F32) + s_ref[:, 0:1] * steer_ref[...]
        grad = s_ref[:, 1:2] * gain_ref[...] * total - s_ref[:, 2:3] * steered
        out_ref[...] = grad.astype(BF16)
        sum_ref[...] = jnp.sum(s_ref[:, 0:1] * grad, axis=0, keepdims=True)

    across = lambda n: pl.BlockSpec((n, width), lambda i: (0, start))
    return pl.pallas_call(
        kernel,
        grid=(1,),
        in_specs=[pl.BlockSpec((rows, width), lambda i: (0, 0))] * len(parts)
        + [
            across(rows),
            pl.BlockSpec(stats.shape, lambda i: (0, 0)),
            pl.BlockSpec(back.shape, lambda i: (0, 0)),
            across(down.shape[0]),
            across(1),
            across(1),
        ],
        out_specs=[pl.BlockSpec((rows, width), lambda i: (0, 0)), pl.BlockSpec((1, width), lambda i: (0, 0))],
        out_shape=[jax.ShapeDtypeStruct((rows, width), BF16), jax.ShapeDtypeStruct((1, width), F32)],
        compiler_params=params(),
        cost_estimate=cost(2 * rows * width * down.shape[0], 10 * rows * width),
        name="finish",
    )(*parts, stream, stats, back, down, steering.reshape(1, -1), gain.reshape(1, -1))


def make_local(dp, hid, ffn):
    def local(stream, steering, strength, gain, weights, down, up, cotangent):
        d, h, f = lax.axis_index("dp"), lax.axis_index("hid"), lax.axis_index("ffn")
        tokens, width = stream.shape
        hidden = weights.shape[2]
        own = tokens // hid
        rank = down.shape[2]
        first_pair = d == 0
        down_rows = jnp.transpose(down, (0, 2, 1)).reshape(2 * rank, width)

        split = width // 2 if hid >= ffn and width % 256 == 0 else width
        if split < width:
            quarter = tokens // ffn
            mine = lax.dynamic_slice(stream, (f * quarter, split), (quarter, width - split))
            far = double(swap(mine, "dp", dp, 1), "ffn", ffn)
            near = swap(stream[:, :split], "dp", dp, 1)
            peer_pieces = [(near, None), (far, GatheredRows(f, ffn, quarter, own))]
        else:
            peer_pieces = [(swap(stream, "dp", dp, 1), None)]
        rows = stream.astype(F32)
        total_rows, total_steer = lax.psum(
            (jnp.sum(rows * rows, axis=1), jnp.sum(steering * steering)), "hid"
        )
        stream_ms = total_rows / MODEL_WIDTH + 1e-06
        steer_ms = total_steer / MODEL_WIDTH + 1e-06
        scale = strength * jnp.sqrt(stream_ms / steer_ms)
        steered = rows + scale[:, None] * steering[None, :]
        steered_power = lax.psum(jnp.sum(steered * steered, axis=1), "hid")
        inv_rms = lax.rsqrt(steered_power / MODEL_WIDTH + 1e-05)
        stats = jnp.stack([scale, inv_rms], axis=1)
        peer_stats = swap(stats, "dp", dp, 1)

        tile = tile_of(hidden, 512)
        count = hidden // tile
        chunks = split_tiles(count, HIDDEN_CHUNKS)
        normed, own_low = normalize([(stream, None)], stats, steering, gain, down_rows, h, hid, 0)
        normed, peer_low = normalize(
            peer_pieces, peer_stats, steering, gain, down_rows, h, hid, 1, into=normed
        )

        low, low_steps = jnp.stack([own_low, peer_low]), []
        for bit in range(bits_of(hid)):
            half = low.shape[1] // 2
            low = low[:, :half] + swap(low[:, half:], "hid", hid, 1 << bit)
            low_steps.append(low)
        low = low.astype(BF16)
        low_own = low[0]

        width_tile = tile_of(width, 512)
        halves = split_tiles(width // width_tile, 2)
        last_bit = 1 << (bits_of(hid) - 1)
        acts, sent, others, grads, back, bases = [], [], [], [], 0.0, []
        mine_grads, peer_grads, own_first, peer_first = [], [], [], []

        def sums_over_hid(c, after_first, after_second):
            first, n = chunks[c]
            middle = (n + 1) // 2
            half_done = forward_matmul(normed, weights, first, n, 0, middle, tile, after=after_first)
            keep, send = forward_matmul(
                normed, weights, first, n, middle, n, tile, into=half_done, after=after_second()
            )
            parts = [keep, swap(send, "hid", hid, 1)]
            for bit in range(1, bits_of(hid) - 1):
                size = parts[-1].shape[0]
                send = total_of(parts, size // 2, size).astype(BF16)
                parts.append(swap(send, "hid", hid, 1 << bit))
            sent.append(share_sums(parts, own))
            peer_got = swap(sent[-1][1], "hid", hid, last_bit)
            own_got = swap(sent[-1][0], "hid", hid, last_bit)
            acts.append((parts, own_got, peer_got))
            others.append(
                swap((total_of(parts, own, 2 * own) + peer_got.astype(F32)).astype(BF16), "dp", dp, 1)
            )

        def gradients(c, after):
            parts, own_got, _ = acts[c]
            mine_grad, other_grad, back_part = gated_gradients(
                d, parts + [own_got], others[c], cotangent, chunks[c][0] * tile, low_own, up, own, after
            )
            peer_grad = swap(other_grad, "dp", dp, 1)
            pieces = []
            for g, firsts in ((mine_grad, own_first), (peer_grad, peer_first)):
                blocks = [g]
                for bit in reversed(range(bits_of(hid))):
                    blocks += [swap(x, "hid", hid, 1 << bit) for x in blocks]
                firsts.append(blocks[1])
                pieces += blocks
            mine_grads.append(mine_grad)
            peer_grads.append(peer_grad)
            grads.append(pieces)
            return back + back_part

        def partial_sums(c, which, base, after):
            first, n = halves[which]
            return backward_matmul(
                grads[c], weights, chunks[c][0] * tile, first, n, width_tile,
                base=base, base_first=first, partial=True, after=after,
            )

        end = len(chunks) - 1
        for c in range(len(chunks)):
            before = tuple(sent[-1]) if c else ()
            if c >= 2:
                back = gradients(c - 2, (peer_grads[-1], own_first[-1]) if c >= 3 else ())
                before += (mine_grads[-1],)

            def between():
                wait = tuple(low_steps[c : c + 1])
                if c:
                    wait += acts[c - 1][1:]
                if c and c == end:
                    nonlocal back
                    back = gradients(c - 1, (peer_grads[-1], own_first[-1]) if c >= 2 else ())
                    wait += (mine_grads[-1],)
                return wait

            sums_over_hid(c, before, between)
        bases = [partial_sums(0, 0, None, tuple(sent[-1]) + (own_first[-1], peer_first[-1]))]
        bases.append(partial_sums(0, 1, None, (bases[0], acts[end][2])))
        back = gradients(end, (bases[1],))
        wait = (peer_grads[-1], own_first[-1])
        for c in range(1, end):
            for which in range(2):
                bases[which] = partial_sums(c, which, bases[which], wait)
                wait = (peer_first[-1],)
        base = bases[-1]
        bases = [(halves[i][0], bases[i]) for i in range(2)]

        for bit in range(bits_of(ffn)):
            back = back + swap(back, "ffn", ffn, 1 << bit)
        back = ordered(back, base)
        back = jnp.stack([back, swap(back, "dp", dp, 1)])
        back = double(back, "hid", hid, dim=1)
        back_low = back[:, :, : 2 * rank].astype(BF16)
        acts_product = back[0, :, 2 * rank]

        line = ffn == 4
        shard = tokens // 2 if line else tokens // ffn
        place = f >> 1 if line else reversed_bits(f, bits_of(ffn))
        middle = (f == 1) | (f == 2)
        block = min(own, shard)

        def natural(row):
            index = row // own
            return (h ^ reversed_bits(index, bits_of(hid))) * own + row % own

        def shard_rows(x):
            return jnp.concatenate(
                [
                    lax.dynamic_slice_in_dim(x, natural(place * shard + i * block), block, axis=0)
                    for i in range(shard // block)
                ],
                axis=0,
            )

        stats_shard = shard_rows(stats)
        dot_shard = lax.dynamic_slice_in_dim(acts_product, place * shard, shard, axis=0)
        dot_factor = stats_shard[:, 1] ** 2 * dot_shard / MODEL_WIDTH
        stats_shard = jnp.concatenate([stats_shard, dot_factor[:, None]], axis=1)
        stream_shard = shard_rows(stream)
        back_shard = lax.dynamic_slice_in_dim(back_low[0], place * shard, shard, axis=0)

        out, sums, gathered, written = None, [], [], []
        tiles = width // width_tile
        steps = [(0, 2), (2, 2), (4, 2), (6, 1), (7, 1)] if tiles == 8 else split_tiles(tiles, 4)
        products, received = [], []
        for first, n in steps:
            held_first, held = [b for b in bases if b[0] <= first][-1]
            keep, send = backward_matmul(
                grads[-1], weights, chunks[-1][0] * tile, first, n, width_tile,
                base=held, base_first=held_first,
            )
            products.append(keep)
            received.append(swap(send, "dp", dp, 1))
        owners = [place, 1 - place] if line else [
            reversed_bits(f ^ reversed_bits(p, bits_of(ffn)), bits_of(ffn)) for p in range(ffn)
        ]
        places = [natural(o * shard + i * block) for o in owners for i in range(shard // block)]
        places = jnp.stack(places + [jnp.where(middle, 1, 0).astype(places[0].dtype)])

        def send_line(x, pairs):
            return lax.ppermute(x, "ffn", pairs)

        for j, (first, n) in enumerate(steps):
            got = ordered(received[j], products[min(j + 2, len(steps) - 1)])
            if j >= 2:
                got = ordered(got, *gathered[j - 2], *(written[j - 3 : j - 2] if j >= 3 else ()))
            if line:
                part = products[j] + got.astype(F32)
                total = part + send_line(part.astype(BF16), [(0, 1), (3, 2)]).astype(F32)
                upper = place == 1
                keep = jnp.where(upper, total[shard:], total[:shard])
                send = jnp.where(upper, total[:shard], total[shard:]).astype(BF16)
                parts = [keep, send_line(send, [(1, 2), (2, 1)])]
            else:
                parts = [products[j], got]
                for bit in range(bits_of(ffn)):
                    half = parts[-1].shape[0] // 2
                    mine = (f >> bit) & 1
                    sides = [
                        [lax.dynamic_slice_in_dim(p, side * half, half, axis=0) for p in parts]
                        for side in (mine, 1 - mine)
                    ]
                    parts = [total_of(sides[0], 0, half)] + [
                        swap(total_of(sides[1], 0, half).astype(BF16), "ffn", ffn, 1 << bit)
                    ]
            result, sum_part = finish(
                parts, stream_shard, stats_shard, back_shard, down_rows, steering, gain, first * width_tile
            )
            if line:
                sum_part = jnp.where(middle, sum_part, 0.0)
                outward = [(1, 0), (2, 3)]
                other = send_line(result, [(1, 2), (2, 1)])
                pieces = [(result, send_line(result, outward)), (other, send_line(other, outward))]
            else:
                blocks = [result]
                for bit in reversed(range(bits_of(ffn))):
                    blocks += [swap(x, "ffn", ffn, 1 << bit) for x in blocks]
                other = blocks[1]
                pieces = [(x, x) for x in blocks]
            sums.append(sum_part)
            gathered.append((other, pieces[0][1]))
            out, token = assemble(pieces, places, block, tokens, width, first * width_tile, into=out)
            written.append(token)

        steering_gradient = jnp.concatenate(sums, axis=1)
        for bit in range(bits_of(ffn)):
            steering_gradient = steering_gradient + swap(steering_gradient, "ffn", ffn, 1 << bit)
        steering_gradient = steering_gradient + swap(steering_gradient, "dp", dp, 1)

        low_mine = jnp.where(first_pair, low[:, :, :rank], low[:, :, rank:])
        low_mine = double(ordered(low_mine, base), "hid", hid, dim=1).reshape(2 * tokens, rank)
        up_mine = jnp.concatenate(adapter_up(ordered(low_mine.T, products[-1]), grads), axis=1)
        up_other = swap(ordered(up_mine.astype(BF16), received[-1]), "dp", dp, 1).astype(F32)
        up_gradient = jnp.where(
            first_pair, jnp.stack([up_mine, up_other]), jnp.stack([up_other, up_mine])
        )
        back_rows = back_low.reshape(2, hid, own, 2 * rank).transpose(1, 0, 2, 3).reshape(2 * tokens, 2 * rank)
        down_gradient = lax.dot_general(
            back_rows, normed, (((0,), (0,)), ((), ())), preferred_element_type=F32
        )
        down_gradient = jnp.transpose(
            (ADAPTER_SCALE * down_gradient).reshape(2, rank, width), (0, 2, 1)
        )
        return out, steering_gradient.reshape(width), down_gradient, up_gradient

    return local


def solution(mesh):
    in_specs = (
        P("dp", "hid"),
        P("hid"),
        P("dp"),
        P("hid"),
        P("dp", "hid", "ffn"),
        P(None, "hid", None),
        P(None, None, "ffn"),
        P(("dp", "hid"), "ffn"),
    )
    out_specs = (P("dp", "hid"), P("hid"), P(None, "hid", None), P(None, None, "ffn"))
    local = make_local(mesh.shape["dp"], mesh.shape["hid"], mesh.shape["ffn"])
    return jax.shard_map(local, mesh=mesh, in_specs=in_specs, out_specs=out_specs, check_vma=False)
```

```python
import jax
import jax.numpy as jnp
from jax import lax
from jax.experimental import pallas as pl
from jax.experimental.pallas import tpu as pltpu
from jax.sharding import PartitionSpec as P

MODEL_WIDTH = 16384
ADAPTER_SCALE = 0.5
VMEM_MIB = 12
MATMUL_VMEM_MIB = 18
COST_SHARE = 0.01

F32 = jnp.float32
BF16 = jnp.bfloat16
ANY = pl.BlockSpec(memory_space=pl.ANY)
RESIDENT = pl.BlockSpec(memory_space=pltpu.VMEM)


def bits_of(n):
    return n.bit_length() - 1


def reversed_bits(x, n):
    out = 0
    for i in range(n):
        out = out + (((x >> i) & 1) << (n - 1 - i))
    return out


def tile_of(n, cap):
    return max(t for t in range(128, cap + 1, 128) if n % t == 0)


def split_tiles(count, parts):
    edges = [count * i // parts for i in range(parts + 1)]
    return [(a, b - a) for a, b in zip(edges, edges[1:]) if b > a]


def swap(x, axis, n, mask):
    return lax.ppermute(x, axis, [(i, i ^ mask) for i in range(n)])


def double(x, axis, n, dim=0):
    for bit in reversed(range(bits_of(n))):
        x = jnp.concatenate([x, swap(x, axis, n, 1 << bit)], axis=dim)
    return x


def ordered(x, *first):
    return lax.optimization_barrier((x, *first))[0]


def total_of(parts, start, stop):
    out = parts[0][start:stop]
    for part in parts[1:]:
        out = out + part[start:stop].astype(F32)
    return out


def params(mib=VMEM_MIB):
    return pltpu.CompilerParams(vmem_limit_bytes=mib * 1024 * 1024)


def cost(flops, size):
    return pl.CostEstimate(
        flops=int(flops * COST_SHARE), bytes_accessed=int(size * COST_SHARE), transcendentals=0
    )


def normalize(stream, stats, steering, gain, down, h, hid, beside=None):
    tokens, width = stream.shape
    block = tokens // hid
    ranks = down.shape[0]
    n_beside = 0 if beside is None else 1

    def token_block(p, h_ref):
        return h_ref[0] ^ reversed_bits(p, bits_of(hid))

    def kernel(h_ref, x_ref, stat_ref, steer_ref, gain_ref, down_ref, *refs):
        steered = x_ref[...].astype(F32) + stat_ref[:, :1] * steer_ref[...]
        normed = (steered * stat_ref[:, 1:] * gain_ref[...]).astype(BF16)
        out_ref, low_ref = refs[n_beside : n_beside + 2]
        out_ref[...] = normed
        low_ref[...] = lax.dot_general(
            normed, down_ref[...], (((1,), (1,)), ((), ())), preferred_element_type=F32
        )
        if n_beside:
            refs[-1][:block, :] = refs[0][...]
            refs[-1][block:, :] = normed

    whole = lambda n: pl.BlockSpec((n, width), lambda p, h_ref: (0, 0))
    rows = lambda n, m: pl.BlockSpec((n, m), lambda p, h_ref: (p, 0))
    return pl.pallas_call(
        kernel,
        grid_spec=pltpu.PrefetchScalarGridSpec(
            num_scalar_prefetch=1,
            grid=(hid,),
            in_specs=[
                pl.BlockSpec((block, width), lambda p, h_ref: (token_block(p, h_ref), 0)),
                pl.BlockSpec((block, 2), lambda p, h_ref: (token_block(p, h_ref), 0)),
                whole(1),
                whole(1),
                whole(ranks),
            ]
            + [rows(block, width)] * n_beside,
            out_specs=[rows(block, width), rows(block, ranks)] + [rows(2 * block, width)] * n_beside,
        ),
        out_shape=[
            jax.ShapeDtypeStruct((tokens, width), BF16),
            jax.ShapeDtypeStruct((tokens, ranks), F32),
        ]
        + [jax.ShapeDtypeStruct((2 * tokens, width), BF16)] * n_beside,
        compiler_params=params(),
        cost_estimate=cost(2 * tokens * width * ranks, 4 * tokens * width),
        name="normalize",
    )(
        h.reshape(1),
        stream,
        stats,
        steering.reshape(1, width),
        gain.reshape(1, width),
        down,
        *((beside,) if n_beside else ()),
    )


def forward_matmul(x, weights, first, tiles, start, stop, tile, into=(), after=()):
    rows, depth = x.shape
    half = rows // 2

    def kernel(x_ref, w_ref, *refs):
        keep_ref, send_ref, token_ref = refs[-3:]
        token_ref[...] = jnp.zeros_like(token_ref)
        y = jnp.dot(x_ref[...], w_ref[0], preferred_element_type=F32)
        keep_ref[...] = y[:half]
        send_ref[...] = y[half:].astype(BF16)

    return pl.pallas_call(
        kernel,
        grid=(stop - start,),
        in_specs=[RESIDENT, pl.BlockSpec((1, depth, tile), lambda i: (0, 0, first + start + i))]
        + [ANY] * (len(into) + len(after)),
        out_specs=[pl.BlockSpec((half, tile), lambda i: (0, start + i))] * 2
        + [pl.BlockSpec((8, 128), lambda i: (0, 0))],
        out_shape=[
            jax.ShapeDtypeStruct((half, tiles * tile), F32),
            jax.ShapeDtypeStruct((half, tiles * tile), BF16),
            jax.ShapeDtypeStruct((8, 128), F32),
        ],
        input_output_aliases={2 + i: i for i in range(len(into))},
        compiler_params=params(MATMUL_VMEM_MIB),
        cost_estimate=cost(2 * rows * depth * (stop - start) * tile, 2 * depth * (rows + (stop - start) * tile) + 6 * half * (stop - start) * tile),
        name="forward_matmul",
    )(x, weights, *into, *after)


def share_sums(parts, rows, count, after=(), places=None):
    columns = parts[0].shape[1]
    tile = tile_of(columns, 1792)

    def kernel(*refs):
        total = refs[0][...].astype(F32)
        for ref in refs[1 : len(parts)]:
            total = total + ref[...].astype(F32)
        for i in range(count):
            refs[i - count][...] = total[i * rows : (i + 1) * rows].astype(BF16)

    return pl.pallas_call(
        kernel,
        grid=(columns // tile,),
        in_specs=[
            pl.BlockSpec((count * rows, tile), lambda i, at=at: (at, i)) for at in places or [1] * len(parts)
        ]
        + [ANY] * len(after),
        out_specs=[pl.BlockSpec((rows, tile), lambda i: (0, i))] * count,
        out_shape=[jax.ShapeDtypeStruct((rows, columns), BF16)] * count,
        compiler_params=params(),
        cost_estimate=cost(count * rows * columns, 8 * count * rows * columns),
        name="share_sums",
    )(*parts, *after)


def gated_gradients(d, mine, other, cotangent, first, low, up, own, after=()):
    columns = other.shape[1]
    rank = up.shape[1]
    tile = max(t for t in range(128, 2049, 128) if columns % t == 0 and first % t == 0)
    tiles = columns // tile
    base = first // tile

    def kernel(d_ref, *refs):
        mine_refs = refs[: len(mine)]
        other_ref, flow_ref, low_ref, up_ref = refs[len(mine) : len(mine) + 4]
        mine_out, other_out, back_ref = refs[-3:]
        own_is_gate = d_ref[0] == 0
        total = mine_refs[0][...].astype(F32)
        for ref in mine_refs[1:]:
            total = total + ref[...].astype(F32)
        passed = other_ref[...].astype(F32)
        low_terms = [
            ADAPTER_SCALE
            * jnp.dot(low_ref[:, k * rank : (k + 1) * rank], up_ref[k], preferred_element_type=F32)
            for k in range(2)
        ]
        gate = jnp.where(own_is_gate, total, passed) + low_terms[0]
        upper = jnp.where(own_is_gate, passed, total) + low_terms[1]
        sigma = 1.0 / (1.0 + jnp.exp(-gate))
        flow = flow_ref[...].astype(F32)
        gate_grad = (flow * upper * sigma * (1.0 + gate * (1.0 - sigma))).astype(BF16)
        upper_grad = (flow * gate * sigma).astype(BF16)
        mine_out[...] = jnp.where(own_is_gate, gate_grad, upper_grad)
        other_out[...] = jnp.where(own_is_gate, upper_grad, gate_grad)

        @pl.when(pl.program_id(0) == 0)
        def _():
            back_ref[...] = jnp.zeros_like(back_ref)

        contract = (((1,), (1,)), ((), ()))
        for k, grad in enumerate((gate_grad, upper_grad)):
            back_ref[:, k * rank : (k + 1) * rank] += lax.dot_general(
                grad, up_ref[k], contract, preferred_element_type=F32
            )
        back_ref[:, 2 * rank :] += jnp.sum(
            gate_grad.astype(F32) * gate + upper_grad.astype(F32) * upper, axis=1, keepdims=True
        )

    here = pl.BlockSpec((own, tile), lambda i, d_ref: (0, i))
    there = pl.BlockSpec((own, tile), lambda i, d_ref: (0, base + i))
    return pl.pallas_call(
        kernel,
        grid_spec=pltpu.PrefetchScalarGridSpec(
            num_scalar_prefetch=1,
            grid=(tiles,),
            in_specs=[here] * (len(mine) + 1)
            + [
                there,
                pl.BlockSpec((own, 2 * rank), lambda i, d_ref: (0, 0)),
                pl.BlockSpec((2, rank, tile), lambda i, d_ref: (0, 0, base + i)),
            ]
            + [ANY] * len(after),
            out_specs=[here, here, pl.BlockSpec((own, 2 * rank + 1), lambda i, d_ref: (0, 0))],
        ),
        out_shape=[
            jax.ShapeDtypeStruct((own, columns), BF16),
            jax.ShapeDtypeStruct((own, columns), BF16),
            jax.ShapeDtypeStruct((own, 2 * rank + 1), F32),
        ],
        compiler_params=params(),
        cost_estimate=cost(8 * own * columns * rank, 16 * own * columns),
        name="gated_gradients",
    )(d.reshape(1), *mine, other, cotangent, low, up, *after)


def backward_matmul(pieces, weights, hidden_start, first, tiles, tile, base=None, base_first=0, partial=False, after=()):
    rows = sum(g.shape[0] for g in pieces)
    half = rows // 2
    n_base = 0 if base is None else 1
    hidden = pieces[0].shape[1]

    def kernel(*refs):
        w_ref = refs[len(pieces)]
        g = jnp.concatenate([ref[...] for ref in refs[: len(pieces)]], axis=0)
        y = lax.dot_general(g, w_ref[0], (((1,), (1,)), ((), ())), preferred_element_type=F32)
        if n_base:
            y = y + refs[len(pieces) + 1][...]
        if partial:
            refs[-1][...] = y
        else:
            refs[-2][...] = y[:half]
            refs[-1][...] = y[half:].astype(BF16)

    if partial:
        out_specs = pl.BlockSpec((rows, tile), lambda i: (0, i))
        out_shape = jax.ShapeDtypeStruct((rows, tiles * tile), F32)
    else:
        out_specs = [pl.BlockSpec((half, tile), lambda i: (0, i))] * 2
        out_shape = [
            jax.ShapeDtypeStruct((half, tiles * tile), F32),
            jax.ShapeDtypeStruct((half, tiles * tile), BF16),
        ]
    return pl.pallas_call(
        kernel,
        grid=(tiles,),
        in_specs=[RESIDENT] * len(pieces)
        + [
            pl.BlockSpec(
                (pl.Element(1), pl.Element(tile), pl.Element(hidden)),
                lambda i: (0, (first + i) * tile, hidden_start),
            )
        ]
        + [pl.BlockSpec((rows, tile), lambda i: (0, first - base_first + i))] * n_base
        + [ANY] * len(after),
        out_specs=out_specs,
        out_shape=out_shape,
        compiler_params=params(MATMUL_VMEM_MIB),
        cost_estimate=cost(2 * rows * hidden * tiles * tile, 2 * hidden * (rows + tiles * tile) + (4 + 4 * n_base) * rows * tiles * tile),
        name="backward_matmul",
    )(*pieces, weights, *(() if base is None else (base,)), *after)


def adapter_products(low, groups):
    rank = low.shape[0]

    def kernel(*refs):
        at = 1
        for i, pieces in enumerate(groups):
            g = jnp.concatenate([ref[...] for ref in refs[at : at + len(pieces)]], axis=0)
            at += len(pieces)
            refs[i - len(groups)][...] = ADAPTER_SCALE * jnp.dot(
                refs[0][...], g, preferred_element_type=F32
            )

    operands = [g for pieces in groups for g in pieces]
    widths = [pieces[0].shape[1] for pieces in groups]
    return pl.pallas_call(
        kernel,
        grid=(1,),
        in_specs=[RESIDENT] * (1 + len(operands)),
        out_specs=[pl.BlockSpec((rank, w), lambda i: (0, 0)) for w in widths],
        out_shape=[jax.ShapeDtypeStruct((rank, w), F32) for w in widths],
        compiler_params=params(),
        cost_estimate=cost(2 * rank * low.shape[1] * sum(widths), 2 * low.shape[1] * sum(widths)),
        name="adapter_products",
    )(low, *operands)


def assemble(pieces, places, block, tokens, width, columns, into=None):
    chunk = pieces[0].shape[1]

    def kernel(place_ref, *refs):
        out_ref = refs[-1]
        i = 0
        for ref in refs[: len(pieces)]:
            for r in range(0, ref.shape[0], block):
                out_ref[pl.ds(pl.multiple_of(place_ref[i], block), block), :] = ref[r : r + block, :]
                i += 1

    n_into = 0 if into is None else 1
    return pl.pallas_call(
        kernel,
        grid_spec=pltpu.PrefetchScalarGridSpec(
            num_scalar_prefetch=1,
            grid=(1,),
            in_specs=[pl.BlockSpec(x.shape, lambda i, p: (0, 0)) for x in pieces] + [ANY] * n_into,
            out_specs=pl.BlockSpec((pl.Element(tokens), pl.Element(chunk)), lambda i, p: (0, columns)),
        ),
        out_shape=jax.ShapeDtypeStruct((tokens, width), BF16),
        input_output_aliases={len(pieces) + 1: 0} if n_into else {},
        compiler_params=params(),
        cost_estimate=cost(0, 4 * tokens * chunk),
        name="assemble",
    )(places, *pieces, *((into,) if n_into else ()))


def finish(parts, stream, stats, back, down, steering, gain, columns):
    rows = stream.shape[0]
    width = parts[0].shape[1]

    def kernel(*refs):
        part_refs = refs[: len(parts)]
        x_ref, s_ref, back_ref, down_ref, steer_ref, gain_ref, out_ref, sum_ref = refs[len(parts) :]
        total = part_refs[0][...].astype(F32)
        for ref in part_refs[1:]:
            total = total + ref[...].astype(F32)
        total = total + ADAPTER_SCALE * jnp.dot(back_ref[...], down_ref[...], preferred_element_type=F32)
        steered = x_ref[...].astype(F32) + s_ref[:, 0:1] * steer_ref[...]
        grad = s_ref[:, 1:2] * gain_ref[...] * total - s_ref[:, 2:3] * steered
        out_ref[...] = grad.astype(BF16)
        sum_ref[...] = jnp.sum(s_ref[:, 0:1] * grad, axis=0, keepdims=True)

    across = lambda n: pl.BlockSpec((pl.Element(n), pl.Element(width)), lambda i: (0, columns))
    return pl.pallas_call(
        kernel,
        grid=(1,),
        in_specs=[pl.BlockSpec((rows, width), lambda i: (0, 0))] * len(parts)
        + [
            across(rows),
            pl.BlockSpec(stats.shape, lambda i: (0, 0)),
            pl.BlockSpec(back.shape, lambda i: (0, 0)),
            across(down.shape[0]),
            across(1),
            across(1),
        ],
        out_specs=[pl.BlockSpec((rows, width), lambda i: (0, 0)), pl.BlockSpec((1, width), lambda i: (0, 0))],
        out_shape=[jax.ShapeDtypeStruct((rows, width), BF16), jax.ShapeDtypeStruct((1, width), F32)],
        compiler_params=params(),
        cost_estimate=cost(2 * rows * width * down.shape[0], 10 * rows * width),
        name="finish",
    )(*parts, stream, stats, back, down, steering.reshape(1, -1), gain.reshape(1, -1))


def make_local(dp, hid, ffn):
    def local(stream, steering, strength, gain, weights, down, up, cotangent):
        d, h, f = lax.axis_index("dp"), lax.axis_index("hid"), lax.axis_index("ffn")
        tokens, width = stream.shape
        hidden = weights.shape[2]
        own = tokens // hid
        rank = down.shape[2]
        first_pair = d == 0
        down_rows = jnp.transpose(down, (0, 2, 1)).reshape(2 * rank, width)

        peer_stream = swap(stream, "dp", dp, 1)
        rows = stream.astype(F32)
        total_rows, total_steer = lax.psum(
            (jnp.sum(rows * rows, axis=1), jnp.sum(steering * steering)), "hid"
        )
        stream_ms = total_rows / MODEL_WIDTH + 1e-06
        steer_ms = total_steer / MODEL_WIDTH + 1e-06
        scale = strength * jnp.sqrt(stream_ms / steer_ms)
        steered = rows + scale[:, None] * steering[None, :]
        steered_power = lax.psum(jnp.sum(steered * steered, axis=1), "hid")
        inv_rms = lax.rsqrt(steered_power / MODEL_WIDTH + 1e-05)
        stats = jnp.stack([scale, inv_rms], axis=1)
        peer_stats = swap(stats, "dp", dp, 1)

        tile = tile_of(hidden, 512)
        count = hidden // tile
        chunks = [(0, (count + 1) // 2), ((count + 1) // 2, count // 2)]
        last_bit = 1 << (bits_of(hid) - 1)
        own_normed, own_low = normalize(stream, stats, steering, gain, down_rows, h, hid)
        def forward(x, c, edges, afters):
            first, n = chunks[c]
            out, token = (), None
            for start, stop, after in zip(edges, edges[1:], afters):
                *out, token = forward_matmul(
                    x, weights, first, n, start, stop, tile, into=tuple(out), after=after(token)
                )
            keep, send = out
            parts = [keep, swap(send, "hid", hid, 1)]
            for bit in range(1, bits_of(hid) - 1):
                size = parts[-1].shape[0]
                send = total_of(parts, size // 2, size).astype(BF16)
                parts.append(swap(send, "hid", hid, 1 << bit))
            return parts

        own_parts = forward(own_normed, 0, (0, chunks[0][1]), (lambda t: (),))
        (own_send,) = share_sums(own_parts, own, 1)
        own_got = swap(own_send, "hid", hid, last_bit)
        peer_normed, peer_low, normed = normalize(
            peer_stream, ordered(peer_stats, own_send), steering, gain, down_rows, h, hid, own_normed
        )

        low, low_steps = jnp.stack([own_low, peer_low]), []
        for bit in range(bits_of(hid)):
            half = low.shape[1] // 2
            low = low[:, :half] + swap(low[:, half:], "hid", hid, 1 << bit)
            low_steps.append(low)
        low = low.astype(BF16)
        low_own = low[0]

        width_tile = tile_of(width, 512)
        tiles = width // width_tile
        steps = [(0, 3), (3, 3), (6, 2)] if tiles == 8 else split_tiles(tiles, 3)
        acts, others, grads = [], [], []

        n = chunks[0][1]
        peer_parts = forward(
            peer_normed, 0, (0, (n + 1) // 2, n), (lambda t: (own_send,), lambda t: (low_steps[0], own_got))
        )
        (peer_send,) = share_sums(peer_parts, own, 1, (low_own,))
        peer_got = swap(peer_send, "hid", hid, last_bit)
        acts.append(own_parts + [own_got])

        def pass_on(token):
            terms = peer_parts + [peer_got]
            (passed,) = share_sums(terms, own, 1, (token,), [0] * len(terms))
            others.append(swap(passed, "dp", dp, 1))
            return peer_got, passed

        n = chunks[1][1]
        first_send = peer_send
        parts = forward(
            normed, 1, (0, n // 3, n - 1, n), (lambda t: (first_send,), pass_on, lambda t: (others[0],))
        )
        own_send, peer_send = share_sums(parts, own, 2)
        peer_got = swap(peer_send, "hid", hid, last_bit)
        own_got = swap(own_send, "hid", hid, last_bit)
        (passed,) = share_sums(parts + [peer_got], own, 1, (), [1] * len(parts) + [0])
        acts.append(parts + [own_got])
        others.append(swap(passed, "dp", dp, 1))

        def gradients(c, after):
            mine_grad, other_grad, back_part = gated_gradients(
                d, acts[c], others[c], cotangent, chunks[c][0] * tile, low_own, up, own, after
            )
            return back_part, mine_grad, swap(other_grad, "dp", dp, 1)

        def spread(*gradients):
            pieces = []
            for g in gradients:
                blocks = [g]
                for bit in reversed(range(bits_of(hid))):
                    blocks += [swap(x, "hid", hid, 1 << bit) for x in blocks]
                pieces += blocks
            grads.append(pieces)

        back, mine_grad, peer_grad = gradients(0, ())
        (peer_grad,) = share_sums([peer_grad], own, 1, (peer_got,), [0])
        spread(mine_grad, peer_grad)
        bases = []

        def first_half(j, after):
            first, n = steps[j]
            bases.append(
                backward_matmul(
                    grads[0], weights, 0, first, n, width_tile, partial=True, after=after
                )
            )

        first_half(0, (passed,))
        more, mine_grad, peer_grad = gradients(1, (peer_grad, bases[0]))
        back = back + more
        for j in range(1, len(steps)):
            first_half(j, (mine_grad,) if j == 1 else (peer_grad,))
            if j == 1:
                peer_grad = ordered(peer_grad, bases[1])
        spread(mine_grad, peer_grad)

        for bit in range(bits_of(ffn)):
            back = back + swap(back, "ffn", ffn, 1 << bit)
        back = jnp.stack([back, swap(back, "dp", dp, 1)])
        shard = tokens // ffn
        place = reversed_bits(f, bits_of(ffn))
        products, received = [], []

        def halving_step(parts, bit):
            half = parts[-1].shape[0] // 2
            mine = (f >> bit) & 1
            sides = [
                [lax.dynamic_slice_in_dim(p, side * half, half, axis=0) for p in parts]
                for side in (mine, 1 - mine)
            ]
            return total_of(sides[0], 0, half), total_of(sides[1], 0, half).astype(BF16)

        first_steps = []
        for j, ((first, n), base) in enumerate(zip(steps, bases)):
            wait = (products[-1] if products else bases[-1],)
            if j == 2:
                first_steps.append(halving_step([products[0], received[0]], 0))
                wait += (first_steps[0][1],)
            keep, send = backward_matmul(
                grads[1], weights, chunks[1][0] * tile, first, n, width_tile, base=base, base_first=first,
                after=wait,
            )
            products.append(keep)
            received.append(swap(send, "dp", dp, 1))
        begun = first_steps[0][1] if first_steps else products[-1]
        back = double(ordered(back, begun), "hid", hid, dim=1)
        back_low = back[:, :, : 2 * rank].astype(BF16)
        acts_product = back[0, :, 2 * rank]

        block = min(own, shard)

        def natural(row):
            index = row // own
            return (h ^ reversed_bits(index, bits_of(hid))) * own + row % own

        def shard_rows(x):
            return jnp.concatenate(
                [
                    lax.dynamic_slice_in_dim(x, natural(place * shard + i * block), block, axis=0)
                    for i in range(shard // block)
                ],
                axis=0,
            )

        stats_shard = shard_rows(stats)
        dot_shard = lax.dynamic_slice_in_dim(acts_product, place * shard, shard, axis=0)
        dot_factor = stats_shard[:, 1] ** 2 * dot_shard / MODEL_WIDTH
        stats_shard = jnp.concatenate([stats_shard, dot_factor[:, None]], axis=1)
        stream_shard = shard_rows(stream)
        back_shard = lax.dynamic_slice_in_dim(back_low[0], place * shard, shard, axis=0)

        out, sums, gathered = None, [], []
        owners = [reversed_bits(f ^ reversed_bits(p, bits_of(ffn)), bits_of(ffn)) for p in range(ffn)]
        places = jnp.stack([natural(o * shard + i * block) for o in owners for i in range(shard // block)])
        for j, (first, n) in enumerate(steps):
            got = received[j]
            if j == 1:
                got = ordered(got, products[-1])
            elif j >= 2:
                got = ordered(got, gathered[j - 2][1])
            parts = [products[j], got]
            for bit in range(bits_of(ffn)):
                if bit == 0 and j < len(first_steps):
                    keep, send = first_steps[j]
                else:
                    keep, send = halving_step(parts, bit)
                if j == 2 and bit == 1:
                    send = ordered(send, gathered[0][-1])
                parts = [keep, swap(send, "ffn", ffn, 1 << bit)]
            result, sum_part = finish(
                parts, stream_shard, stats_shard, back_shard, down_rows, steering, gain, first * width_tile
            )
            sums.append(sum_part)
            blocks = [result]
            for bit in reversed(range(bits_of(ffn))):
                if j == len(steps) - 1 and bit == 0:
                    steering_gradient = lax.psum(jnp.concatenate(sums, axis=1), ("dp", "ffn"))
                    blocks = [ordered(x, steering_gradient) for x in blocks]
                blocks += [swap(x, "ffn", ffn, 1 << bit) for x in blocks]
            gathered.append(blocks)
            out = assemble(blocks, places, block, tokens, width, first * width_tile, into=out)

        low_mine = jnp.where(first_pair, low[:, :, :rank], low[:, :, rank:])
        low_mine = double(ordered(low_mine, begun), "hid", hid, dim=1).reshape(2 * tokens, rank)
        up_mine = jnp.concatenate(adapter_products(ordered(low_mine.T, products[-1]), grads), axis=1)
        up_other = swap(ordered(up_mine.astype(BF16), received[-1]), "dp", dp, 1).astype(F32)
        up_gradient = jnp.where(
            first_pair, jnp.stack([up_mine, up_other]), jnp.stack([up_other, up_mine])
        )
        back_rows = back_low.reshape(2, hid, own, 2 * rank).transpose(1, 0, 2, 3).reshape(2 * tokens, 2 * rank)
        (down_gradient,) = adapter_products(back_rows.T, [[normed]])
        down_gradient = jnp.transpose(
            down_gradient.reshape(2, rank, width), (0, 2, 1)
        )
        return out, steering_gradient.reshape(width), down_gradient, up_gradient

    return local


def solution(mesh):
    in_specs = (
        P("dp", "hid"),
        P("hid"),
        P("dp"),
        P("hid"),
        P("dp", "hid", "ffn"),
        P(None, "hid", None),
        P(None, None, "ffn"),
        P(("dp", "hid"), "ffn"),
    )
    out_specs = (P("dp", "hid"), P("hid"), P(None, "hid", None), P(None, None, "ffn"))
    local = make_local(mesh.shape["dp"], mesh.shape["hid"], mesh.shape["ffn"])
    return jax.shard_map(local, mesh=mesh, in_specs=in_specs, out_specs=out_specs, check_vma=False)
```

```python
import jax
import jax.numpy as jnp
from jax import lax
from jax.experimental import pallas as pl
from jax.experimental.pallas import tpu as pltpu
from jax.sharding import PartitionSpec as P

MODEL_WIDTH = 16384
ADAPTER_SCALE = 0.5
VMEM_MIB = 12
MATMUL_VMEM_MIB = 24
COST_SHARE = 0.01

F32 = jnp.float32
BF16 = jnp.bfloat16
ANY = pl.BlockSpec(memory_space=pl.ANY)
RESIDENT = pl.BlockSpec(memory_space=pltpu.VMEM)


def bits_of(n):
    return n.bit_length() - 1


def reversed_bits(x, n):
    out = 0
    for i in range(n):
        out = out + (((x >> i) & 1) << (n - 1 - i))
    return out


def tile_of(n, cap):
    return max(t for t in range(128, cap + 1, 128) if n % t == 0)


def split_tiles(count, parts):
    edges = [count * i // parts for i in range(parts + 1)]
    return [(a, b - a) for a, b in zip(edges, edges[1:]) if b > a]


def swap(x, axis, n, mask):
    return lax.ppermute(x, axis, [(i, i ^ mask) for i in range(n)])


def double(x, axis, n, dim=0):
    for bit in reversed(range(bits_of(n))):
        x = jnp.concatenate([x, swap(x, axis, n, 1 << bit)], axis=dim)
    return x


def ordered(x, *first):
    return lax.optimization_barrier((x, *first))[0]


def total_of(parts, start, stop):
    out = parts[0][start:stop]
    for part in parts[1:]:
        out = out + part[start:stop].astype(F32)
    return out


def params(mib=VMEM_MIB):
    return pltpu.CompilerParams(vmem_limit_bytes=mib * 1024 * 1024)


def cost(flops, size):
    return pl.CostEstimate(
        flops=int(flops * COST_SHARE), bytes_accessed=int(size * COST_SHARE), transcendentals=0
    )


def normalize(stream, stats, steering, gain, down, h, hid, beside=None):
    tokens, width = stream.shape
    block = tokens // hid
    ranks = down.shape[0]
    n_beside = 0 if beside is None else 1

    def token_block(p, h_ref):
        return h_ref[0] ^ reversed_bits(p, bits_of(hid))

    def kernel(h_ref, x_ref, stat_ref, steer_ref, gain_ref, down_ref, *refs):
        steered = x_ref[...].astype(F32) + stat_ref[:, :1] * steer_ref[...]
        normed = (steered * stat_ref[:, 1:] * gain_ref[...]).astype(BF16)
        out_ref, low_ref = refs[n_beside : n_beside + 2]
        out_ref[...] = normed
        low_ref[...] = lax.dot_general(
            normed, down_ref[...], (((1,), (1,)), ((), ())), preferred_element_type=F32
        )
        if n_beside:
            refs[-1][:block, :] = refs[0][...]
            refs[-1][block:, :] = normed

    whole = lambda n: pl.BlockSpec((n, width), lambda p, h_ref: (0, 0))
    rows = lambda n, m: pl.BlockSpec((n, m), lambda p, h_ref: (p, 0))
    return pl.pallas_call(
        kernel,
        grid_spec=pltpu.PrefetchScalarGridSpec(
            num_scalar_prefetch=1,
            grid=(hid,),
            in_specs=[
                pl.BlockSpec((block, width), lambda p, h_ref: (token_block(p, h_ref), 0)),
                pl.BlockSpec((block, 2), lambda p, h_ref: (token_block(p, h_ref), 0)),
                whole(1),
                whole(1),
                whole(ranks),
            ]
            + [rows(block, width)] * n_beside,
            out_specs=[rows(block, width), rows(block, ranks)] + [rows(2 * block, width)] * n_beside,
        ),
        out_shape=[
            jax.ShapeDtypeStruct((tokens, width), BF16),
            jax.ShapeDtypeStruct((tokens, ranks), F32),
        ]
        + [jax.ShapeDtypeStruct((2 * tokens, width), BF16)] * n_beside,
        compiler_params=params(),
        cost_estimate=cost(2 * tokens * width * ranks, 4 * tokens * width),
        name="normalize",
    )(
        h.reshape(1),
        stream,
        stats,
        steering.reshape(1, width),
        gain.reshape(1, width),
        down,
        *((beside,) if n_beside else ()),
    )


def forward_matmul(x, weights, first, tiles, start, stop, tile, into=(), after=()):
    rows, depth = x.shape
    half = rows // 2

    def kernel(x_ref, w_ref, *refs):
        keep_ref, send_ref, token_ref = refs[-3:]
        token_ref[...] = jnp.zeros_like(token_ref)
        y = jnp.dot(x_ref[...], w_ref[0], preferred_element_type=F32)
        keep_ref[...] = y[:half]
        send_ref[...] = y[half:].astype(BF16)

    return pl.pallas_call(
        kernel,
        grid=(stop - start,),
        in_specs=[RESIDENT, pl.BlockSpec((1, depth, tile), lambda i: (0, 0, first + start + i))]
        + [ANY] * (len(into) + len(after)),
        out_specs=[pl.BlockSpec((half, tile), lambda i: (0, start + i))] * 2
        + [pl.BlockSpec((8, 128), lambda i: (0, 0))],
        out_shape=[
            jax.ShapeDtypeStruct((half, tiles * tile), F32),
            jax.ShapeDtypeStruct((half, tiles * tile), BF16),
            jax.ShapeDtypeStruct((8, 128), F32),
        ],
        input_output_aliases={2 + i: i for i in range(len(into))},
        compiler_params=params(MATMUL_VMEM_MIB),
        cost_estimate=cost(2 * rows * depth * (stop - start) * tile, 2 * depth * (rows + (stop - start) * tile) + 6 * half * (stop - start) * tile),
        name="forward_matmul",
    )(x, weights, *into, *after)


def share_sums(parts, rows, count, after=(), places=None):
    columns = parts[0].shape[1]
    tile = tile_of(columns, 1792)

    def kernel(*refs):
        total = refs[0][...].astype(F32)
        for ref in refs[1 : len(parts)]:
            total = total + ref[...].astype(F32)
        for i in range(count):
            refs[i - count][...] = total[i * rows : (i + 1) * rows].astype(BF16)

    return pl.pallas_call(
        kernel,
        grid=(columns // tile,),
        in_specs=[
            pl.BlockSpec((count * rows, tile), lambda i, at=at: (at, i)) for at in places or [1] * len(parts)
        ]
        + [ANY] * len(after),
        out_specs=[pl.BlockSpec((rows, tile), lambda i: (0, i))] * count,
        out_shape=[jax.ShapeDtypeStruct((rows, columns), BF16)] * count,
        compiler_params=params(),
        cost_estimate=cost(count * rows * columns, 8 * count * rows * columns),
        name="share_sums",
    )(*parts, *after)


def gated_gradients(d, mine, other, cotangent, first, low, up, own, after=()):
    columns = other.shape[1]
    rank = up.shape[1]
    tile = max(t for t in range(128, 2049, 128) if columns % t == 0 and first % t == 0)
    tiles = columns // tile
    base = first // tile

    def kernel(d_ref, *refs):
        mine_refs = refs[: len(mine)]
        other_ref, flow_ref, low_ref, up_ref = refs[len(mine) : len(mine) + 4]
        mine_out, other_out, back_ref = refs[-3:]
        own_is_gate = d_ref[0] == 0
        total = mine_refs[0][...].astype(F32)
        for ref in mine_refs[1:]:
            total = total + ref[...].astype(F32)
        passed = other_ref[...].astype(F32)
        low_terms = [
            ADAPTER_SCALE
            * jnp.dot(low_ref[:, k * rank : (k + 1) * rank], up_ref[k], preferred_element_type=F32)
            for k in range(2)
        ]
        gate = jnp.where(own_is_gate, total, passed) + low_terms[0]
        upper = jnp.where(own_is_gate, passed, total) + low_terms[1]
        sigma = 1.0 / (1.0 + jnp.exp(-gate))
        flow = flow_ref[...].astype(F32)
        gate_grad = (flow * upper * sigma * (1.0 + gate * (1.0 - sigma))).astype(BF16)
        upper_grad = (flow * gate * sigma).astype(BF16)
        mine_out[...] = jnp.where(own_is_gate, gate_grad, upper_grad)
        other_out[...] = jnp.where(own_is_gate, upper_grad, gate_grad)

        @pl.when(pl.program_id(0) == 0)
        def _():
            back_ref[...] = jnp.zeros_like(back_ref)

        contract = (((1,), (1,)), ((), ()))
        for k, grad in enumerate((gate_grad, upper_grad)):
            back_ref[:, k * rank : (k + 1) * rank] += lax.dot_general(
                grad, up_ref[k], contract, preferred_element_type=F32
            )
        back_ref[:, 2 * rank :] += jnp.sum(
            gate_grad.astype(F32) * gate + upper_grad.astype(F32) * upper, axis=1, keepdims=True
        )

    here = pl.BlockSpec((own, tile), lambda i, d_ref: (0, i))
    there = pl.BlockSpec((own, tile), lambda i, d_ref: (0, base + i))
    return pl.pallas_call(
        kernel,
        grid_spec=pltpu.PrefetchScalarGridSpec(
            num_scalar_prefetch=1,
            grid=(tiles,),
            in_specs=[here] * (len(mine) + 1)
            + [
                there,
                pl.BlockSpec((own, 2 * rank), lambda i, d_ref: (0, 0)),
                pl.BlockSpec((2, rank, tile), lambda i, d_ref: (0, 0, base + i)),
            ]
            + [ANY] * len(after),
            out_specs=[here, here, pl.BlockSpec((own, 2 * rank + 1), lambda i, d_ref: (0, 0))],
        ),
        out_shape=[
            jax.ShapeDtypeStruct((own, columns), BF16),
            jax.ShapeDtypeStruct((own, columns), BF16),
            jax.ShapeDtypeStruct((own, 2 * rank + 1), F32),
        ],
        compiler_params=params(),
        cost_estimate=cost(8 * own * columns * rank, 16 * own * columns),
        name="gated_gradients",
    )(d.reshape(1), *mine, other, cotangent, low, up, *after)


def backward_matmul(pieces, weights, hidden_start, first, tiles, tile, base=None, base_first=0, partial=False, after=()):
    rows = sum(g.shape[0] for g in pieces)
    half = rows // 2
    n_base = 0 if base is None else 1
    hidden = pieces[0].shape[1]

    def kernel(*refs):
        w_ref = refs[len(pieces)]
        g = jnp.concatenate([ref[...] for ref in refs[: len(pieces)]], axis=0)
        y = lax.dot_general(g, w_ref[0], (((1,), (1,)), ((), ())), preferred_element_type=F32)
        if n_base:
            y = y + refs[len(pieces) + 1][...]
        if partial:
            refs[-1][...] = y
        else:
            refs[-2][...] = y[:half]
            refs[-1][...] = y[half:].astype(BF16)

    if partial:
        out_specs = pl.BlockSpec((rows, tile), lambda i: (0, i))
        out_shape = jax.ShapeDtypeStruct((rows, tiles * tile), F32)
    else:
        out_specs = [pl.BlockSpec((half, tile), lambda i: (0, i))] * 2
        out_shape = [
            jax.ShapeDtypeStruct((half, tiles * tile), F32),
            jax.ShapeDtypeStruct((half, tiles * tile), BF16),
        ]
    return pl.pallas_call(
        kernel,
        grid=(tiles,),
        in_specs=[
            pl.BlockSpec(g.shape, lambda i: (0, 0), pipeline_mode=pl.Buffered(1)) for g in pieces
        ]
        + [
            pl.BlockSpec(
                (pl.Element(1), pl.Element(tile), pl.Element(hidden)),
                lambda i: (0, (first + i) * tile, hidden_start),
            )
        ]
        + [pl.BlockSpec((rows, tile), lambda i: (0, first - base_first + i))] * n_base
        + [ANY] * len(after),
        out_specs=out_specs,
        out_shape=out_shape,
        compiler_params=params(MATMUL_VMEM_MIB),
        cost_estimate=cost(2 * rows * hidden * tiles * tile, 2 * hidden * (rows + tiles * tile) + (4 + 4 * n_base) * rows * tiles * tile),
        name="backward_matmul",
    )(*pieces, weights, *(() if base is None else (base,)), *after)


def adapter_products(low, groups, after=()):
    rank = low.shape[0]

    def kernel(*refs):
        at = 1
        for i, pieces in enumerate(groups):
            g = jnp.concatenate([ref[...] for ref in refs[at : at + len(pieces)]], axis=0)
            at += len(pieces)
            refs[i - len(groups)][...] = ADAPTER_SCALE * jnp.dot(
                refs[0][...], g, preferred_element_type=F32
            )

    operands = [g for pieces in groups for g in pieces]
    widths = [pieces[0].shape[1] for pieces in groups]
    return pl.pallas_call(
        kernel,
        grid=(1,),
        in_specs=[pl.BlockSpec(x.shape, lambda i: (0, 0)) for x in [low] + operands] + [ANY] * len(after),
        out_specs=[pl.BlockSpec((rank, w), lambda i: (0, 0)) for w in widths],
        out_shape=[jax.ShapeDtypeStruct((rank, w), F32) for w in widths],
        compiler_params=params(),
        cost_estimate=cost(2 * rank * low.shape[1] * sum(widths), 2 * low.shape[1] * sum(widths)),
        name="adapter_products",
    )(low, *operands, *after)


def assemble(pieces, places, block, rows, tokens, width, columns, into=None):
    chunk = pieces[0].shape[1]

    def kernel(place_ref, *refs):
        out_ref = refs[-1]
        i = 0
        for ref in refs[: len(pieces)]:
            for r in range(0, rows, block):
                out_ref[pl.ds(pl.multiple_of(place_ref[i], block), block), :] = ref[r : r + block, :]
                i += 1

    n_into = 0 if into is None else 1
    return pl.pallas_call(
        kernel,
        grid_spec=pltpu.PrefetchScalarGridSpec(
            num_scalar_prefetch=1,
            grid=(1,),
            in_specs=[pl.BlockSpec(x.shape, lambda i, p: (0, 0)) for x in pieces] + [ANY] * n_into,
            out_specs=pl.BlockSpec((pl.Element(tokens), pl.Element(chunk)), lambda i, p: (0, columns)),
        ),
        out_shape=jax.ShapeDtypeStruct((tokens, width), BF16),
        input_output_aliases={len(pieces) + 1: 0} if n_into else {},
        compiler_params=params(),
        cost_estimate=cost(0, 4 * tokens * chunk),
        name="assemble",
    )(places, *pieces, *((into,) if n_into else ()))


def finish(parts, stream, stats, back, down, steering, gain, columns, after=()):
    rows = stream.shape[0]
    width = parts[0].shape[1]

    def kernel(*refs):
        part_refs = refs[: len(parts)]
        x_ref, s_ref, back_ref, down_ref, steer_ref, gain_ref = refs[len(parts) : len(parts) + 6]
        out_ref, sum_ref = refs[-2:]
        total = part_refs[0][...].astype(F32)
        for ref in part_refs[1:]:
            total = total + ref[...].astype(F32)
        total = total + ADAPTER_SCALE * jnp.dot(back_ref[...], down_ref[...], preferred_element_type=F32)
        steered = x_ref[...].astype(F32) + s_ref[:, 0:1] * steer_ref[...]
        grad = s_ref[:, 1:2] * gain_ref[...] * total - s_ref[:, 2:3] * steered
        out_ref[...] = grad.astype(BF16)
        sum_ref[...] = jnp.sum(s_ref[:, 0:1] * grad, axis=0, keepdims=True)

    across = lambda n: pl.BlockSpec((pl.Element(n), pl.Element(width)), lambda i: (0, columns))
    return pl.pallas_call(
        kernel,
        grid=(1,),
        in_specs=[pl.BlockSpec((rows, width), lambda i: (0, 0))] * len(parts)
        + [
            across(rows),
            pl.BlockSpec(stats.shape, lambda i: (0, 0)),
            pl.BlockSpec(back.shape, lambda i: (0, 0)),
            across(down.shape[0]),
            across(1),
            across(1),
        ]
        + [ANY] * len(after),
        out_specs=[pl.BlockSpec((rows, width), lambda i: (0, 0)), pl.BlockSpec((1, width), lambda i: (0, 0))],
        out_shape=[jax.ShapeDtypeStruct((rows, width), BF16), jax.ShapeDtypeStruct((1, width), F32)],
        compiler_params=params(),
        cost_estimate=cost(2 * rows * width * down.shape[0], 10 * rows * width),
        name="finish",
    )(*parts, stream, stats, back, down, steering.reshape(1, -1), gain.reshape(1, -1), *after)


def make_local(dp, hid, ffn):
    def local(stream, steering, strength, gain, weights, down, up, cotangent):
        d, h, f = lax.axis_index("dp"), lax.axis_index("hid"), lax.axis_index("ffn")
        tokens, width = stream.shape
        hidden = weights.shape[2]
        own = tokens // hid
        rank = down.shape[2]
        first_pair = d == 0
        down_rows = jnp.transpose(down, (0, 2, 1)).reshape(2 * rank, width)

        peer_stream = swap(stream, "dp", dp, 1)
        rows = stream.astype(F32)
        total_rows, total_steer = lax.psum(
            (jnp.sum(rows * rows, axis=1), jnp.sum(steering * steering)), "hid"
        )
        stream_ms = total_rows / MODEL_WIDTH + 1e-06
        steer_ms = total_steer / MODEL_WIDTH + 1e-06
        scale = strength * jnp.sqrt(stream_ms / steer_ms)
        steered = rows + scale[:, None] * steering[None, :]
        steered_power = lax.psum(jnp.sum(steered * steered, axis=1), "hid")
        inv_rms = lax.rsqrt(steered_power / MODEL_WIDTH + 1e-05)
        stats = jnp.stack([scale, inv_rms], axis=1)
        peer_stats = swap(stats, "dp", dp, 1)

        tile = tile_of(hidden, 512)
        count = hidden // tile
        chunks = [(0, (count + 1) // 2), ((count + 1) // 2, count // 2)]
        last_bit = 1 << (bits_of(hid) - 1)
        own_normed, own_low = normalize(stream, stats, steering, gain, down_rows, h, hid)
        def forward(x, c, edges, afters):
            first, n = chunks[c]
            out, token = (), None
            for start, stop, after in zip(edges, edges[1:], afters):
                *out, token = forward_matmul(
                    x, weights, first, n, start, stop, tile, into=tuple(out), after=after(token)
                )
            keep, send = out
            parts = [keep, swap(send, "hid", hid, 1)]
            for bit in range(1, bits_of(hid) - 1):
                size = parts[-1].shape[0]
                send = total_of(parts, size // 2, size).astype(BF16)
                parts.append(swap(send, "hid", hid, 1 << bit))
            return parts

        own_parts = forward(own_normed, 0, (0, chunks[0][1]), (lambda t: (),))
        (own_send,) = share_sums(own_parts, own, 1)
        own_got = swap(own_send, "hid", hid, last_bit)
        peer_normed, peer_low, normed = normalize(
            peer_stream, ordered(peer_stats, own_send), steering, gain, down_rows, h, hid, own_normed
        )

        low, low_steps = jnp.stack([own_low, peer_low]), []
        for bit in range(bits_of(hid)):
            half = low.shape[1] // 2
            low = low[:, :half] + swap(low[:, half:], "hid", hid, 1 << bit)
            low_steps.append(low)
        low = low.astype(BF16)
        low_own = low[0]

        width_tile = tile_of(width, 512)
        tiles = width // width_tile
        steps = [(0, 3), (3, 3), (6, 2)] if tiles == 8 else split_tiles(tiles, 3)
        acts, others, grads = [], [], []

        def gradients(c, after):
            mine_grad, other_grad, back_part = gated_gradients(
                d, acts[c], others[c], cotangent, chunks[c][0] * tile, low_own, up, own, after
            )
            return back_part, mine_grad, swap(other_grad, "dp", dp, 1)

        def spread(g):
            blocks = [g]
            for bit in reversed(range(bits_of(hid))):
                blocks += [swap(x, "hid", hid, 1 << bit) for x in blocks]
            return blocks

        n = chunks[0][1]
        peer_parts = forward(
            peer_normed, 0, (0, (n + 1) // 2, n), (lambda t: (own_send,), lambda t: (low_steps[0], own_got))
        )
        (peer_send,) = share_sums(peer_parts, own, 1, (low_own,))
        peer_got = swap(peer_send, "hid", hid, last_bit)
        acts.append(own_parts + [own_got])

        def pass_on(token):
            terms = peer_parts + [peer_got]
            (passed,) = share_sums(terms, own, 1, (token,), [0] * len(terms))
            others.append(swap(passed, "dp", dp, 1))
            return peer_got, passed

        n = chunks[1][1]
        first_send = peer_send
        first_half_done = []

        def first_gradients(token):
            more, mine_grad, peer_grad = gradients(0, (token,))
            own_pieces, peer_pieces = spread(mine_grad), spread(peer_grad)
            grads.append(own_pieces + peer_pieces)
            first_half_done.append(more)
            return peer_grad, own_pieces[1]

        parts = forward(
            normed, 1, (0, n // 3, n - 1, n), (lambda t: (first_send,), pass_on, first_gradients)
        )
        own_send, peer_send = share_sums(parts, own, 2)
        peer_got = swap(peer_send, "hid", hid, last_bit)
        own_got = swap(own_send, "hid", hid, last_bit)
        bases = []

        def first_half(j, after):
            first, n = steps[j]
            bases.append(
                backward_matmul(
                    grads[0], weights, 0, first, n, width_tile, partial=True, after=after
                )
            )

        first_half(0, (own_send,))
        (passed,) = share_sums(parts + [peer_got], own, 1, (bases[0],), [1] * len(parts) + [0])
        acts.append(parts + [own_got])
        others.append(swap(passed, "dp", dp, 1))
        more, mine_grad, peer_grad = gradients(1, ())
        back = first_half_done[0] + more
        for bit in range(bits_of(ffn)):
            back = back + swap(back, "ffn", ffn, 1 << bit)
        back = jnp.stack([back, swap(back, "dp", dp, 1)])
        for j in range(1, len(steps)):
            first_half(j, (mine_grad,) if j == 1 else (peer_grad, back))
            if j == 1:
                (peer_grad,) = share_sums([peer_grad], own, 1, (bases[1],), [0])
        own_pieces = spread(mine_grad)
        grads.append(own_pieces + spread(peer_grad))

        back = double(back, "hid", hid, dim=1)
        low_mine = jnp.where(first_pair, low[:, :, :rank], low[:, :, rank:])
        low_mine = double(low_mine, "hid", hid, dim=1).reshape(2 * tokens, rank).T
        shard = tokens // ffn
        place = reversed_bits(f, bits_of(ffn))
        products, received = [], []

        def halving_step(parts, bit):
            half = parts[-1].shape[0] // 2
            mine = (f >> bit) & 1
            sides = [
                [lax.dynamic_slice_in_dim(p, side * half, half, axis=0) for p in parts]
                for side in (mine, 1 - mine)
            ]
            return total_of(sides[0], 0, half), total_of(sides[1], 0, half).astype(BF16)

        first_steps = []
        for j, ((first, n), base) in enumerate(zip(steps, bases)):
            wait = (products[-1],) if products else tuple(bases)
            if j == 2:
                first_steps.append(halving_step([products[0], received[0]], 0))
                wait += (first_steps[0][1], back, low_mine)
            keep, send = backward_matmul(
                grads[1], weights, chunks[1][0] * tile, first, n, width_tile, base=base, base_first=first,
                after=wait,
            )
            products.append(keep)
            received.append(swap(send, "dp", dp, 1))
        back_low = back[:, :, : 2 * rank].astype(BF16)
        acts_product = back[0, :, 2 * rank]

        block = min(own, shard)

        def natural(row):
            index = row // own
            return (h ^ reversed_bits(index, bits_of(hid))) * own + row % own

        def shard_rows(x):
            return jnp.concatenate(
                [
                    lax.dynamic_slice_in_dim(x, natural(place * shard + i * block), block, axis=0)
                    for i in range(shard // block)
                ],
                axis=0,
            )

        stats_shard = shard_rows(stats)
        dot_shard = lax.dynamic_slice_in_dim(acts_product, place * shard, shard, axis=0)
        dot_factor = stats_shard[:, 1] ** 2 * dot_shard / MODEL_WIDTH
        stats_shard = jnp.concatenate([stats_shard, dot_factor[:, None]], axis=1)
        stream_shard = shard_rows(stream)
        back_shard = lax.dynamic_slice_in_dim(back_low[0], place * shard, shard, axis=0)

        out, sums, gathered = None, [], []
        owners = [reversed_bits(f ^ reversed_bits(p, bits_of(ffn)), bits_of(ffn)) for p in range(ffn)]
        places = jnp.stack([natural(o * shard + i * block) for o in owners for i in range(shard // block)])
        for j, (first, n) in enumerate(steps):
            got = received[j]
            if j == 1:
                got = ordered(got, products[-1])
            elif j >= 2:
                got = ordered(got, gathered[j - 2][1])
            parts = [products[j], got]
            for bit in range(bits_of(ffn)):
                if bit == 0 and j < len(first_steps):
                    keep, send = first_steps[j]
                else:
                    keep, send = halving_step(parts, bit)
                if j == 2 and bit == 1:
                    send = ordered(send, gathered[0][-1])
                parts = [keep, swap(send, "ffn", ffn, 1 << bit)]
            result, sum_part = finish(
                parts, stream_shard, stats_shard, back_shard, down_rows, steering, gain, first * width_tile,
                after=tuple(gathered[j - 1][1:2] if j else ()) + tuple(gathered[j - 2][2:] if j >= 2 else ()),
            )
            sums.append(sum_part)
            if j == len(steps) - 1:
                sums = jnp.concatenate(sums, axis=1).reshape(-1, result.shape[1])
                high = sums.astype(BF16)
                low_term = (sums - high.astype(F32)).astype(BF16)
                rows = 2 * sums.shape[0]
                empty = jnp.zeros((-rows % 16, result.shape[1]), BF16)
                result = jnp.concatenate([result, high, low_term, empty], axis=0)
            blocks = [result]
            for bit in reversed(range(bits_of(ffn))):
                blocks += [swap(x, "ffn", ffn, 1 << bit) for x in blocks]
            gathered.append(blocks)
            out = assemble(blocks, places, block, shard, tokens, width, first * width_tile, into=out)

        half = rows // 2
        terms = [
            x[shard : shard + half].astype(F32) + x[shard + half : shard + rows].astype(F32) for x in blocks
        ]
        while len(terms) > 1:
            terms = [a + b for a, b in zip(terms[: len(terms) // 2], terms[len(terms) // 2 :])]
        steering_gradient = terms[0] + swap(terms[0], "dp", dp, 1)

        up_mine = jnp.concatenate(adapter_products(low_mine, grads, products[-1:]), axis=1)
        up_other = swap(ordered(up_mine.astype(BF16), received[-1]), "dp", dp, 1).astype(F32)
        up_gradient = jnp.where(
            first_pair, jnp.stack([up_mine, up_other]), jnp.stack([up_other, up_mine])
        )
        back_rows = back_low.reshape(2, hid, own, 2 * rank).transpose(1, 0, 2, 3).reshape(2 * tokens, 2 * rank)
        (down_gradient,) = adapter_products(back_rows.T, [[normed]])
        down_gradient = jnp.transpose(
            down_gradient.reshape(2, rank, width), (0, 2, 1)
        )
        return out, steering_gradient.reshape(width), down_gradient, up_gradient

    return local


def solution(mesh):
    in_specs = (
        P("dp", "hid"),
        P("hid"),
        P("dp"),
        P("hid"),
        P("dp", "hid", "ffn"),
        P(None, "hid", None),
        P(None, None, "ffn"),
        P(("dp", "hid"), "ffn"),
    )
    out_specs = (P("dp", "hid"), P("hid"), P(None, "hid", None), P(None, None, "ffn"))
    local = make_local(mesh.shape["dp"], mesh.shape["hid"], mesh.shape["ffn"])
    return jax.shard_map(local, mesh=mesh, in_specs=in_specs, out_specs=out_specs, check_vma=False)
```

```python
import jax
import jax.numpy as jnp
from jax import lax
from jax.experimental import pallas as pl
from jax.experimental.pallas import tpu as pltpu
from jax.sharding import PartitionSpec as P

MODEL_WIDTH = 16384
ADAPTER_SCALE = 0.5
VMEM_MIB = 40
COST_SHARE = 0.01

F32 = jnp.float32
BF16 = jnp.bfloat16
ANY = pl.BlockSpec(memory_space=pl.ANY)
RESIDENT = pl.BlockSpec(memory_space=pltpu.VMEM)


def bits_of(n):
    return n.bit_length() - 1


def reversed_bits(x, n):
    out = 0
    for i in range(n):
        out = out + (((x >> i) & 1) << (n - 1 - i))
    return out


def tile_of(n, cap):
    return max(t for t in range(128, cap + 1, 128) if n % t == 0)


def split_tiles(count, parts):
    edges = [count * i // parts for i in range(parts + 1)]
    return [(a, b - a) for a, b in zip(edges, edges[1:]) if b > a]


def swap(x, axis, n, mask):
    return lax.ppermute(x, axis, [(i, i ^ mask) for i in range(n)])


def double(x, axis, n, dim=0):
    for bit in reversed(range(bits_of(n))):
        x = jnp.concatenate([x, swap(x, axis, n, 1 << bit)], axis=dim)
    return x


def total_of(parts, start, stop):
    out = parts[0][start:stop]
    for part in parts[1:]:
        out = out + part[start:stop].astype(F32)
    return out


def params():
    return pltpu.CompilerParams(vmem_limit_bytes=VMEM_MIB * 1024 * 1024)


def cost(flops, size):
    return pl.CostEstimate(
        flops=int(flops * COST_SHARE), bytes_accessed=int(size * COST_SHARE), transcendentals=0
    )


def normalize(stream, stats, steering, gain, down, h, hid, after=()):
    tokens, width = stream.shape
    block = tokens // hid
    ranks = down.shape[0]

    def token_block(p, h_ref):
        return h_ref[0] ^ reversed_bits(p, bits_of(hid))

    def kernel(h_ref, x_ref, stat_ref, steer_ref, gain_ref, down_ref, *refs):
        steered = x_ref[...].astype(F32) + stat_ref[:, :1] * steer_ref[...]
        normed = (steered * stat_ref[:, 1:] * gain_ref[...]).astype(BF16)
        refs[-2][...] = normed
        refs[-1][...] = lax.dot_general(
            normed, down_ref[...], (((1,), (1,)), ((), ())), preferred_element_type=F32
        )

    whole = lambda n: pl.BlockSpec((n, width), lambda p, h_ref: (0, 0))
    rows = lambda n, m: pl.BlockSpec((n, m), lambda p, h_ref: (p, 0))
    return pl.pallas_call(
        kernel,
        grid_spec=pltpu.PrefetchScalarGridSpec(
            num_scalar_prefetch=1,
            grid=(hid,),
            in_specs=[
                pl.BlockSpec((block, width), lambda p, h_ref: (token_block(p, h_ref), 0)),
                pl.BlockSpec((block, 2), lambda p, h_ref: (token_block(p, h_ref), 0)),
                whole(1),
                whole(1),
                whole(ranks),
            ]
            + [ANY] * len(after),
            out_specs=[rows(block, width), rows(block, ranks)],
        ),
        out_shape=[
            jax.ShapeDtypeStruct((tokens, width), BF16),
            jax.ShapeDtypeStruct((tokens, ranks), F32),
        ],
        compiler_params=params(),
        cost_estimate=cost(2 * tokens * width * ranks, 4 * tokens * width),
        name="normalize",
    )(
        h.reshape(1),
        stream,
        stats,
        steering.reshape(1, width),
        gain.reshape(1, width),
        down,
        *after,
    )


def relay(x, after):
    def kernel(x_ref, *refs):
        refs[-1][...] = x_ref[...]

    whole = pl.BlockSpec(x.shape, lambda i: (0,) * x.ndim)
    return pl.pallas_call(
        kernel,
        grid=(1,),
        in_specs=[whole] + [ANY] * len(after),
        out_specs=whole,
        out_shape=jax.ShapeDtypeStruct(x.shape, x.dtype),
        compiler_params=params(),
        cost_estimate=cost(0, 4 * x.size),
        name="relay",
    )(x, *after)


def forward_matmul(x, weights, first, tiles, start, stop, tile, into=(), after=()):
    rows, depth = x.shape
    half = rows // 2

    def kernel(x_ref, w_ref, *refs):
        keep_ref, send_ref, token_ref = refs[-3:]
        token_ref[...] = jnp.zeros_like(token_ref)
        y = jnp.dot(x_ref[...], w_ref[0], preferred_element_type=F32)
        keep_ref[...] = y[:half]
        send_ref[...] = y[half:].astype(BF16)

    return pl.pallas_call(
        kernel,
        grid=(stop - start,),
        in_specs=[RESIDENT, pl.BlockSpec((1, depth, tile), lambda i: (0, 0, first + start + i))]
        + [ANY] * (len(into) + len(after)),
        out_specs=[pl.BlockSpec((half, tile), lambda i: (0, start + i))] * 2
        + [pl.BlockSpec((8, 128), lambda i: (0, 0))],
        out_shape=[
            jax.ShapeDtypeStruct((half, tiles * tile), F32),
            jax.ShapeDtypeStruct((half, tiles * tile), BF16),
            jax.ShapeDtypeStruct((8, 128), F32),
        ],
        input_output_aliases={2 + i: i for i in range(len(into))},
        compiler_params=params(),
        cost_estimate=cost(2 * rows * depth * (stop - start) * tile, 2 * depth * (rows + (stop - start) * tile) + 6 * half * (stop - start) * tile),
        name="forward_matmul",
    )(x, weights, *into, *after)


def share_sums(parts, rows, count, after=(), places=None):
    columns = parts[0].shape[1]
    tile = tile_of(columns, 1792)

    def kernel(*refs):
        total = refs[0][...].astype(F32)
        for ref in refs[1 : len(parts)]:
            total = total + ref[...].astype(F32)
        for i in range(count):
            refs[i - count][...] = total[i * rows : (i + 1) * rows].astype(BF16)

    return pl.pallas_call(
        kernel,
        grid=(columns // tile,),
        in_specs=[
            pl.BlockSpec((count * rows, tile), lambda i, at=at: (at, i)) for at in places or [1] * len(parts)
        ]
        + [ANY] * len(after),
        out_specs=[pl.BlockSpec((rows, tile), lambda i: (0, i))] * count,
        out_shape=[jax.ShapeDtypeStruct((rows, columns), BF16)] * count,
        compiler_params=params(),
        cost_estimate=cost(count * rows * columns, 8 * count * rows * columns),
        name="share_sums",
    )(*parts, *after)


def gated_gradients(d, mine, other, cotangent, first, low, up, own, after=()):
    columns = other.shape[1]
    rank = up.shape[1]
    tile = max(t for t in range(128, 2049, 128) if columns % t == 0 and first % t == 0)
    tiles = columns // tile
    base = first // tile

    def kernel(d_ref, *refs):
        mine_refs = refs[: len(mine)]
        other_ref, flow_ref, low_ref, up_ref = refs[len(mine) : len(mine) + 4]
        mine_out, other_out, back_ref = refs[-3:]
        own_is_gate = d_ref[0] == 0
        total = mine_refs[0][...].astype(F32)
        for ref in mine_refs[1:]:
            total = total + ref[...].astype(F32)
        passed = other_ref[...].astype(F32)
        low_terms = [
            ADAPTER_SCALE
            * jnp.dot(low_ref[:, k * rank : (k + 1) * rank], up_ref[k], preferred_element_type=F32)
            for k in range(2)
        ]
        gate = jnp.where(own_is_gate, total, passed) + low_terms[0]
        upper = jnp.where(own_is_gate, passed, total) + low_terms[1]
        sigma = 1.0 / (1.0 + jnp.exp(-gate))
        flow = flow_ref[...].astype(F32)
        gate_grad = (flow * upper * sigma * (1.0 + gate * (1.0 - sigma))).astype(BF16)
        upper_grad = (flow * gate * sigma).astype(BF16)
        mine_out[...] = jnp.where(own_is_gate, gate_grad, upper_grad)
        other_out[...] = jnp.where(own_is_gate, upper_grad, gate_grad)

        @pl.when(pl.program_id(0) == 0)
        def _():
            back_ref[...] = jnp.zeros_like(back_ref)

        contract = (((1,), (1,)), ((), ()))
        for k, grad in enumerate((gate_grad, upper_grad)):
            back_ref[:, k * rank : (k + 1) * rank] += lax.dot_general(
                grad, up_ref[k], contract, preferred_element_type=F32
            )
        back_ref[:, 2 * rank :] += jnp.sum(
            gate_grad.astype(F32) * gate + upper_grad.astype(F32) * upper, axis=1, keepdims=True
        )

    here = pl.BlockSpec((own, tile), lambda i, d_ref: (0, i))
    there = pl.BlockSpec((own, tile), lambda i, d_ref: (0, base + i))
    return pl.pallas_call(
        kernel,
        grid_spec=pltpu.PrefetchScalarGridSpec(
            num_scalar_prefetch=1,
            grid=(tiles,),
            in_specs=[here] * (len(mine) + 1)
            + [
                there,
                pl.BlockSpec((own, 2 * rank), lambda i, d_ref: (0, 0)),
                pl.BlockSpec((2, rank, tile), lambda i, d_ref: (0, 0, base + i)),
            ]
            + [ANY] * len(after),
            out_specs=[here, here, pl.BlockSpec((own, 2 * rank + 1), lambda i, d_ref: (0, 0))],
        ),
        out_shape=[
            jax.ShapeDtypeStruct((own, columns), BF16),
            jax.ShapeDtypeStruct((own, columns), BF16),
            jax.ShapeDtypeStruct((own, 2 * rank + 1), F32),
        ],
        compiler_params=params(),
        cost_estimate=cost(8 * own * columns * rank, 16 * own * columns),
        name="gated_gradients",
    )(d.reshape(1), *mine, other, cotangent, low, up, *after)


def backward_matmul(pieces, weights, hidden_start, first, tiles, tile, base=None, base_first=0, partial=False, after=()):
    rows = sum(g.shape[0] for g in pieces)
    half = rows // 2
    n_base = 0 if base is None else 1
    hidden = pieces[0].shape[1]

    def kernel(*refs):
        w_ref = refs[len(pieces)]
        g = jnp.concatenate([ref[...] for ref in refs[: len(pieces)]], axis=0)
        y = lax.dot_general(g, w_ref[0], (((1,), (1,)), ((), ())), preferred_element_type=F32)
        if n_base:
            y = y + refs[len(pieces) + 1][...]
        if partial:
            refs[-1][...] = y
        else:
            refs[-2][...] = y[:half]
            refs[-1][...] = y[half:].astype(BF16)

    if partial:
        out_specs = pl.BlockSpec((rows, tile), lambda i: (0, i))
        out_shape = jax.ShapeDtypeStruct((rows, tiles * tile), F32)
    else:
        out_specs = [pl.BlockSpec((half, tile), lambda i: (0, i))] * 2
        out_shape = [
            jax.ShapeDtypeStruct((half, tiles * tile), F32),
            jax.ShapeDtypeStruct((half, tiles * tile), BF16),
        ]
    return pl.pallas_call(
        kernel,
        grid=(tiles,),
        in_specs=[
            pl.BlockSpec(g.shape, lambda i: (0, 0), pipeline_mode=pl.Buffered(1)) for g in pieces
        ]
        + [
            pl.BlockSpec(
                (pl.Element(1), pl.Element(tile), pl.Element(hidden)),
                lambda i: (0, (first + i) * tile, hidden_start),
            )
        ]
        + [pl.BlockSpec((rows, tile), lambda i: (0, first - base_first + i))] * n_base
        + [ANY] * len(after),
        out_specs=out_specs,
        out_shape=out_shape,
        compiler_params=params(),
        cost_estimate=cost(2 * rows * hidden * tiles * tile, 2 * hidden * (rows + tiles * tile) + (4 + 4 * n_base) * rows * tiles * tile),
        name="backward_matmul",
    )(*pieces, weights, *(() if base is None else (base,)), *after)


def adapter_products(low, groups, after=()):
    rank = low.shape[0]

    def kernel(*refs):
        at = 1
        for i, pieces in enumerate(groups):
            g = jnp.concatenate([ref[...] for ref in refs[at : at + len(pieces)]], axis=0)
            at += len(pieces)
            refs[i - len(groups)][...] = ADAPTER_SCALE * jnp.dot(
                refs[0][...], g, preferred_element_type=F32
            )

    operands = [g for pieces in groups for g in pieces]
    widths = [pieces[0].shape[1] for pieces in groups]
    return pl.pallas_call(
        kernel,
        grid=(1,),
        in_specs=[pl.BlockSpec(x.shape, lambda i: (0, 0)) for x in [low] + operands] + [ANY] * len(after),
        out_specs=[pl.BlockSpec((rank, w), lambda i: (0, 0)) for w in widths],
        out_shape=[jax.ShapeDtypeStruct((rank, w), F32) for w in widths],
        compiler_params=params(),
        cost_estimate=cost(2 * rank * low.shape[1] * sum(widths), 2 * low.shape[1] * sum(widths)),
        name="adapter_products",
    )(low, *operands, *after)


def assemble(pieces, places, block, rows, tokens, width, columns, into=None):
    chunk = pieces[0].shape[1]

    def kernel(place_ref, *refs):
        out_ref = refs[-1]
        i = 0
        for ref in refs[: len(pieces)]:
            for r in range(0, rows, block):
                out_ref[pl.ds(pl.multiple_of(place_ref[i], block), block), :] = ref[r : r + block, :]
                i += 1

    n_into = 0 if into is None else 1
    return pl.pallas_call(
        kernel,
        grid_spec=pltpu.PrefetchScalarGridSpec(
            num_scalar_prefetch=1,
            grid=(1,),
            in_specs=[pl.BlockSpec(x.shape, lambda i, p: (0, 0)) for x in pieces] + [ANY] * n_into,
            out_specs=pl.BlockSpec((pl.Element(tokens), pl.Element(chunk)), lambda i, p: (0, columns)),
        ),
        out_shape=jax.ShapeDtypeStruct((tokens, width), BF16),
        input_output_aliases={len(pieces) + 1: 0} if n_into else {},
        compiler_params=params(),
        cost_estimate=cost(0, 4 * tokens * chunk),
        name="assemble",
    )(places, *pieces, *((into,) if n_into else ()))


def finish(parts, stream, stats, back, down, steering, gain, columns, after=()):
    rows = stream.shape[0]
    width = parts[0].shape[1]

    def kernel(*refs):
        part_refs = refs[: len(parts)]
        x_ref, s_ref, back_ref, down_ref, steer_ref, gain_ref = refs[len(parts) : len(parts) + 6]
        out_ref, sum_ref = refs[-2:]
        total = part_refs[0][...].astype(F32)
        for ref in part_refs[1:]:
            total = total + ref[...].astype(F32)
        total = total + ADAPTER_SCALE * jnp.dot(back_ref[...], down_ref[...], preferred_element_type=F32)
        steered = x_ref[...].astype(F32) + s_ref[:, 0:1] * steer_ref[...]
        grad = s_ref[:, 1:2] * gain_ref[...] * total - s_ref[:, 2:3] * steered
        out_ref[...] = grad.astype(BF16)
        sum_ref[...] = jnp.sum(s_ref[:, 0:1] * grad, axis=0, keepdims=True)

    across = lambda n: pl.BlockSpec((pl.Element(n), pl.Element(width)), lambda i: (0, columns))
    return pl.pallas_call(
        kernel,
        grid=(1,),
        in_specs=[pl.BlockSpec((rows, width), lambda i: (0, 0))] * len(parts)
        + [
            across(rows),
            pl.BlockSpec(stats.shape, lambda i: (0, 0)),
            pl.BlockSpec(back.shape, lambda i: (0, 0)),
            across(down.shape[0]),
            across(1),
            across(1),
        ]
        + [ANY] * len(after),
        out_specs=[pl.BlockSpec((rows, width), lambda i: (0, 0)), pl.BlockSpec((1, width), lambda i: (0, 0))],
        out_shape=[jax.ShapeDtypeStruct((rows, width), BF16), jax.ShapeDtypeStruct((1, width), F32)],
        compiler_params=params(),
        cost_estimate=cost(2 * rows * width * down.shape[0], 10 * rows * width),
        name="finish",
    )(*parts, stream, stats, back, down, steering.reshape(1, -1), gain.reshape(1, -1), *after)


def make_local(dp, hid, ffn):
    def local(stream, steering, strength, gain, weights, down, up, cotangent):
        d, h, f = lax.axis_index("dp"), lax.axis_index("hid"), lax.axis_index("ffn")
        tokens, width = stream.shape
        hidden = weights.shape[2]
        own = tokens // hid
        rank = down.shape[2]
        first_pair = d == 0
        down_rows = jnp.transpose(down, (0, 2, 1)).reshape(2 * rank, width)

        peer_stream = swap(stream, "dp", dp, 1)
        rows = stream.astype(F32)
        total_rows, total_steer = lax.psum(
            (jnp.sum(rows * rows, axis=1), jnp.sum(steering * steering)), "hid"
        )
        stream_ms = total_rows / MODEL_WIDTH + 1e-06
        steer_ms = total_steer / MODEL_WIDTH + 1e-06
        scale = strength * jnp.sqrt(stream_ms / steer_ms)
        steered = rows + scale[:, None] * steering[None, :]
        steered_power = lax.psum(jnp.sum(steered * steered, axis=1), "hid")
        inv_rms = lax.rsqrt(steered_power / MODEL_WIDTH + 1e-05)
        stats = jnp.stack([scale, inv_rms], axis=1)
        peer_stats = swap(stats, "dp", dp, 1)

        tile = tile_of(hidden, 512)
        count = hidden // tile
        chunks = [(0, (count + 1) // 2), ((count + 1) // 2, count // 2)]
        last_bit = 1 << (bits_of(hid) - 1)
        own_normed, own_low = normalize(stream, stats, steering, gain, down_rows, h, hid)

        def forward(x, c, edges, afters):
            first, n = chunks[c]
            out, token = (), None
            for start, stop, after in zip(edges, edges[1:], afters):
                *out, token = forward_matmul(
                    x, weights, first, n, start, stop, tile, into=tuple(out), after=after(token)
                )
            keep, send = out
            parts = [keep, swap(send, "hid", hid, 1)]
            for bit in range(1, bits_of(hid) - 1):
                size = parts[-1].shape[0]
                send = total_of(parts, size // 2, size).astype(BF16)
                parts.append(swap(send, "hid", hid, 1 << bit))
            return parts, token

        width_tile = tile_of(width, 512)
        tiles = width // width_tile
        steps = [(0, 2), (2, 3), (5, 3)] if tiles == 8 else split_tiles(tiles, 3)

        own_parts, own_sends, own_gots = [], [], []
        for c in range(2):
            wait = tuple(own_sends)
            parts, token = forward(own_normed, c, (0, chunks[c][1]), (lambda t: wait,))
            own_parts.append(parts)
            (send,) = share_sums(own_parts[c], own, 1)
            own_sends.append(send)
            own_gots.append(swap(send, "hid", hid, last_bit))

        peer_normed, _ = normalize(
            peer_stream, peer_stats, steering, gain, down_rows, h, hid, (own_sends[0], token)
        )

        low, low_steps = relay(own_low, (peer_normed,)), []
        for bit in range(bits_of(hid)):
            half = low.shape[0] // 2
            low = low[:half] + swap(low[half:], "hid", hid, 1 << bit)
            low_steps.append(low)
        low_own = low.astype(BF16)

        passed, others = [], []

        def pass_on(c, after):
            terms = peer_parts[c] + [peer_gots[c]]
            (sums,) = share_sums(terms, own, 1, after, [0] * len(terms))
            passed.append(sums)
            others.append(swap(sums, "dp", dp, 1))

        def after_first_part(token):
            pass_on(0, (token,))
            return (passed[0],)

        peer_parts, peer_sends, peer_gots = [], [], []
        waits = [
            (
                lambda t: (own_sends[1],),
                lambda t: (own_gots[0], low_steps[0]),
                lambda t: (own_gots[1],),
            ),
            (lambda t: (peer_sends[0],), after_first_part),
        ]
        for c in range(2):
            n = chunks[c][1]
            edges = (0, 2 * n // 3, n) if c else (0, 3 * n // 7, 5 * n // 7, n)
            peer_parts.append(forward(peer_normed, c, edges, waits[c])[0])
            (send,) = share_sums(peer_parts[c], own, 1, () if c else (low_own,))
            peer_sends.append(send)
            peer_gots.append(swap(send, "hid", hid, last_bit))

        def gradients(c, after):
            mine_grad, other_grad, back_part = gated_gradients(
                d, own_parts[c] + [own_gots[c]], others[c], cotangent, chunks[c][0] * tile, low_own, up, own, after
            )
            return back_part, mine_grad, swap(other_grad, "dp", dp, 1)

        def spread(g):
            blocks = [g]
            for bit in reversed(range(bits_of(hid))):
                blocks += [swap(x, "hid", hid, 1 << bit) for x in blocks]
            return blocks

        back, mine_grad, peer_grad = gradients(0, (peer_sends[1],))
        own_pieces = spread(mine_grad)
        pass_on(1, (own_pieces[1],))
        peer_pieces = spread(relay(peer_grad, (passed[1],)))
        grads = [own_pieces + peer_pieces]
        more, mine_grad, peer_grad = gradients(1, (peer_pieces[1],))
        back = back + more

        def first_half(j, after):
            first, n = steps[j]
            return backward_matmul(grads[0], weights, 0, first, n, width_tile, partial=True, after=after)

        bases = [first_half(0, (mine_grad,))]
        own_pieces = spread(mine_grad)
        peer_pieces = spread(relay(peer_grad, (bases[0],)))
        grads.append(own_pieces + peer_pieces)
        back_steps = []
        for bit in range(bits_of(ffn)):
            back = back + swap(back, "ffn", ffn, 1 << bit)
            back_steps.append(back)
        for j in range(1, len(steps)):
            bases.append(first_half(j, (own_pieces[1], back_steps[0], bases[-1])))

        shard = tokens // ffn
        place = reversed_bits(f, bits_of(ffn))
        products, received = [], []

        def halving_step(parts, bit):
            half = parts[-1].shape[0] // 2
            mine = (f >> bit) & 1
            sides = [
                [lax.dynamic_slice_in_dim(p, side * half, half, axis=0) for p in parts]
                for side in (mine, 1 - mine)
            ]
            return total_of(sides[0], 0, half), total_of(sides[1], 0, half).astype(BF16)

        begun = []
        for j, (first, n) in enumerate(steps):
            wait = (products[-1],) if products else (bases[-1], back_steps[-1])
            if j == 2:
                back = double(relay(back, (products[0],)), "hid", hid)
                keep, send = halving_step([products[0], received[0]], 0)
                begun = [keep, swap(send, "ffn", ffn, 1)]
                wait += (back, begun[1])
            keep, send = backward_matmul(
                grads[1], weights, chunks[1][0] * tile, first, n, width_tile, base=bases[j], base_first=first,
                after=wait,
            )
            products.append(keep)
            received.append(swap(send, "dp", dp, 1))
        low_all = double(relay(low_own, (products[-1],)), "hid", hid)
        low_mine = jnp.where(first_pair, low_all[:, :rank], low_all[:, rank:])
        low_other = swap(jnp.where(first_pair, low_all[:, rank:], low_all[:, :rank]), "dp", dp, 1)
        if len(steps) < 3:
            back = double(back, "hid", hid)
        back_low = back[:, : 2 * rank].astype(BF16)
        acts_product = back[:, 2 * rank]

        block = min(own, shard)

        def natural(row):
            index = row // own
            return (h ^ reversed_bits(index, bits_of(hid))) * own + row % own

        def shard_rows(x):
            return jnp.concatenate(
                [
                    lax.dynamic_slice_in_dim(x, natural(place * shard + i * block), block, axis=0)
                    for i in range(shard // block)
                ],
                axis=0,
            )

        stats_shard = shard_rows(stats)
        dot_shard = lax.dynamic_slice_in_dim(acts_product, place * shard, shard, axis=0)
        dot_factor = stats_shard[:, 1] ** 2 * dot_shard / MODEL_WIDTH
        stats_shard = jnp.concatenate([stats_shard, dot_factor[:, None]], axis=1)
        stream_shard = shard_rows(stream)
        back_shard = lax.dynamic_slice_in_dim(back_low, place * shard, shard, axis=0)

        out, sums, gathered = None, [], []
        owners = [reversed_bits(f ^ reversed_bits(p, bits_of(ffn)), bits_of(ffn)) for p in range(ffn)]
        places = jnp.stack([natural(o * shard + i * block) for o in owners for i in range(shard // block)])
        for j, (first, n) in enumerate(steps):
            parts = [products[j], received[j]]
            for bit in range(bits_of(ffn)):
                if j == 0 and bit == 0 and begun:
                    parts = begun
                    continue
                keep, send = halving_step(parts, bit)
                parts = [keep, swap(send, "ffn", ffn, 1 << bit)]
            result, sum_part = finish(
                parts, stream_shard, stats_shard, back_shard, down_rows, steering, gain, first * width_tile,
                after=tuple(gathered[j - 1][1:2] if j else ()) + tuple(gathered[j - 2][2:] if j >= 2 else ()),
            )
            sums.append(sum_part)
            if j == len(steps) - 1:
                sums = jnp.concatenate(sums, axis=1)
                sums = jnp.pad(sums, ((0, 0), (0, -width % result.shape[1]))).reshape(-1, result.shape[1])
                high = sums.astype(BF16)
                low_term = (sums - high.astype(F32)).astype(BF16)
                rows = 2 * sums.shape[0]
                empty = jnp.zeros((-rows % 16, result.shape[1]), BF16)
                result = jnp.concatenate([result, high, low_term, empty], axis=0)
            blocks = [result]
            for bit in reversed(range(bits_of(ffn))):
                blocks += [swap(x, "ffn", ffn, 1 << bit) for x in blocks]
            gathered.append(blocks)
            out = assemble(blocks, places, block, shard, tokens, width, first * width_tile, into=out)

        half = rows // 2
        terms = [
            x[shard : shard + half].astype(F32) + x[shard + half : shard + rows].astype(F32) for x in blocks
        ]
        while len(terms) > 1:
            terms = [a + b for a, b in zip(terms[: len(terms) // 2], terms[len(terms) // 2 :])]
        steering_gradient = terms[0] + swap(terms[0], "dp", dp, 1)

        low_rows = jnp.concatenate([low_mine, low_other], axis=0).T
        up_mine = jnp.concatenate(adapter_products(low_rows, grads, (received[-1],)), axis=1)
        up_other = swap(up_mine.astype(BF16), "dp", dp, 1).astype(F32)
        up_gradient = jnp.where(
            first_pair, jnp.stack([up_mine, up_other]), jnp.stack([up_other, up_mine])
        )
        peer_back = swap(relay(back_low, (received[-1],)), "dp", dp, 1)
        back_rows = jnp.concatenate([back_low, peer_back], axis=0).T
        (down_gradient,) = adapter_products(back_rows, [[own_normed, peer_normed]])
        down_gradient = jnp.transpose(
            down_gradient.reshape(2, rank, width), (0, 2, 1)
        )
        return out, steering_gradient.reshape(-1)[:width], down_gradient, up_gradient

    return local


def solution(mesh):
    in_specs = (
        P("dp", "hid"),
        P("hid"),
        P("dp"),
        P("hid"),
        P("dp", "hid", "ffn"),
        P(None, "hid", None),
        P(None, None, "ffn"),
        P(("dp", "hid"), "ffn"),
    )
    out_specs = (P("dp", "hid"), P("hid"), P(None, "hid", None), P(None, None, "ffn"))
    local = make_local(mesh.shape["dp"], mesh.shape["hid"], mesh.shape["ffn"])
    return jax.shard_map(local, mesh=mesh, in_specs=in_specs, out_specs=out_specs, check_vma=False)
```

```python
import jax
import jax.numpy as jnp
from jax import lax
from jax.experimental import pallas as pl
from jax.experimental.pallas import tpu as pltpu
from jax.sharding import PartitionSpec as P

MODEL_WIDTH = 16384
ADAPTER_SCALE = 0.5
VMEM_MIB = 12
MATMUL_VMEM_MIB = 24
COST_SHARE = 0.01

F32 = jnp.float32
BF16 = jnp.bfloat16
ANY = pl.BlockSpec(memory_space=pl.ANY)
RESIDENT = pl.BlockSpec(memory_space=pltpu.VMEM)


def bits_of(n):
    return n.bit_length() - 1


def reversed_bits(x, n):
    out = 0
    for i in range(n):
        out = out + (((x >> i) & 1) << (n - 1 - i))
    return out


def tile_of(n, cap):
    return max(t for t in range(128, cap + 1, 128) if n % t == 0)


def split_tiles(count, parts):
    edges = [count * i // parts for i in range(parts + 1)]
    return [(a, b - a) for a, b in zip(edges, edges[1:]) if b > a]


def swap(x, axis, n, mask):
    return lax.ppermute(x, axis, [(i, i ^ mask) for i in range(n)])


def double(x, axis, n, dim=0):
    for bit in reversed(range(bits_of(n))):
        x = jnp.concatenate([x, swap(x, axis, n, 1 << bit)], axis=dim)
    return x


def total_of(parts, start, stop):
    out = parts[0][start:stop]
    for part in parts[1:]:
        out = out + part[start:stop].astype(F32)
    return out


def params(mib=VMEM_MIB):
    return pltpu.CompilerParams(vmem_limit_bytes=mib * 1024 * 1024)


def cost(flops, size):
    return pl.CostEstimate(
        flops=int(flops * COST_SHARE), bytes_accessed=int(size * COST_SHARE), transcendentals=0
    )


def normalize(stream, stats, steering, gain, down, h, hid, after=()):
    tokens, width = stream.shape
    block = tokens // hid
    ranks = down.shape[0]

    def token_block(p, h_ref):
        return h_ref[0] ^ reversed_bits(p, bits_of(hid))

    def kernel(h_ref, x_ref, stat_ref, steer_ref, gain_ref, down_ref, *refs):
        steered = x_ref[...].astype(F32) + stat_ref[:, :1] * steer_ref[...]
        normed = (steered * stat_ref[:, 1:] * gain_ref[...]).astype(BF16)
        refs[-2][...] = normed
        refs[-1][...] = lax.dot_general(
            normed, down_ref[...], (((1,), (1,)), ((), ())), preferred_element_type=F32
        )

    whole = lambda n: pl.BlockSpec((n, width), lambda p, h_ref: (0, 0))
    rows = lambda n, m: pl.BlockSpec((n, m), lambda p, h_ref: (p, 0))
    return pl.pallas_call(
        kernel,
        grid_spec=pltpu.PrefetchScalarGridSpec(
            num_scalar_prefetch=1,
            grid=(hid,),
            in_specs=[
                pl.BlockSpec((block, width), lambda p, h_ref: (token_block(p, h_ref), 0)),
                pl.BlockSpec((block, 2), lambda p, h_ref: (token_block(p, h_ref), 0)),
                whole(1),
                whole(1),
                whole(ranks),
            ]
            + [ANY] * len(after),
            out_specs=[rows(block, width), rows(block, ranks)],
        ),
        out_shape=[
            jax.ShapeDtypeStruct((tokens, width), BF16),
            jax.ShapeDtypeStruct((tokens, ranks), F32),
        ],
        compiler_params=params(),
        cost_estimate=cost(2 * tokens * width * ranks, 4 * tokens * width),
        name="normalize",
    )(
        h.reshape(1),
        stream,
        stats,
        steering.reshape(1, width),
        gain.reshape(1, width),
        down,
        *after,
    )


def relay(x, after):
    def kernel(x_ref, *refs):
        refs[-1][...] = x_ref[...]

    whole = pl.BlockSpec(x.shape, lambda i: (0,) * x.ndim)
    return pl.pallas_call(
        kernel,
        grid=(1,),
        in_specs=[whole] + [ANY] * len(after),
        out_specs=whole,
        out_shape=jax.ShapeDtypeStruct(x.shape, x.dtype),
        compiler_params=params(),
        cost_estimate=cost(0, 4 * x.size),
        name="relay",
    )(x, *after)


def forward_matmul(x, weights, first, tiles, start, stop, tile, into=(), after=()):
    rows, depth = x.shape
    half = rows // 2

    def kernel(x_ref, w_ref, *refs):
        keep_ref, send_ref, token_ref = refs[-3:]
        token_ref[...] = jnp.zeros_like(token_ref)
        y = jnp.dot(x_ref[...], w_ref[0], preferred_element_type=F32)
        keep_ref[...] = y[:half]
        send_ref[...] = y[half:].astype(BF16)

    return pl.pallas_call(
        kernel,
        grid=(stop - start,),
        in_specs=[RESIDENT, pl.BlockSpec((1, depth, tile), lambda i: (0, 0, first + start + i))]
        + [ANY] * (len(into) + len(after)),
        out_specs=[pl.BlockSpec((half, tile), lambda i: (0, start + i))] * 2
        + [pl.BlockSpec((8, 128), lambda i: (0, 0))],
        out_shape=[
            jax.ShapeDtypeStruct((half, tiles * tile), F32),
            jax.ShapeDtypeStruct((half, tiles * tile), BF16),
            jax.ShapeDtypeStruct((8, 128), F32),
        ],
        input_output_aliases={2 + i: i for i in range(len(into))},
        compiler_params=params(MATMUL_VMEM_MIB),
        cost_estimate=cost(2 * rows * depth * (stop - start) * tile, 2 * depth * (rows + (stop - start) * tile) + 6 * half * (stop - start) * tile),
        name="forward_matmul",
    )(x, weights, *into, *after)


def share_sums(parts, rows, count, after=(), places=None):
    columns = parts[0].shape[1]
    tile = tile_of(columns, 1792)

    def kernel(*refs):
        total = refs[0][...].astype(F32)
        for ref in refs[1 : len(parts)]:
            total = total + ref[...].astype(F32)
        for i in range(count):
            refs[i - count][...] = total[i * rows : (i + 1) * rows].astype(BF16)

    return pl.pallas_call(
        kernel,
        grid=(columns // tile,),
        in_specs=[
            pl.BlockSpec((count * rows, tile), lambda i, at=at: (at, i)) for at in places or [1] * len(parts)
        ]
        + [ANY] * len(after),
        out_specs=[pl.BlockSpec((rows, tile), lambda i: (0, i))] * count,
        out_shape=[jax.ShapeDtypeStruct((rows, columns), BF16)] * count,
        compiler_params=params(),
        cost_estimate=cost(count * rows * columns, 8 * count * rows * columns),
        name="share_sums",
    )(*parts, *after)


def gated_gradients(d, mine, other, cotangent, first, low, up, own, after=()):
    columns = other.shape[1]
    rank = up.shape[1]
    tile = max(t for t in range(128, 2049, 128) if columns % t == 0 and first % t == 0)
    tiles = columns // tile
    base = first // tile

    def kernel(d_ref, *refs):
        mine_refs = refs[: len(mine)]
        other_ref, flow_ref, low_ref, up_ref = refs[len(mine) : len(mine) + 4]
        mine_out, other_out, back_ref = refs[-3:]
        own_is_gate = d_ref[0] == 0
        total = mine_refs[0][...].astype(F32)
        for ref in mine_refs[1:]:
            total = total + ref[...].astype(F32)
        passed = other_ref[...].astype(F32)
        low_terms = [
            ADAPTER_SCALE
            * jnp.dot(low_ref[:, k * rank : (k + 1) * rank], up_ref[k], preferred_element_type=F32)
            for k in range(2)
        ]
        gate = jnp.where(own_is_gate, total, passed) + low_terms[0]
        upper = jnp.where(own_is_gate, passed, total) + low_terms[1]
        sigma = 1.0 / (1.0 + jnp.exp(-gate))
        flow = flow_ref[...].astype(F32)
        gate_grad = (flow * upper * sigma * (1.0 + gate * (1.0 - sigma))).astype(BF16)
        upper_grad = (flow * gate * sigma).astype(BF16)
        mine_out[...] = jnp.where(own_is_gate, gate_grad, upper_grad)
        other_out[...] = jnp.where(own_is_gate, upper_grad, gate_grad)

        @pl.when(pl.program_id(0) == 0)
        def _():
            back_ref[...] = jnp.zeros_like(back_ref)

        contract = (((1,), (1,)), ((), ()))
        for k, grad in enumerate((gate_grad, upper_grad)):
            back_ref[:, k * rank : (k + 1) * rank] += lax.dot_general(
                grad, up_ref[k], contract, preferred_element_type=F32
            )
        back_ref[:, 2 * rank :] += jnp.sum(
            gate_grad.astype(F32) * gate + upper_grad.astype(F32) * upper, axis=1, keepdims=True
        )

    here = pl.BlockSpec((own, tile), lambda i, d_ref: (0, i))
    there = pl.BlockSpec((own, tile), lambda i, d_ref: (0, base + i))
    return pl.pallas_call(
        kernel,
        grid_spec=pltpu.PrefetchScalarGridSpec(
            num_scalar_prefetch=1,
            grid=(tiles,),
            in_specs=[here] * (len(mine) + 1)
            + [
                there,
                pl.BlockSpec((own, 2 * rank), lambda i, d_ref: (0, 0)),
                pl.BlockSpec((2, rank, tile), lambda i, d_ref: (0, 0, base + i)),
            ]
            + [ANY] * len(after),
            out_specs=[here, here, pl.BlockSpec((own, 2 * rank + 1), lambda i, d_ref: (0, 0))],
        ),
        out_shape=[
            jax.ShapeDtypeStruct((own, columns), BF16),
            jax.ShapeDtypeStruct((own, columns), BF16),
            jax.ShapeDtypeStruct((own, 2 * rank + 1), F32),
        ],
        compiler_params=params(),
        cost_estimate=cost(8 * own * columns * rank, 16 * own * columns),
        name="gated_gradients",
    )(d.reshape(1), *mine, other, cotangent, low, up, *after)


def backward_matmul(pieces, weights, hidden_start, first, tiles, tile, base=None, base_first=0, partial=False, after=()):
    rows = sum(g.shape[0] for g in pieces)
    half = rows // 2
    n_base = 0 if base is None else 1
    hidden = pieces[0].shape[1]

    def kernel(*refs):
        w_ref = refs[len(pieces)]
        g = jnp.concatenate([ref[...] for ref in refs[: len(pieces)]], axis=0)
        y = lax.dot_general(g, w_ref[0], (((1,), (1,)), ((), ())), preferred_element_type=F32)
        if n_base:
            y = y + refs[len(pieces) + 1][...]
        if partial:
            refs[-1][...] = y
        else:
            refs[-2][...] = y[:half]
            refs[-1][...] = y[half:].astype(BF16)

    if partial:
        out_specs = pl.BlockSpec((rows, tile), lambda i: (0, i))
        out_shape = jax.ShapeDtypeStruct((rows, tiles * tile), F32)
    else:
        out_specs = [pl.BlockSpec((half, tile), lambda i: (0, i))] * 2
        out_shape = [
            jax.ShapeDtypeStruct((half, tiles * tile), F32),
            jax.ShapeDtypeStruct((half, tiles * tile), BF16),
        ]
    return pl.pallas_call(
        kernel,
        grid=(tiles,),
        in_specs=[
            pl.BlockSpec(g.shape, lambda i: (0, 0), pipeline_mode=pl.Buffered(1)) for g in pieces
        ]
        + [
            pl.BlockSpec(
                (pl.Element(1), pl.Element(tile), pl.Element(hidden)),
                lambda i: (0, (first + i) * tile, hidden_start),
            )
        ]
        + [pl.BlockSpec((rows, tile), lambda i: (0, first - base_first + i))] * n_base
        + [ANY] * len(after),
        out_specs=out_specs,
        out_shape=out_shape,
        compiler_params=params(MATMUL_VMEM_MIB),
        cost_estimate=cost(2 * rows * hidden * tiles * tile, 2 * hidden * (rows + tiles * tile) + (4 + 4 * n_base) * rows * tiles * tile),
        name="backward_matmul",
    )(*pieces, weights, *(() if base is None else (base,)), *after)


def adapter_products(low, groups, after=()):
    rank = low.shape[0]

    def kernel(*refs):
        at = 1
        for i, pieces in enumerate(groups):
            g = jnp.concatenate([ref[...] for ref in refs[at : at + len(pieces)]], axis=0)
            at += len(pieces)
            refs[i - len(groups)][...] = ADAPTER_SCALE * jnp.dot(
                refs[0][...], g, preferred_element_type=F32
            )

    operands = [g for pieces in groups for g in pieces]
    widths = [pieces[0].shape[1] for pieces in groups]
    return pl.pallas_call(
        kernel,
        grid=(1,),
        in_specs=[pl.BlockSpec(x.shape, lambda i: (0, 0)) for x in [low] + operands] + [ANY] * len(after),
        out_specs=[pl.BlockSpec((rank, w), lambda i: (0, 0)) for w in widths],
        out_shape=[jax.ShapeDtypeStruct((rank, w), F32) for w in widths],
        compiler_params=params(),
        cost_estimate=cost(2 * rank * low.shape[1] * sum(widths), 2 * low.shape[1] * sum(widths)),
        name="adapter_products",
    )(low, *operands, *after)


def assemble(pieces, places, block, rows, tokens, width, columns, into=None):
    chunk = pieces[0].shape[1]

    def kernel(place_ref, *refs):
        out_ref = refs[-1]
        i = 0
        for ref in refs[: len(pieces)]:
            for r in range(0, rows, block):
                out_ref[pl.ds(pl.multiple_of(place_ref[i], block), block), :] = ref[r : r + block, :]
                i += 1

    n_into = 0 if into is None else 1
    return pl.pallas_call(
        kernel,
        grid_spec=pltpu.PrefetchScalarGridSpec(
            num_scalar_prefetch=1,
            grid=(1,),
            in_specs=[pl.BlockSpec(x.shape, lambda i, p: (0, 0)) for x in pieces] + [ANY] * n_into,
            out_specs=pl.BlockSpec((pl.Element(tokens), pl.Element(chunk)), lambda i, p: (0, columns)),
        ),
        out_shape=jax.ShapeDtypeStruct((tokens, width), BF16),
        input_output_aliases={len(pieces) + 1: 0} if n_into else {},
        compiler_params=params(),
        cost_estimate=cost(0, 4 * tokens * chunk),
        name="assemble",
    )(places, *pieces, *((into,) if n_into else ()))


def finish(parts, stream, stats, back, down, steering, gain, columns, after=()):
    rows = stream.shape[0]
    width = parts[0].shape[1]

    def kernel(*refs):
        part_refs = refs[: len(parts)]
        x_ref, s_ref, back_ref, down_ref, steer_ref, gain_ref = refs[len(parts) : len(parts) + 6]
        out_ref, sum_ref = refs[-2:]
        total = part_refs[0][...].astype(F32)
        for ref in part_refs[1:]:
            total = total + ref[...].astype(F32)
        total = total + ADAPTER_SCALE * jnp.dot(back_ref[...], down_ref[...], preferred_element_type=F32)
        steered = x_ref[...].astype(F32) + s_ref[:, 0:1] * steer_ref[...]
        grad = s_ref[:, 1:2] * gain_ref[...] * total - s_ref[:, 2:3] * steered
        out_ref[...] = grad.astype(BF16)
        sum_ref[...] = jnp.sum(s_ref[:, 0:1] * grad, axis=0, keepdims=True)

    across = lambda n: pl.BlockSpec((pl.Element(n), pl.Element(width)), lambda i: (0, columns))
    return pl.pallas_call(
        kernel,
        grid=(1,),
        in_specs=[pl.BlockSpec((rows, width), lambda i: (0, 0))] * len(parts)
        + [
            across(rows),
            pl.BlockSpec(stats.shape, lambda i: (0, 0)),
            pl.BlockSpec(back.shape, lambda i: (0, 0)),
            across(down.shape[0]),
            across(1),
            across(1),
        ]
        + [ANY] * len(after),
        out_specs=[pl.BlockSpec((rows, width), lambda i: (0, 0)), pl.BlockSpec((1, width), lambda i: (0, 0))],
        out_shape=[jax.ShapeDtypeStruct((rows, width), BF16), jax.ShapeDtypeStruct((1, width), F32)],
        compiler_params=params(),
        cost_estimate=cost(2 * rows * width * down.shape[0], 10 * rows * width),
        name="finish",
    )(*parts, stream, stats, back, down, steering.reshape(1, -1), gain.reshape(1, -1), *after)


def make_local(dp, hid, ffn):
    def local(stream, steering, strength, gain, weights, down, up, cotangent):
        d, h, f = lax.axis_index("dp"), lax.axis_index("hid"), lax.axis_index("ffn")
        tokens, width = stream.shape
        hidden = weights.shape[2]
        own = tokens // hid
        rank = down.shape[2]
        first_pair = d == 0
        down_rows = jnp.transpose(down, (0, 2, 1)).reshape(2 * rank, width)

        peer_stream = swap(stream, "dp", dp, 1)
        rows = stream.astype(F32)
        total_rows, total_steer = lax.psum(
            (jnp.sum(rows * rows, axis=1), jnp.sum(steering * steering)), "hid"
        )
        stream_ms = total_rows / MODEL_WIDTH + 1e-06
        steer_ms = total_steer / MODEL_WIDTH + 1e-06
        scale = strength * jnp.sqrt(stream_ms / steer_ms)
        steered = rows + scale[:, None] * steering[None, :]
        steered_power = lax.psum(jnp.sum(steered * steered, axis=1), "hid")
        inv_rms = lax.rsqrt(steered_power / MODEL_WIDTH + 1e-05)
        stats = jnp.stack([scale, inv_rms], axis=1)
        peer_stats = swap(stats, "dp", dp, 1)

        tile = tile_of(hidden, 512)
        count = hidden // tile
        chunks = [(0, (count + 1) // 2), ((count + 1) // 2, count // 2)]
        last_bit = 1 << (bits_of(hid) - 1)
        own_normed, own_low = normalize(stream, stats, steering, gain, down_rows, h, hid)

        def forward(x, c, edges, afters):
            first, n = chunks[c]
            out, token = (), None
            for start, stop, after in zip(edges, edges[1:], afters):
                *out, token = forward_matmul(
                    x, weights, first, n, start, stop, tile, into=tuple(out), after=after(token)
                )
            keep, send = out
            parts = [keep, swap(send, "hid", hid, 1)]
            for bit in range(1, bits_of(hid) - 1):
                size = parts[-1].shape[0]
                send = total_of(parts, size // 2, size).astype(BF16)
                parts.append(swap(send, "hid", hid, 1 << bit))
            return parts, token

        width_tile = tile_of(width, 512)
        tiles = width // width_tile
        steps = [(0, 2), (2, 3), (5, 3)] if tiles == 8 else split_tiles(tiles, 3)

        own_parts, own_sends, own_gots = [], [], []
        for c in range(2):
            wait = tuple(own_sends)
            parts, token = forward(own_normed, c, (0, chunks[c][1]), (lambda t: wait,))
            own_parts.append(parts)
            (send,) = share_sums(own_parts[c], own, 1)
            own_sends.append(send)
            own_gots.append(swap(send, "hid", hid, last_bit))

        peer_normed, _ = normalize(
            peer_stream, peer_stats, steering, gain, down_rows, h, hid, (own_sends[0], token)
        )

        low, low_steps = relay(own_low, (peer_normed,)), []
        for bit in range(bits_of(hid)):
            half = low.shape[0] // 2
            low = low[:half] + swap(low[half:], "hid", hid, 1 << bit)
            low_steps.append(low)
        low_own = low.astype(BF16)

        passed, others = [], []

        def pass_on(c, after):
            terms = peer_parts[c] + [peer_gots[c]]
            (sums,) = share_sums(terms, own, 1, after, [0] * len(terms))
            passed.append(sums)
            others.append(swap(sums, "dp", dp, 1))

        def after_first_part(token):
            pass_on(0, (token,))
            return (passed[0],)

        peer_parts, peer_sends, peer_gots = [], [], []
        waits = [
            (
                lambda t: (own_sends[1],),
                lambda t: (own_gots[0], low_steps[0]),
                lambda t: (own_gots[1],),
            ),
            (lambda t: (peer_sends[0],), after_first_part),
        ]
        for c in range(2):
            n = chunks[c][1]
            edges = (0, 2 * n // 3, n) if c else (0, 3 * n // 7, 5 * n // 7, n)
            peer_parts.append(forward(peer_normed, c, edges, waits[c])[0])
            (send,) = share_sums(peer_parts[c], own, 1, () if c else (low_own,))
            peer_sends.append(send)
            peer_gots.append(swap(send, "hid", hid, last_bit))

        def gradients(c, after):
            mine_grad, other_grad, back_part = gated_gradients(
                d, own_parts[c] + [own_gots[c]], others[c], cotangent, chunks[c][0] * tile, low_own, up, own, after
            )
            return back_part, mine_grad, swap(other_grad, "dp", dp, 1)

        def spread(g):
            blocks = [g]
            for bit in reversed(range(bits_of(hid))):
                blocks += [swap(x, "hid", hid, 1 << bit) for x in blocks]
            return blocks

        pass_on(1, (others[0],))
        back, mine_grad, peer_grad = gradients(0, (passed[1],))
        own_pieces = spread(mine_grad)
        more, mine_grad, second_peer_grad = gradients(1, (own_pieces[1],))
        back = back + more
        grads = [own_pieces + spread(relay(peer_grad, (mine_grad,)))]

        def first_half(j, after):
            first, n = steps[j]
            return backward_matmul(grads[0], weights, 0, first, n, width_tile, partial=True, after=after)

        own_pieces = spread(mine_grad)
        peer_grad = relay(second_peer_grad, (own_pieces[1],))
        grads.append(own_pieces + spread(peer_grad))
        back_steps = []
        for bit in range(bits_of(ffn)):
            back = back + swap(back, "ffn", ffn, 1 << bit)
            back_steps.append(back)
        bases = [first_half(0, (peer_grad, back_steps[0]))]

        shard = tokens // ffn
        place = reversed_bits(f, bits_of(ffn))
        products, received = [], []

        def halving_step(parts, bit):
            half = parts[-1].shape[0] // 2
            mine = (f >> bit) & 1
            sides = [
                [lax.dynamic_slice_in_dim(p, side * half, half, axis=0) for p in parts]
                for side in (mine, 1 - mine)
            ]
            return total_of(sides[0], 0, half), total_of(sides[1], 0, half).astype(BF16)

        begun = []
        for j, (first, n) in enumerate(steps):
            wait = (products[-1],) if products else (back_steps[-1],)
            if j:
                bases.append(first_half(j, wait))
            if j == 2:
                back = double(relay(back, (products[0],)), "hid", hid)
                keep, send = halving_step([products[0], received[0]], 0)
                begun = [keep, swap(send, "ffn", ffn, 1)]
                wait += (back, begun[1])
            keep, send = backward_matmul(
                grads[1], weights, chunks[1][0] * tile, first, n, width_tile, base=bases[j], base_first=first,
                after=wait,
            )
            products.append(keep)
            received.append(swap(send, "dp", dp, 1))
        low_all = double(relay(low_own, (products[-1],)), "hid", hid)
        low_mine = jnp.where(first_pair, low_all[:, :rank], low_all[:, rank:])
        low_other = swap(jnp.where(first_pair, low_all[:, rank:], low_all[:, :rank]), "dp", dp, 1)
        if len(steps) < 3:
            back = double(back, "hid", hid)
        back_low = back[:, : 2 * rank].astype(BF16)
        acts_product = back[:, 2 * rank]

        block = min(own, shard)

        def natural(row):
            index = row // own
            return (h ^ reversed_bits(index, bits_of(hid))) * own + row % own

        def shard_rows(x):
            return jnp.concatenate(
                [
                    lax.dynamic_slice_in_dim(x, natural(place * shard + i * block), block, axis=0)
                    for i in range(shard // block)
                ],
                axis=0,
            )

        stats_shard = shard_rows(stats)
        dot_shard = lax.dynamic_slice_in_dim(acts_product, place * shard, shard, axis=0)
        dot_factor = stats_shard[:, 1] ** 2 * dot_shard / MODEL_WIDTH
        stats_shard = jnp.concatenate([stats_shard, dot_factor[:, None]], axis=1)
        stream_shard = shard_rows(stream)
        back_shard = lax.dynamic_slice_in_dim(back_low, place * shard, shard, axis=0)

        out, sums, gathered = None, [], []
        owners = [reversed_bits(f ^ reversed_bits(p, bits_of(ffn)), bits_of(ffn)) for p in range(ffn)]
        places = jnp.stack([natural(o * shard + i * block) for o in owners for i in range(shard // block)])
        for j, (first, n) in enumerate(steps):
            parts = [products[j], received[j]]
            for bit in range(bits_of(ffn)):
                if j == 0 and bit == 0 and begun:
                    parts = begun
                    continue
                keep, send = halving_step(parts, bit)
                parts = [keep, swap(send, "ffn", ffn, 1 << bit)]
            result, sum_part = finish(
                parts, stream_shard, stats_shard, back_shard, down_rows, steering, gain, first * width_tile,
                after=tuple(gathered[j - 1][1:2] if j else ()) + tuple(gathered[j - 2][2:] if j >= 2 else ()),
            )
            sums.append(sum_part)
            if j == len(steps) - 1:
                sums = jnp.concatenate(sums, axis=1)
                sums = jnp.pad(sums, ((0, 0), (0, -width % result.shape[1]))).reshape(-1, result.shape[1])
                high = sums.astype(BF16)
                low_term = (sums - high.astype(F32)).astype(BF16)
                rows = 2 * sums.shape[0]
                empty = jnp.zeros((-rows % 16, result.shape[1]), BF16)
                result = jnp.concatenate([result, high, low_term, empty], axis=0)
            blocks = [result]
            for bit in reversed(range(bits_of(ffn))):
                blocks += [swap(x, "ffn", ffn, 1 << bit) for x in blocks]
            gathered.append(blocks)
            out = assemble(blocks, places, block, shard, tokens, width, first * width_tile, into=out)

        half = rows // 2
        terms = [
            x[shard : shard + half].astype(F32) + x[shard + half : shard + rows].astype(F32) for x in blocks
        ]
        while len(terms) > 1:
            terms = [a + b for a, b in zip(terms[: len(terms) // 2], terms[len(terms) // 2 :])]
        steering_gradient = terms[0] + swap(terms[0], "dp", dp, 1)

        low_rows = jnp.concatenate([low_mine, low_other], axis=0).T
        up_mine = jnp.concatenate(adapter_products(low_rows, grads, (received[-1],)), axis=1)
        up_other = swap(up_mine.astype(BF16), "dp", dp, 1).astype(F32)
        up_gradient = jnp.where(
            first_pair, jnp.stack([up_mine, up_other]), jnp.stack([up_other, up_mine])
        )
        peer_back = swap(relay(back_low, (received[-1],)), "dp", dp, 1)
        back_rows = jnp.concatenate([back_low, peer_back], axis=0).T
        (down_gradient,) = adapter_products(back_rows, [[own_normed, peer_normed]])
        down_gradient = jnp.transpose(
            down_gradient.reshape(2, rank, width), (0, 2, 1)
        )
        return out, steering_gradient.reshape(-1)[:width], down_gradient, up_gradient

    return local


def solution(mesh):
    in_specs = (
        P("dp", "hid"),
        P("hid"),
        P("dp"),
        P("hid"),
        P("dp", "hid", "ffn"),
        P(None, "hid", None),
        P(None, None, "ffn"),
        P(("dp", "hid"), "ffn"),
    )
    out_specs = (P("dp", "hid"), P("hid"), P(None, "hid", None), P(None, None, "ffn"))
    local = make_local(mesh.shape["dp"], mesh.shape["hid"], mesh.shape["ffn"])
    return jax.shard_map(local, mesh=mesh, in_specs=in_specs, out_specs=out_specs, check_vma=False)
```

```python
import jax
import jax.numpy as jnp
from jax import lax
from jax.experimental import pallas as pl
from jax.experimental.pallas import tpu as pltpu
from jax.sharding import PartitionSpec as P

MODEL_WIDTH = 16384
ADAPTER_SCALE = 0.5
VMEM_MIB = 12
MATMUL_VMEM_MIB = 24
COST_SHARE = 0.01

F32 = jnp.float32
BF16 = jnp.bfloat16
ANY = pl.BlockSpec(memory_space=pl.ANY)
RESIDENT = pl.BlockSpec(memory_space=pltpu.VMEM)


def bits_of(n):
    return n.bit_length() - 1


def reversed_bits(x, n):
    out = 0
    for i in range(n):
        out = out + (((x >> i) & 1) << (n - 1 - i))
    return out


def tile_of(n, cap):
    return max(t for t in range(128, cap + 1, 128) if n % t == 0)


def split_tiles(count, parts):
    edges = [count * i // parts for i in range(parts + 1)]
    return [(a, b - a) for a, b in zip(edges, edges[1:]) if b > a]


def swap(x, axis, n, mask):
    return lax.ppermute(x, axis, [(i, i ^ mask) for i in range(n)])


def double(x, axis, n, dim=0):
    for bit in reversed(range(bits_of(n))):
        x = jnp.concatenate([x, swap(x, axis, n, 1 << bit)], axis=dim)
    return x


def ordered(x, *first):
    return lax.optimization_barrier((x, *first))[0]


def total_of(parts, start, stop):
    out = parts[0][start:stop]
    for part in parts[1:]:
        out = out + part[start:stop].astype(F32)
    return out


def params(mib=VMEM_MIB):
    return pltpu.CompilerParams(vmem_limit_bytes=mib * 1024 * 1024)


def cost(flops, size):
    return pl.CostEstimate(
        flops=int(flops * COST_SHARE), bytes_accessed=int(size * COST_SHARE), transcendentals=0
    )


def normalize(stream, stats, steering, gain, down, h, hid, beside=None):
    tokens, width = stream.shape
    block = tokens // hid
    ranks = down.shape[0]
    n_beside = 0 if beside is None else 1

    def token_block(p, h_ref):
        return h_ref[0] ^ reversed_bits(p, bits_of(hid))

    def kernel(h_ref, x_ref, stat_ref, steer_ref, gain_ref, down_ref, *refs):
        steered = x_ref[...].astype(F32) + stat_ref[:, :1] * steer_ref[...]
        normed = (steered * stat_ref[:, 1:] * gain_ref[...]).astype(BF16)
        out_ref, low_ref = refs[n_beside : n_beside + 2]
        out_ref[...] = normed
        low_ref[...] = lax.dot_general(
            normed, down_ref[...], (((1,), (1,)), ((), ())), preferred_element_type=F32
        )
        if n_beside:
            refs[-1][:block, :] = refs[0][...]
            refs[-1][block:, :] = normed

    whole = lambda n: pl.BlockSpec((n, width), lambda p, h_ref: (0, 0))
    rows = lambda n, m: pl.BlockSpec((n, m), lambda p, h_ref: (p, 0))
    return pl.pallas_call(
        kernel,
        grid_spec=pltpu.PrefetchScalarGridSpec(
            num_scalar_prefetch=1,
            grid=(hid,),
            in_specs=[
                pl.BlockSpec((block, width), lambda p, h_ref: (token_block(p, h_ref), 0)),
                pl.BlockSpec((block, 2), lambda p, h_ref: (token_block(p, h_ref), 0)),
                whole(1),
                whole(1),
                whole(ranks),
            ]
            + [rows(block, width)] * n_beside,
            out_specs=[rows(block, width), rows(block, ranks)] + [rows(2 * block, width)] * n_beside,
        ),
        out_shape=[
            jax.ShapeDtypeStruct((tokens, width), BF16),
            jax.ShapeDtypeStruct((tokens, ranks), F32),
        ]
        + [jax.ShapeDtypeStruct((2 * tokens, width), BF16)] * n_beside,
        compiler_params=params(),
        cost_estimate=cost(2 * tokens * width * ranks, 4 * tokens * width),
        name="normalize",
    )(
        h.reshape(1),
        stream,
        stats,
        steering.reshape(1, width),
        gain.reshape(1, width),
        down,
        *((beside,) if n_beside else ()),
    )


def forward_matmul(x, weights, first, tiles, start, stop, tile, into=(), after=()):
    rows, depth = x.shape
    half = rows // 2

    def kernel(x_ref, w_ref, *refs):
        keep_ref, send_ref, token_ref = refs[-3:]
        token_ref[...] = jnp.zeros_like(token_ref)
        y = jnp.dot(x_ref[...], w_ref[0], preferred_element_type=F32)
        keep_ref[...] = y[:half]
        send_ref[...] = y[half:].astype(BF16)

    return pl.pallas_call(
        kernel,
        grid=(stop - start,),
        in_specs=[RESIDENT, pl.BlockSpec((1, depth, tile), lambda i: (0, 0, first + start + i))]
        + [ANY] * (len(into) + len(after)),
        out_specs=[pl.BlockSpec((half, tile), lambda i: (0, start + i))] * 2
        + [pl.BlockSpec((8, 128), lambda i: (0, 0))],
        out_shape=[
            jax.ShapeDtypeStruct((half, tiles * tile), F32),
            jax.ShapeDtypeStruct((half, tiles * tile), BF16),
            jax.ShapeDtypeStruct((8, 128), F32),
        ],
        input_output_aliases={2 + i: i for i in range(len(into))},
        compiler_params=params(MATMUL_VMEM_MIB),
        cost_estimate=cost(2 * rows * depth * (stop - start) * tile, 2 * depth * (rows + (stop - start) * tile) + 6 * half * (stop - start) * tile),
        name="forward_matmul",
    )(x, weights, *into, *after)


def relay(x, after):
    def kernel(x_ref, *refs):
        refs[-1][...] = x_ref[...]

    whole = pl.BlockSpec(x.shape, lambda i: (0,) * x.ndim)
    return pl.pallas_call(
        kernel,
        grid=(1,),
        in_specs=[whole] + [ANY] * len(after),
        out_specs=whole,
        out_shape=jax.ShapeDtypeStruct(x.shape, x.dtype),
        compiler_params=params(),
        cost_estimate=cost(0, 4 * x.size),
        name="relay",
    )(x, *after)


def share_sums(parts, rows, count, after=(), places=None):
    columns = parts[0].shape[1]
    tile = tile_of(columns, 1792)

    def kernel(*refs):
        total = refs[0][...].astype(F32)
        for ref in refs[1 : len(parts)]:
            total = total + ref[...].astype(F32)
        for i in range(count):
            refs[i - count][...] = total[i * rows : (i + 1) * rows].astype(BF16)

    return pl.pallas_call(
        kernel,
        grid=(columns // tile,),
        in_specs=[
            pl.BlockSpec((count * rows, tile), lambda i, at=at: (at, i)) for at in places or [1] * len(parts)
        ]
        + [ANY] * len(after),
        out_specs=[pl.BlockSpec((rows, tile), lambda i: (0, i))] * count,
        out_shape=[jax.ShapeDtypeStruct((rows, columns), BF16)] * count,
        compiler_params=params(),
        cost_estimate=cost(count * rows * columns, 8 * count * rows * columns),
        name="share_sums",
    )(*parts, *after)


def gated_gradients(d, mine, other, cotangent, first, low, up, own, after=()):
    columns = other.shape[1]
    rank = up.shape[1]
    tile = max(t for t in range(128, 2049, 128) if columns % t == 0 and first % t == 0)
    tiles = columns // tile
    base = first // tile

    def kernel(d_ref, *refs):
        mine_refs = refs[: len(mine)]
        other_ref, flow_ref, low_ref, up_ref = refs[len(mine) : len(mine) + 4]
        mine_out, other_out, back_ref = refs[-3:]
        own_is_gate = d_ref[0] == 0
        total = mine_refs[0][...].astype(F32)
        for ref in mine_refs[1:]:
            total = total + ref[...].astype(F32)
        passed = other_ref[...].astype(F32)
        low_terms = [
            ADAPTER_SCALE
            * jnp.dot(low_ref[:, k * rank : (k + 1) * rank], up_ref[k], preferred_element_type=F32)
            for k in range(2)
        ]
        gate = jnp.where(own_is_gate, total, passed) + low_terms[0]
        upper = jnp.where(own_is_gate, passed, total) + low_terms[1]
        sigma = 1.0 / (1.0 + jnp.exp(-gate))
        flow = flow_ref[...].astype(F32)
        gate_grad = (flow * upper * sigma * (1.0 + gate * (1.0 - sigma))).astype(BF16)
        upper_grad = (flow * gate * sigma).astype(BF16)
        mine_out[...] = jnp.where(own_is_gate, gate_grad, upper_grad)
        other_out[...] = jnp.where(own_is_gate, upper_grad, gate_grad)

        @pl.when(pl.program_id(0) == 0)
        def _():
            back_ref[...] = jnp.zeros_like(back_ref)

        contract = (((1,), (1,)), ((), ()))
        for k, grad in enumerate((gate_grad, upper_grad)):
            back_ref[:, k * rank : (k + 1) * rank] += lax.dot_general(
                grad, up_ref[k], contract, preferred_element_type=F32
            )
        back_ref[:, 2 * rank :] += jnp.sum(
            gate_grad.astype(F32) * gate + upper_grad.astype(F32) * upper, axis=1, keepdims=True
        )

    here = pl.BlockSpec((own, tile), lambda i, d_ref: (0, i))
    there = pl.BlockSpec((own, tile), lambda i, d_ref: (0, base + i))
    return pl.pallas_call(
        kernel,
        grid_spec=pltpu.PrefetchScalarGridSpec(
            num_scalar_prefetch=1,
            grid=(tiles,),
            in_specs=[here] * (len(mine) + 1)
            + [
                there,
                pl.BlockSpec((own, 2 * rank), lambda i, d_ref: (0, 0)),
                pl.BlockSpec((2, rank, tile), lambda i, d_ref: (0, 0, base + i)),
            ]
            + [ANY] * len(after),
            out_specs=[here, here, pl.BlockSpec((own, 2 * rank + 1), lambda i, d_ref: (0, 0))],
        ),
        out_shape=[
            jax.ShapeDtypeStruct((own, columns), BF16),
            jax.ShapeDtypeStruct((own, columns), BF16),
            jax.ShapeDtypeStruct((own, 2 * rank + 1), F32),
        ],
        compiler_params=params(),
        cost_estimate=cost(8 * own * columns * rank, 16 * own * columns),
        name="gated_gradients",
    )(d.reshape(1), *mine, other, cotangent, low, up, *after)


def backward_matmul(pieces, weights, hidden_start, first, tiles, tile, base=None, base_first=0, partial=False, after=()):
    rows = sum(g.shape[0] for g in pieces)
    half = rows // 2
    n_base = 0 if base is None else 1
    hidden = pieces[0].shape[1]

    def kernel(*refs):
        w_ref = refs[len(pieces)]
        g = jnp.concatenate([ref[...] for ref in refs[: len(pieces)]], axis=0)
        y = lax.dot_general(g, w_ref[0], (((1,), (1,)), ((), ())), preferred_element_type=F32)
        if n_base:
            y = y + refs[len(pieces) + 1][...]
        if partial:
            refs[-1][...] = y
        else:
            refs[-2][...] = y[:half]
            refs[-1][...] = y[half:].astype(BF16)

    if partial:
        out_specs = pl.BlockSpec((rows, tile), lambda i: (0, i))
        out_shape = jax.ShapeDtypeStruct((rows, tiles * tile), F32)
    else:
        out_specs = [pl.BlockSpec((half, tile), lambda i: (0, i))] * 2
        out_shape = [
            jax.ShapeDtypeStruct((half, tiles * tile), F32),
            jax.ShapeDtypeStruct((half, tiles * tile), BF16),
        ]
    return pl.pallas_call(
        kernel,
        grid=(tiles,),
        in_specs=[
            pl.BlockSpec(g.shape, lambda i: (0, 0), pipeline_mode=pl.Buffered(1)) for g in pieces
        ]
        + [
            pl.BlockSpec(
                (pl.Element(1), pl.Element(tile), pl.Element(hidden)),
                lambda i: (0, (first + i) * tile, hidden_start),
            )
        ]
        + [pl.BlockSpec((rows, tile), lambda i: (0, first - base_first + i))] * n_base
        + [ANY] * len(after),
        out_specs=out_specs,
        out_shape=out_shape,
        compiler_params=params(MATMUL_VMEM_MIB),
        cost_estimate=cost(2 * rows * hidden * tiles * tile, 2 * hidden * (rows + tiles * tile) + (4 + 4 * n_base) * rows * tiles * tile),
        name="backward_matmul",
    )(*pieces, weights, *(() if base is None else (base,)), *after)


def adapter_products(low, groups, after=()):
    rank = low.shape[0]

    def kernel(*refs):
        at = 1
        for i, pieces in enumerate(groups):
            g = jnp.concatenate([ref[...] for ref in refs[at : at + len(pieces)]], axis=0)
            at += len(pieces)
            refs[i - len(groups)][...] = ADAPTER_SCALE * jnp.dot(
                refs[0][...], g, preferred_element_type=F32
            )

    operands = [g for pieces in groups for g in pieces]
    widths = [pieces[0].shape[1] for pieces in groups]
    return pl.pallas_call(
        kernel,
        grid=(1,),
        in_specs=[pl.BlockSpec(x.shape, lambda i: (0, 0)) for x in [low] + operands] + [ANY] * len(after),
        out_specs=[pl.BlockSpec((rank, w), lambda i: (0, 0)) for w in widths],
        out_shape=[jax.ShapeDtypeStruct((rank, w), F32) for w in widths],
        compiler_params=params(),
        cost_estimate=cost(2 * rank * low.shape[1] * sum(widths), 2 * low.shape[1] * sum(widths)),
        name="adapter_products",
    )(low, *operands, *after)


def assemble(pieces, places, block, rows, tokens, width, columns, into=None):
    chunk = pieces[0].shape[1]

    def kernel(place_ref, *refs):
        out_ref = refs[-1]
        i = 0
        for ref in refs[: len(pieces)]:
            for r in range(0, rows, block):
                out_ref[pl.ds(pl.multiple_of(place_ref[i], block), block), :] = ref[r : r + block, :]
                i += 1

    n_into = 0 if into is None else 1
    return pl.pallas_call(
        kernel,
        grid_spec=pltpu.PrefetchScalarGridSpec(
            num_scalar_prefetch=1,
            grid=(1,),
            in_specs=[pl.BlockSpec(x.shape, lambda i, p: (0, 0)) for x in pieces] + [ANY] * n_into,
            out_specs=pl.BlockSpec((pl.Element(tokens), pl.Element(chunk)), lambda i, p: (0, columns)),
        ),
        out_shape=jax.ShapeDtypeStruct((tokens, width), BF16),
        input_output_aliases={len(pieces) + 1: 0} if n_into else {},
        compiler_params=params(),
        cost_estimate=cost(0, 4 * tokens * chunk),
        name="assemble",
    )(places, *pieces, *((into,) if n_into else ()))


def finish(parts, stream, stats, back, down, steering, gain, columns, after=()):
    rows = stream.shape[0]
    width = parts[0].shape[1]

    def kernel(*refs):
        part_refs = refs[: len(parts)]
        x_ref, s_ref, back_ref, down_ref, steer_ref, gain_ref = refs[len(parts) : len(parts) + 6]
        out_ref, sum_ref = refs[-2:]
        total = part_refs[0][...].astype(F32)
        for ref in part_refs[1:]:
            total = total + ref[...].astype(F32)
        total = total + ADAPTER_SCALE * jnp.dot(back_ref[...], down_ref[...], preferred_element_type=F32)
        steered = x_ref[...].astype(F32) + s_ref[:, 0:1] * steer_ref[...]
        grad = s_ref[:, 1:2] * gain_ref[...] * total - s_ref[:, 2:3] * steered
        out_ref[...] = grad.astype(BF16)
        sum_ref[...] = jnp.sum(s_ref[:, 0:1] * grad, axis=0, keepdims=True)

    across = lambda n: pl.BlockSpec((pl.Element(n), pl.Element(width)), lambda i: (0, columns))
    return pl.pallas_call(
        kernel,
        grid=(1,),
        in_specs=[pl.BlockSpec((rows, width), lambda i: (0, 0))] * len(parts)
        + [
            across(rows),
            pl.BlockSpec(stats.shape, lambda i: (0, 0)),
            pl.BlockSpec(back.shape, lambda i: (0, 0)),
            across(down.shape[0]),
            across(1),
            across(1),
        ]
        + [ANY] * len(after),
        out_specs=[pl.BlockSpec((rows, width), lambda i: (0, 0)), pl.BlockSpec((1, width), lambda i: (0, 0))],
        out_shape=[jax.ShapeDtypeStruct((rows, width), BF16), jax.ShapeDtypeStruct((1, width), F32)],
        compiler_params=params(),
        cost_estimate=cost(2 * rows * width * down.shape[0], 10 * rows * width),
        name="finish",
    )(*parts, stream, stats, back, down, steering.reshape(1, -1), gain.reshape(1, -1), *after)


def make_local(dp, hid, ffn):
    def local(stream, steering, strength, gain, weights, down, up, cotangent):
        d, h, f = lax.axis_index("dp"), lax.axis_index("hid"), lax.axis_index("ffn")
        tokens, width = stream.shape
        hidden = weights.shape[2]
        own = tokens // hid
        rank = down.shape[2]
        first_pair = d == 0
        down_rows = jnp.transpose(down, (0, 2, 1)).reshape(2 * rank, width)

        peer_stream = swap(stream, "dp", dp, 1)
        rows = stream.astype(F32)
        total_rows, total_steer = lax.psum(
            (jnp.sum(rows * rows, axis=1), jnp.sum(steering * steering)), "hid"
        )
        stream_ms = total_rows / MODEL_WIDTH + 1e-06
        steer_ms = total_steer / MODEL_WIDTH + 1e-06
        scale = strength * jnp.sqrt(stream_ms / steer_ms)
        steered = rows + scale[:, None] * steering[None, :]
        steered_power = lax.psum(jnp.sum(steered * steered, axis=1), "hid")
        inv_rms = lax.rsqrt(steered_power / MODEL_WIDTH + 1e-05)
        stats = jnp.stack([scale, inv_rms], axis=1)
        peer_stats = swap(stats, "dp", dp, 1)

        tile = tile_of(hidden, 512)
        count = hidden // tile
        chunks = [(0, (count + 1) // 2), ((count + 1) // 2, count // 2)]
        last_bit = 1 << (bits_of(hid) - 1)
        own_normed, own_low = normalize(stream, stats, steering, gain, down_rows, h, hid)
        def forward(x, c, edges, afters):
            first, n = chunks[c]
            out, token = (), None
            for start, stop, after in zip(edges, edges[1:], afters):
                *out, token = forward_matmul(
                    x, weights, first, n, start, stop, tile, into=tuple(out), after=after(token)
                )
            keep, send = out
            parts = [keep, swap(send, "hid", hid, 1)]
            for bit in range(1, bits_of(hid) - 1):
                size = parts[-1].shape[0]
                send = total_of(parts, size // 2, size).astype(BF16)
                parts.append(swap(send, "hid", hid, 1 << bit))
            return parts

        own_parts = forward(own_normed, 0, (0, chunks[0][1]), (lambda t: (),))
        (own_send,) = share_sums(own_parts, own, 1)
        own_got = swap(own_send, "hid", hid, last_bit)
        peer_normed, peer_low, normed = normalize(
            peer_stream, ordered(peer_stats, own_send), steering, gain, down_rows, h, hid, own_normed
        )

        low, low_steps = jnp.stack([own_low, peer_low]), []
        for bit in range(bits_of(hid)):
            half = low.shape[1] // 2
            low = low[:, :half] + swap(low[:, half:], "hid", hid, 1 << bit)
            low_steps.append(low)
        low = low.astype(BF16)
        low_own = low[0]

        width_tile = tile_of(width, 512)
        tiles = width // width_tile
        steps = [(0, 3), (3, 3), (6, 2)] if tiles == 8 else split_tiles(tiles, 3)
        acts, others, grads = [], [], []

        def gradients(c, after):
            mine_grad, other_grad, back_part = gated_gradients(
                d, acts[c], others[c], cotangent, chunks[c][0] * tile, low_own, up, own, after
            )
            return back_part, mine_grad, swap(other_grad, "dp", dp, 1)

        def spread(g):
            blocks = [g]
            for bit in reversed(range(bits_of(hid))):
                blocks += [swap(x, "hid", hid, 1 << bit) for x in blocks]
            return blocks

        n = chunks[0][1]
        peer_parts = forward(
            peer_normed, 0, (0, (n + 1) // 2, n), (lambda t: (own_send,), lambda t: (low_steps[0], own_got))
        )
        (peer_send,) = share_sums(peer_parts, own, 1, (low_own,))
        peer_got = swap(peer_send, "hid", hid, last_bit)
        acts.append(own_parts + [own_got])

        def pass_on(token):
            terms = peer_parts + [peer_got]
            (passed,) = share_sums(terms, own, 1, (token,), [0] * len(terms))
            others.append(swap(passed, "dp", dp, 1))
            return peer_got, passed

        n = chunks[1][1]
        first_send = peer_send
        first_half_done = []

        def first_gradients(token):
            more, mine_grad, peer_grad = gradients(0, (token,))
            own_pieces, peer_pieces = spread(mine_grad), spread(peer_grad)
            grads.append(own_pieces + peer_pieces)
            first_half_done.append(more)
            return peer_grad, own_pieces[1]

        parts = forward(
            normed, 1, (0, n // 3, n - 1, n), (lambda t: (first_send,), pass_on, first_gradients)
        )
        own_send, peer_send = share_sums(parts, own, 2)
        peer_got = swap(peer_send, "hid", hid, last_bit)
        own_got = swap(own_send, "hid", hid, last_bit)
        bases = []

        def first_half(j, after):
            first, n = steps[j]
            bases.append(
                backward_matmul(
                    grads[0], weights, 0, first, n, width_tile, partial=True, after=after
                )
            )

        first_half(0, (own_send,))
        (passed,) = share_sums(parts + [peer_got], own, 1, (bases[0],), [1] * len(parts) + [0])
        acts.append(parts + [own_got])
        others.append(swap(passed, "dp", dp, 1))
        more, mine_grad, peer_grad = gradients(1, ())
        back = first_half_done[0] + more
        for j in range(1, len(steps)):
            first_half(j, (mine_grad,) if j == 1 else (peer_grad,))
            if j == 1:
                (peer_grad,) = share_sums([peer_grad], own, 1, (bases[1],), [0])
        own_pieces = spread(mine_grad)
        grads.append(own_pieces + spread(peer_grad))

        shard = tokens // ffn
        place = reversed_bits(f, bits_of(ffn))
        products, received = [], []

        def halving_step(parts, bit):
            half = parts[-1].shape[0] // 2
            mine = (f >> bit) & 1
            sides = [
                [lax.dynamic_slice_in_dim(p, side * half, half, axis=0) for p in parts]
                for side in (mine, 1 - mine)
            ]
            return total_of(sides[0], 0, half), total_of(sides[1], 0, half).astype(BF16)

        first_steps = []
        for j, ((first, n), base) in enumerate(zip(steps, bases)):
            wait = (products[-1],) if products else tuple(bases)
            if j == 2:
                back = relay(back, (products[1],))
                for bit in range(bits_of(ffn)):
                    back = back + swap(back, "ffn", ffn, 1 << bit)
                back = double(back, "hid", hid)
                first_steps.append(halving_step([products[0], received[0]], 0))
                wait += (first_steps[0][1], back)
            keep, send = backward_matmul(
                grads[1], weights, chunks[1][0] * tile, first, n, width_tile, base=base, base_first=first,
                after=wait,
            )
            products.append(keep)
            received.append(swap(send, "dp", dp, 1))
        if len(steps) < 3:
            for bit in range(bits_of(ffn)):
                back = back + swap(back, "ffn", ffn, 1 << bit)
            back = double(back, "hid", hid)
        low = relay(low, (products[-1],))
        low_mine = jnp.where(first_pair, low[:, :, :rank], low[:, :, rank:])
        low_mine = double(low_mine, "hid", hid, dim=1).reshape(2 * tokens, rank).T
        back_low = back[:, : 2 * rank].astype(BF16)
        acts_product = back[:, 2 * rank]

        block = min(own, shard)

        def natural(row):
            index = row // own
            return (h ^ reversed_bits(index, bits_of(hid))) * own + row % own

        def shard_rows(x):
            return jnp.concatenate(
                [
                    lax.dynamic_slice_in_dim(x, natural(place * shard + i * block), block, axis=0)
                    for i in range(shard // block)
                ],
                axis=0,
            )

        stats_shard = shard_rows(stats)
        dot_shard = lax.dynamic_slice_in_dim(acts_product, place * shard, shard, axis=0)
        dot_factor = stats_shard[:, 1] ** 2 * dot_shard / MODEL_WIDTH
        stats_shard = jnp.concatenate([stats_shard, dot_factor[:, None]], axis=1)
        stream_shard = shard_rows(stream)
        back_shard = lax.dynamic_slice_in_dim(back_low, place * shard, shard, axis=0)

        out, sums, gathered = None, [], []
        owners = [reversed_bits(f ^ reversed_bits(p, bits_of(ffn)), bits_of(ffn)) for p in range(ffn)]
        places = jnp.stack([natural(o * shard + i * block) for o in owners for i in range(shard // block)])
        for j, (first, n) in enumerate(steps):
            got = received[j]
            if j == 1:
                got = ordered(got, products[-1])
            elif j >= 2:
                got = ordered(got, gathered[j - 2][1])
            parts = [products[j], got]
            for bit in range(bits_of(ffn)):
                if bit == 0 and j < len(first_steps):
                    keep, send = first_steps[j]
                else:
                    keep, send = halving_step(parts, bit)
                if j == 2 and bit == 1:
                    send = ordered(send, gathered[0][-1])
                parts = [keep, swap(send, "ffn", ffn, 1 << bit)]
            result, sum_part = finish(
                parts, stream_shard, stats_shard, back_shard, down_rows, steering, gain, first * width_tile,
                after=tuple(gathered[j - 1][1:2] if j else ()) + tuple(gathered[j - 2][2:] if j >= 2 else ()),
            )
            sums.append(sum_part)
            if j == len(steps) - 1:
                sums = jnp.concatenate(sums, axis=1).reshape(-1, result.shape[1])
                high = sums.astype(BF16)
                low_term = (sums - high.astype(F32)).astype(BF16)
                rows = 2 * sums.shape[0]
                empty = jnp.zeros((-rows % 16, result.shape[1]), BF16)
                result = jnp.concatenate([result, high, low_term, empty], axis=0)
            blocks = [result]
            for bit in reversed(range(bits_of(ffn))):
                blocks += [swap(x, "ffn", ffn, 1 << bit) for x in blocks]
            gathered.append(blocks)
            out = assemble(blocks, places, block, shard, tokens, width, first * width_tile, into=out)

        half = rows // 2
        terms = [
            x[shard : shard + half].astype(F32) + x[shard + half : shard + rows].astype(F32) for x in blocks
        ]
        while len(terms) > 1:
            terms = [a + b for a, b in zip(terms[: len(terms) // 2], terms[len(terms) // 2 :])]
        steering_gradient = terms[0] + swap(terms[0], "dp", dp, 1)

        up_mine = jnp.concatenate(adapter_products(low_mine, grads, products[-1:]), axis=1)
        up_other = swap(ordered(up_mine.astype(BF16), received[-1]), "dp", dp, 1).astype(F32)
        up_gradient = jnp.where(
            first_pair, jnp.stack([up_mine, up_other]), jnp.stack([up_other, up_mine])
        )
        peer_back = swap(relay(back_low, (received[-1],)), "dp", dp, 1)
        back_rows = jnp.stack([back_low, peer_back]).reshape(2, hid, own, 2 * rank).transpose(1, 0, 2, 3).reshape(2 * tokens, 2 * rank)
        (down_gradient,) = adapter_products(back_rows.T, [[normed]])
        down_gradient = jnp.transpose(
            down_gradient.reshape(2, rank, width), (0, 2, 1)
        )
        return out, steering_gradient.reshape(width), down_gradient, up_gradient

    return local


def solution(mesh):
    in_specs = (
        P("dp", "hid"),
        P("hid"),
        P("dp"),
        P("hid"),
        P("dp", "hid", "ffn"),
        P(None, "hid", None),
        P(None, None, "ffn"),
        P(("dp", "hid"), "ffn"),
    )
    out_specs = (P("dp", "hid"), P("hid"), P(None, "hid", None), P(None, None, "ffn"))
    local = make_local(mesh.shape["dp"], mesh.shape["hid"], mesh.shape["ffn"])
    return jax.shard_map(local, mesh=mesh, in_specs=in_specs, out_specs=out_specs, check_vma=False)
```

```python
import jax
import jax.numpy as jnp
from jax import lax
from jax.experimental import pallas as pl
from jax.experimental.pallas import tpu as pltpu
from jax.sharding import PartitionSpec as P

MODEL_WIDTH = 16384
ADAPTER_SCALE = 0.5
VMEM_MIB = 12
MATMUL_VMEM_MIB = 24
COST_SHARE = 0.01

F32 = jnp.float32
BF16 = jnp.bfloat16
ANY = pl.BlockSpec(memory_space=pl.ANY)
RESIDENT = pl.BlockSpec(memory_space=pltpu.VMEM)


def bits_of(n):
    return n.bit_length() - 1


def reversed_bits(x, n):
    out = 0
    for i in range(n):
        out = out + (((x >> i) & 1) << (n - 1 - i))
    return out


def tile_of(n, cap):
    return max(t for t in range(128, cap + 1, 128) if n % t == 0)


def split_tiles(count, parts):
    edges = [count * i // parts for i in range(parts + 1)]
    return [(a, b - a) for a, b in zip(edges, edges[1:]) if b > a]


def swap(x, axis, n, mask):
    return lax.ppermute(x, axis, [(i, i ^ mask) for i in range(n)])


def double(x, axis, n, dim=0):
    for bit in reversed(range(bits_of(n))):
        x = jnp.concatenate([x, swap(x, axis, n, 1 << bit)], axis=dim)
    return x


def ordered(x, *first):
    return lax.optimization_barrier((x, *first))[0]


def total_of(parts, start, stop):
    out = parts[0][start:stop]
    for part in parts[1:]:
        out = out + part[start:stop].astype(F32)
    return out


def params(mib=VMEM_MIB):
    return pltpu.CompilerParams(vmem_limit_bytes=mib * 1024 * 1024)


def cost(flops, size):
    return pl.CostEstimate(
        flops=int(flops * COST_SHARE), bytes_accessed=int(size * COST_SHARE), transcendentals=0
    )


def normalize(stream, stats, steering, gain, down, h, hid, beside=None):
    tokens, width = stream.shape
    block = tokens // hid
    ranks = down.shape[0]
    n_beside = 0 if beside is None else 1

    def token_block(p, h_ref):
        return h_ref[0] ^ reversed_bits(p, bits_of(hid))

    def kernel(h_ref, x_ref, stat_ref, steer_ref, gain_ref, down_ref, *refs):
        steered = x_ref[...].astype(F32) + stat_ref[:, :1] * steer_ref[...]
        normed = (steered * stat_ref[:, 1:] * gain_ref[...]).astype(BF16)
        out_ref, low_ref = refs[n_beside : n_beside + 2]
        out_ref[...] = normed
        low_ref[...] = lax.dot_general(
            normed, down_ref[...], (((1,), (1,)), ((), ())), preferred_element_type=F32
        )
        if n_beside:
            refs[-1][:block, :] = refs[0][...]
            refs[-1][block:, :] = normed

    whole = lambda n: pl.BlockSpec((n, width), lambda p, h_ref: (0, 0))
    rows = lambda n, m: pl.BlockSpec((n, m), lambda p, h_ref: (p, 0))
    return pl.pallas_call(
        kernel,
        grid_spec=pltpu.PrefetchScalarGridSpec(
            num_scalar_prefetch=1,
            grid=(hid,),
            in_specs=[
                pl.BlockSpec((block, width), lambda p, h_ref: (token_block(p, h_ref), 0)),
                pl.BlockSpec((block, 2), lambda p, h_ref: (token_block(p, h_ref), 0)),
                whole(1),
                whole(1),
                whole(ranks),
            ]
            + [rows(block, width)] * n_beside,
            out_specs=[rows(block, width), rows(block, ranks)] + [rows(2 * block, width)] * n_beside,
        ),
        out_shape=[
            jax.ShapeDtypeStruct((tokens, width), BF16),
            jax.ShapeDtypeStruct((tokens, ranks), F32),
        ]
        + [jax.ShapeDtypeStruct((2 * tokens, width), BF16)] * n_beside,
        compiler_params=params(),
        cost_estimate=cost(2 * tokens * width * ranks, 4 * tokens * width),
        name="normalize",
    )(
        h.reshape(1),
        stream,
        stats,
        steering.reshape(1, width),
        gain.reshape(1, width),
        down,
        *((beside,) if n_beside else ()),
    )


def forward_matmul(x, weights, first, tiles, start, stop, tile, into=(), after=()):
    rows, depth = x.shape
    half = rows // 2

    def kernel(x_ref, w_ref, *refs):
        keep_ref, send_ref, token_ref = refs[-3:]
        token_ref[...] = jnp.zeros_like(token_ref)
        y = jnp.dot(x_ref[...], w_ref[0], preferred_element_type=F32)
        keep_ref[...] = y[:half]
        send_ref[...] = y[half:].astype(BF16)

    return pl.pallas_call(
        kernel,
        grid=(stop - start,),
        in_specs=[RESIDENT, pl.BlockSpec((1, depth, tile), lambda i: (0, 0, first + start + i))]
        + [ANY] * (len(into) + len(after)),
        out_specs=[pl.BlockSpec((half, tile), lambda i: (0, start + i))] * 2
        + [pl.BlockSpec((8, 128), lambda i: (0, 0))],
        out_shape=[
            jax.ShapeDtypeStruct((half, tiles * tile), F32),
            jax.ShapeDtypeStruct((half, tiles * tile), BF16),
            jax.ShapeDtypeStruct((8, 128), F32),
        ],
        input_output_aliases={2 + i: i for i in range(len(into))},
        compiler_params=params(MATMUL_VMEM_MIB),
        cost_estimate=cost(2 * rows * depth * (stop - start) * tile, 2 * depth * (rows + (stop - start) * tile) + 6 * half * (stop - start) * tile),
        name="forward_matmul",
    )(x, weights, *into, *after)


def relay(x, after):
    def kernel(x_ref, *refs):
        refs[-1][...] = x_ref[...]

    whole = pl.BlockSpec(x.shape, lambda i: (0,) * x.ndim)
    return pl.pallas_call(
        kernel,
        grid=(1,),
        in_specs=[whole] + [ANY] * len(after),
        out_specs=whole,
        out_shape=jax.ShapeDtypeStruct(x.shape, x.dtype),
        compiler_params=params(),
        cost_estimate=cost(0, 4 * x.size),
        name="relay",
    )(x, *after)


def share_sums(parts, rows, count, after=(), places=None):
    columns = parts[0].shape[1]
    tile = tile_of(columns, 1792)

    def kernel(*refs):
        total = refs[0][...].astype(F32)
        for ref in refs[1 : len(parts)]:
            total = total + ref[...].astype(F32)
        for i in range(count):
            refs[i - count][...] = total[i * rows : (i + 1) * rows].astype(BF16)

    return pl.pallas_call(
        kernel,
        grid=(columns // tile,),
        in_specs=[
            pl.BlockSpec((count * rows, tile), lambda i, at=at: (at, i)) for at in places or [1] * len(parts)
        ]
        + [ANY] * len(after),
        out_specs=[pl.BlockSpec((rows, tile), lambda i: (0, i))] * count,
        out_shape=[jax.ShapeDtypeStruct((rows, columns), BF16)] * count,
        compiler_params=params(),
        cost_estimate=cost(count * rows * columns, 8 * count * rows * columns),
        name="share_sums",
    )(*parts, *after)


def gated_gradients(d, mine, other, cotangent, first, low, up, own, after=()):
    columns = other.shape[1]
    rank = up.shape[1]
    tile = max(t for t in range(128, 2049, 128) if columns % t == 0 and first % t == 0)
    tiles = columns // tile
    base = first // tile

    def kernel(d_ref, *refs):
        mine_refs = refs[: len(mine)]
        other_ref, flow_ref, low_ref, up_ref = refs[len(mine) : len(mine) + 4]
        mine_out, other_out, back_ref = refs[-3:]
        own_is_gate = d_ref[0] == 0
        total = mine_refs[0][...].astype(F32)
        for ref in mine_refs[1:]:
            total = total + ref[...].astype(F32)
        passed = other_ref[...].astype(F32)
        low_terms = [
            ADAPTER_SCALE
            * jnp.dot(low_ref[:, k * rank : (k + 1) * rank], up_ref[k], preferred_element_type=F32)
            for k in range(2)
        ]
        gate = jnp.where(own_is_gate, total, passed) + low_terms[0]
        upper = jnp.where(own_is_gate, passed, total) + low_terms[1]
        sigma = 1.0 / (1.0 + jnp.exp(-gate))
        flow = flow_ref[...].astype(F32)
        gate_grad = (flow * upper * sigma * (1.0 + gate * (1.0 - sigma))).astype(BF16)
        upper_grad = (flow * gate * sigma).astype(BF16)
        mine_out[...] = jnp.where(own_is_gate, gate_grad, upper_grad)
        other_out[...] = jnp.where(own_is_gate, upper_grad, gate_grad)

        @pl.when(pl.program_id(0) == 0)
        def _():
            back_ref[...] = jnp.zeros_like(back_ref)

        contract = (((1,), (1,)), ((), ()))
        for k, grad in enumerate((gate_grad, upper_grad)):
            back_ref[:, k * rank : (k + 1) * rank] += lax.dot_general(
                grad, up_ref[k], contract, preferred_element_type=F32
            )
        back_ref[:, 2 * rank :] += jnp.sum(
            gate_grad.astype(F32) * gate + upper_grad.astype(F32) * upper, axis=1, keepdims=True
        )

    here = pl.BlockSpec((own, tile), lambda i, d_ref: (0, i))
    there = pl.BlockSpec((own, tile), lambda i, d_ref: (0, base + i))
    return pl.pallas_call(
        kernel,
        grid_spec=pltpu.PrefetchScalarGridSpec(
            num_scalar_prefetch=1,
            grid=(tiles,),
            in_specs=[here] * (len(mine) + 1)
            + [
                there,
                pl.BlockSpec((own, 2 * rank), lambda i, d_ref: (0, 0)),
                pl.BlockSpec((2, rank, tile), lambda i, d_ref: (0, 0, base + i)),
            ]
            + [ANY] * len(after),
            out_specs=[here, here, pl.BlockSpec((own, 2 * rank + 1), lambda i, d_ref: (0, 0))],
        ),
        out_shape=[
            jax.ShapeDtypeStruct((own, columns), BF16),
            jax.ShapeDtypeStruct((own, columns), BF16),
            jax.ShapeDtypeStruct((own, 2 * rank + 1), F32),
        ],
        compiler_params=params(),
        cost_estimate=cost(8 * own * columns * rank, 16 * own * columns),
        name="gated_gradients",
    )(d.reshape(1), *mine, other, cotangent, low, up, *after)


def backward_matmul(pieces, weights, hidden_start, first, tiles, tile, base=None, base_first=0, partial=False, after=()):
    rows = sum(g.shape[0] for g in pieces)
    half = rows // 2
    n_base = 0 if base is None else 1
    hidden = pieces[0].shape[1]

    def kernel(*refs):
        w_ref = refs[len(pieces)]
        g = jnp.concatenate([ref[...] for ref in refs[: len(pieces)]], axis=0)
        y = lax.dot_general(g, w_ref[0], (((1,), (1,)), ((), ())), preferred_element_type=F32)
        if n_base:
            y = y + refs[len(pieces) + 1][...]
        if partial:
            refs[-1][...] = y
        else:
            refs[-2][...] = y[:half]
            refs[-1][...] = y[half:].astype(BF16)

    if partial:
        out_specs = pl.BlockSpec((rows, tile), lambda i: (0, i))
        out_shape = jax.ShapeDtypeStruct((rows, tiles * tile), F32)
    else:
        out_specs = [pl.BlockSpec((half, tile), lambda i: (0, i))] * 2
        out_shape = [
            jax.ShapeDtypeStruct((half, tiles * tile), F32),
            jax.ShapeDtypeStruct((half, tiles * tile), BF16),
        ]
    return pl.pallas_call(
        kernel,
        grid=(tiles,),
        in_specs=[
            pl.BlockSpec(g.shape, lambda i: (0, 0), pipeline_mode=pl.Buffered(1)) for g in pieces
        ]
        + [
            pl.BlockSpec(
                (pl.Element(1), pl.Element(tile), pl.Element(hidden)),
                lambda i: (0, (first + i) * tile, hidden_start),
            )
        ]
        + [pl.BlockSpec((rows, tile), lambda i: (0, first - base_first + i))] * n_base
        + [ANY] * len(after),
        out_specs=out_specs,
        out_shape=out_shape,
        compiler_params=params(MATMUL_VMEM_MIB),
        cost_estimate=cost(2 * rows * hidden * tiles * tile, 2 * hidden * (rows + tiles * tile) + (4 + 4 * n_base) * rows * tiles * tile),
        name="backward_matmul",
    )(*pieces, weights, *(() if base is None else (base,)), *after)


def adapter_products(low, groups, after=()):
    rank = low.shape[0]

    def kernel(*refs):
        at = 1
        for i, pieces in enumerate(groups):
            g = jnp.concatenate([ref[...] for ref in refs[at : at + len(pieces)]], axis=0)
            at += len(pieces)
            refs[i - len(groups)][...] = ADAPTER_SCALE * jnp.dot(
                refs[0][...], g, preferred_element_type=F32
            )

    operands = [g for pieces in groups for g in pieces]
    widths = [pieces[0].shape[1] for pieces in groups]
    return pl.pallas_call(
        kernel,
        grid=(1,),
        in_specs=[pl.BlockSpec(x.shape, lambda i: (0, 0)) for x in [low] + operands] + [ANY] * len(after),
        out_specs=[pl.BlockSpec((rank, w), lambda i: (0, 0)) for w in widths],
        out_shape=[jax.ShapeDtypeStruct((rank, w), F32) for w in widths],
        compiler_params=params(),
        cost_estimate=cost(2 * rank * low.shape[1] * sum(widths), 2 * low.shape[1] * sum(widths)),
        name="adapter_products",
    )(low, *operands, *after)


def assemble(pieces, places, block, rows, tokens, width, columns, into=None):
    chunk = pieces[0].shape[1]

    def kernel(place_ref, *refs):
        out_ref = refs[-1]
        i = 0
        for ref in refs[: len(pieces)]:
            for r in range(0, rows, block):
                out_ref[pl.ds(pl.multiple_of(place_ref[i], block), block), :] = ref[r : r + block, :]
                i += 1

    n_into = 0 if into is None else 1
    return pl.pallas_call(
        kernel,
        grid_spec=pltpu.PrefetchScalarGridSpec(
            num_scalar_prefetch=1,
            grid=(1,),
            in_specs=[pl.BlockSpec(x.shape, lambda i, p: (0, 0)) for x in pieces] + [ANY] * n_into,
            out_specs=pl.BlockSpec((pl.Element(tokens), pl.Element(chunk)), lambda i, p: (0, columns)),
        ),
        out_shape=jax.ShapeDtypeStruct((tokens, width), BF16),
        input_output_aliases={len(pieces) + 1: 0} if n_into else {},
        compiler_params=params(),
        cost_estimate=cost(0, 4 * tokens * chunk),
        name="assemble",
    )(places, *pieces, *((into,) if n_into else ()))


def finish(parts, stream, stats, back, down, steering, gain, columns, after=()):
    rows = stream.shape[0]
    width = parts[0].shape[1]

    def kernel(*refs):
        part_refs = refs[: len(parts)]
        x_ref, s_ref, back_ref, down_ref, steer_ref, gain_ref = refs[len(parts) : len(parts) + 6]
        out_ref, sum_ref = refs[-2:]
        total = part_refs[0][...].astype(F32)
        for ref in part_refs[1:]:
            total = total + ref[...].astype(F32)
        total = total + ADAPTER_SCALE * jnp.dot(back_ref[...], down_ref[...], preferred_element_type=F32)
        steered = x_ref[...].astype(F32) + s_ref[:, 0:1] * steer_ref[...]
        grad = s_ref[:, 1:2] * gain_ref[...] * total - s_ref[:, 2:3] * steered
        out_ref[...] = grad.astype(BF16)
        sum_ref[...] = jnp.sum(s_ref[:, 0:1] * grad, axis=0, keepdims=True)

    across = lambda n: pl.BlockSpec((pl.Element(n), pl.Element(width)), lambda i: (0, columns))
    return pl.pallas_call(
        kernel,
        grid=(1,),
        in_specs=[pl.BlockSpec((rows, width), lambda i: (0, 0))] * len(parts)
        + [
            across(rows),
            pl.BlockSpec(stats.shape, lambda i: (0, 0)),
            pl.BlockSpec(back.shape, lambda i: (0, 0)),
            across(down.shape[0]),
            across(1),
            across(1),
        ]
        + [ANY] * len(after),
        out_specs=[pl.BlockSpec((rows, width), lambda i: (0, 0)), pl.BlockSpec((1, width), lambda i: (0, 0))],
        out_shape=[jax.ShapeDtypeStruct((rows, width), BF16), jax.ShapeDtypeStruct((1, width), F32)],
        compiler_params=params(),
        cost_estimate=cost(2 * rows * width * down.shape[0], 10 * rows * width),
        name="finish",
    )(*parts, stream, stats, back, down, steering.reshape(1, -1), gain.reshape(1, -1), *after)


def make_local(dp, hid, ffn):
    def local(stream, steering, strength, gain, weights, down, up, cotangent):
        d, h, f = lax.axis_index("dp"), lax.axis_index("hid"), lax.axis_index("ffn")
        tokens, width = stream.shape
        hidden = weights.shape[2]
        own = tokens // hid
        rank = down.shape[2]
        first_pair = d == 0
        down_rows = jnp.transpose(down, (0, 2, 1)).reshape(2 * rank, width)

        peer_stream = swap(stream, "dp", dp, 1)
        rows = stream.astype(F32)
        total_rows, total_steer = lax.psum(
            (jnp.sum(rows * rows, axis=1), jnp.sum(steering * steering)), "hid"
        )
        stream_ms = total_rows / MODEL_WIDTH + 1e-06
        steer_ms = total_steer / MODEL_WIDTH + 1e-06
        scale = strength * jnp.sqrt(stream_ms / steer_ms)
        steered = rows + scale[:, None] * steering[None, :]
        steered_power = lax.psum(jnp.sum(steered * steered, axis=1), "hid")
        inv_rms = lax.rsqrt(steered_power / MODEL_WIDTH + 1e-05)
        stats = jnp.stack([scale, inv_rms], axis=1)
        peer_stats = swap(stats, "dp", dp, 1)

        tile = tile_of(hidden, 512)
        count = hidden // tile
        chunks = [(0, (count + 1) // 2), ((count + 1) // 2, count // 2)]
        last_bit = 1 << (bits_of(hid) - 1)
        own_normed, own_low = normalize(stream, stats, steering, gain, down_rows, h, hid)
        def forward(x, c, edges, afters):
            first, n = chunks[c]
            out, token = (), None
            for start, stop, after in zip(edges, edges[1:], afters):
                *out, token = forward_matmul(
                    x, weights, first, n, start, stop, tile, into=tuple(out), after=after(token)
                )
            keep, send = out
            parts = [keep, swap(send, "hid", hid, 1)]
            for bit in range(1, bits_of(hid) - 1):
                size = parts[-1].shape[0]
                send = total_of(parts, size // 2, size).astype(BF16)
                parts.append(swap(send, "hid", hid, 1 << bit))
            return parts

        own_parts = forward(own_normed, 0, (0, chunks[0][1]), (lambda t: (),))
        (own_send,) = share_sums(own_parts, own, 1)
        own_got = swap(own_send, "hid", hid, last_bit)
        peer_normed, peer_low, normed = normalize(
            peer_stream, ordered(peer_stats, own_send), steering, gain, down_rows, h, hid, own_normed
        )

        low, low_steps = jnp.stack([own_low, peer_low]), []
        for bit in range(bits_of(hid)):
            half = low.shape[1] // 2
            low = low[:, :half] + swap(low[:, half:], "hid", hid, 1 << bit)
            low_steps.append(low)
        low = low.astype(BF16)
        low_own = low[0]

        width_tile = tile_of(width, 512)
        tiles = width // width_tile
        steps = [(0, 3), (3, 3), (6, 2)] if tiles == 8 else split_tiles(tiles, 3)
        acts, others, grads = [], [], []

        def gradients(c, after):
            mine_grad, other_grad, back_part = gated_gradients(
                d, acts[c], others[c], cotangent, chunks[c][0] * tile, low_own, up, own, after
            )
            return back_part, mine_grad, swap(other_grad, "dp", dp, 1)

        def spread(g):
            blocks = [g]
            for bit in reversed(range(bits_of(hid))):
                blocks += [swap(x, "hid", hid, 1 << bit) for x in blocks]
            return blocks

        n = chunks[0][1]
        peer_parts = forward(
            peer_normed, 0, (0, (n + 1) // 2, n), (lambda t: (own_send,), lambda t: (low_steps[0], own_got))
        )
        (peer_send,) = share_sums(peer_parts, own, 1, (low_own,))
        peer_got = swap(peer_send, "hid", hid, last_bit)
        acts.append(own_parts + [own_got])

        def pass_on(token):
            terms = peer_parts + [peer_got]
            (passed,) = share_sums(terms, own, 1, (token,), [0] * len(terms))
            others.append(swap(passed, "dp", dp, 1))
            return peer_got, passed

        n = chunks[1][1]
        first_send = peer_send
        first_half_done = []

        def first_gradients(token):
            more, mine_grad, peer_grad = gradients(0, (token,))
            own_pieces, peer_pieces = spread(mine_grad), spread(peer_grad)
            grads.append(own_pieces + peer_pieces)
            first_half_done.append(more)
            return peer_grad, own_pieces[1]

        parts = forward(
            normed, 1, (0, n // 3, n - 1, n), (lambda t: (first_send,), pass_on, first_gradients)
        )
        own_send, peer_send = share_sums(parts, own, 2)
        peer_got = swap(peer_send, "hid", hid, last_bit)
        own_got = swap(own_send, "hid", hid, last_bit)
        bases = []

        def first_half(j, after):
            first, n = steps[j]
            bases.append(
                backward_matmul(
                    grads[0], weights, 0, first, n, width_tile, partial=True, after=after
                )
            )

        first_half(0, (own_send,))
        (passed,) = share_sums(parts + [peer_got], own, 1, (bases[0],), [1] * len(parts) + [0])
        acts.append(parts + [own_got])
        others.append(swap(passed, "dp", dp, 1))
        more, mine_grad, peer_grad = gradients(1, ())
        back = first_half_done[0] + more
        for j in range(1, len(steps)):
            first_half(j, (mine_grad,) if j == 1 else (peer_grad,))
            if j == 1:
                (peer_grad,) = share_sums([peer_grad], own, 1, (bases[1],), [0])
        own_pieces = spread(mine_grad)
        grads.append(own_pieces + spread(peer_grad))

        shard = tokens // ffn
        place = reversed_bits(f, bits_of(ffn))
        products, received = [], []

        def halving_step(parts, bit):
            half = parts[-1].shape[0] // 2
            mine = (f >> bit) & 1
            sides = [
                [lax.dynamic_slice_in_dim(p, side * half, half, axis=0) for p in parts]
                for side in (mine, 1 - mine)
            ]
            return total_of(sides[0], 0, half), total_of(sides[1], 0, half).astype(BF16)

        begun = []
        for j, ((first, n), base) in enumerate(zip(steps, bases)):
            wait = (products[-1],) if products else tuple(bases)
            if j == 2:
                keep, send = halving_step([products[0], relay(received[0], (products[1],))], 0)
                begun = [keep, swap(send, "ffn", ffn, 1)]
                wait += (send,)
            keep, send = backward_matmul(
                grads[1], weights, chunks[1][0] * tile, first, n, width_tile, base=base, base_first=first,
                after=wait,
            )
            products.append(keep)
            received.append(swap(send, "dp", dp, 1))
        back = relay(back, (products[-1], *begun[1:]))
        for bit in range(bits_of(ffn)):
            back = back + swap(back, "ffn", ffn, 1 << bit)
        back = double(back, "hid", hid)
        low = relay(low, (products[-1], received[-1]))
        low_mine = jnp.where(first_pair, low[:, :, :rank], low[:, :, rank:])
        low_mine = double(low_mine, "hid", hid, dim=1).reshape(2 * tokens, rank).T
        back_low = back[:, : 2 * rank].astype(BF16)
        acts_product = back[:, 2 * rank]

        block = min(own, shard)

        def natural(row):
            index = row // own
            return (h ^ reversed_bits(index, bits_of(hid))) * own + row % own

        def shard_rows(x):
            return jnp.concatenate(
                [
                    lax.dynamic_slice_in_dim(x, natural(place * shard + i * block), block, axis=0)
                    for i in range(shard // block)
                ],
                axis=0,
            )

        stats_shard = shard_rows(stats)
        dot_shard = lax.dynamic_slice_in_dim(acts_product, place * shard, shard, axis=0)
        dot_factor = stats_shard[:, 1] ** 2 * dot_shard / MODEL_WIDTH
        stats_shard = jnp.concatenate([stats_shard, dot_factor[:, None]], axis=1)
        stream_shard = shard_rows(stream)
        back_shard = lax.dynamic_slice_in_dim(back_low, place * shard, shard, axis=0)

        out, sums, gathered = None, [], []
        owners = [reversed_bits(f ^ reversed_bits(p, bits_of(ffn)), bits_of(ffn)) for p in range(ffn)]
        places = jnp.stack([natural(o * shard + i * block) for o in owners for i in range(shard // block)])
        for j, (first, n) in enumerate(steps):
            got = received[j]
            if j == 1:
                got = ordered(got, products[-1])
            elif j >= 2:
                got = ordered(got, gathered[j - 2][1])
            parts = [products[j], got]
            for bit in range(bits_of(ffn)):
                if j == 0 and bit == 0 and begun:
                    parts = begun
                    continue
                keep, send = halving_step(parts, bit)
                if j == 2 and bit == 1:
                    send = ordered(send, gathered[0][-1])
                parts = [keep, swap(send, "ffn", ffn, 1 << bit)]
            result, sum_part = finish(
                parts, stream_shard, stats_shard, back_shard, down_rows, steering, gain, first * width_tile,
                after=tuple(gathered[j - 1][1:2] if j else ()) + tuple(gathered[j - 2][2:] if j >= 2 else ()),
            )
            sums.append(sum_part)
            if j == len(steps) - 1:
                sums = jnp.concatenate(sums, axis=1).reshape(-1, result.shape[1])
                high = sums.astype(BF16)
                low_term = (sums - high.astype(F32)).astype(BF16)
                rows = 2 * sums.shape[0]
                empty = jnp.zeros((-rows % 16, result.shape[1]), BF16)
                result = jnp.concatenate([result, high, low_term, empty], axis=0)
            blocks = [result]
            for bit in reversed(range(bits_of(ffn))):
                blocks += [swap(x, "ffn", ffn, 1 << bit) for x in blocks]
            gathered.append(blocks)
            out = assemble(blocks, places, block, shard, tokens, width, first * width_tile, into=out)

        half = rows // 2
        terms = [
            x[shard : shard + half].astype(F32) + x[shard + half : shard + rows].astype(F32) for x in blocks
        ]
        while len(terms) > 1:
            terms = [a + b for a, b in zip(terms[: len(terms) // 2], terms[len(terms) // 2 :])]
        steering_gradient = terms[0] + swap(terms[0], "dp", dp, 1)

        up_mine = jnp.concatenate(adapter_products(low_mine, grads, products[-1:]), axis=1)
        up_other = swap(ordered(up_mine.astype(BF16), received[-1]), "dp", dp, 1).astype(F32)
        up_gradient = jnp.where(
            first_pair, jnp.stack([up_mine, up_other]), jnp.stack([up_other, up_mine])
        )
        peer_back = swap(relay(back_low, (received[-1],)), "dp", dp, 1)
        back_rows = jnp.stack([back_low, peer_back]).reshape(2, hid, own, 2 * rank).transpose(1, 0, 2, 3).reshape(2 * tokens, 2 * rank)
        (down_gradient,) = adapter_products(back_rows.T, [[normed]])
        down_gradient = jnp.transpose(
            down_gradient.reshape(2, rank, width), (0, 2, 1)
        )
        return out, steering_gradient.reshape(width), down_gradient, up_gradient

    return local


def solution(mesh):
    in_specs = (
        P("dp", "hid"),
        P("hid"),
        P("dp"),
        P("hid"),
        P("dp", "hid", "ffn"),
        P(None, "hid", None),
        P(None, None, "ffn"),
        P(("dp", "hid"), "ffn"),
    )
    out_specs = (P("dp", "hid"), P("hid"), P(None, "hid", None), P(None, None, "ffn"))
    local = make_local(mesh.shape["dp"], mesh.shape["hid"], mesh.shape["ffn"])
    return jax.shard_map(local, mesh=mesh, in_specs=in_specs, out_specs=out_specs, check_vma=False)
```
